32 devices in a mesh: groups: 2 (over x), lat: 16 (over z, y, core).
Axes of the slice: x: 2, y: 2, z: 4, core: 2. Of those that a mesh axis runs over, the one named last changes fastest.
Arguments:
- tangent: float32 [128, 128, 1024], P(('groups', 'lat')), parts along dimension 0, may hold values from -6 to 6
- wind_code: int32 [4, 128, 128], P(None, ('groups', 'lat')), parts along dimension 1, may hold values from 0 to 14
- courant: float32 [1024], replicated, may hold values from 0.2 to 0.8
- obs_index: int32 [32, 480], P(('groups', 'lat')), parts along dimension 0, may hold values from 0 to 511, as said below
- obs_count: int32 [32], P(('groups', 'lat')), parts along dimension 0, may hold values from 96 to 480, as said below
- obs_quality: bfloat16 [32, 480], P(('groups', 'lat')), parts along dimension 0, may hold values from 0.29882812 to 3
- background: bfloat16 [32, 480, 1024], P(('groups', 'lat')), parts along dimension 0, may hold values from -6 to 6
- w_first: bfloat16 [1024, 1024], replicated, may hold values from -0.1875 to 0.1875
- w_second: bfloat16 [1024, 1024], replicated, may hold values from -0.1875 to 0.1875
- w_third: bfloat16 [1024, 1024], replicated, may hold values from -0.1875 to 0.1875
- chan_weight: float32 [1024], replicated, may hold values from 0.3 to 3
Outputs:
- adjoint_field: float32 [128, 128, 1024], P(('groups', 'lat')), parts along dimension 0
The draws below stay inside these ranges and needn't reach their ends.
There are 2 independent parts, one for each index of `groups`. The reference program is written for one: setup_inputs(seed, part) draws one part's arguments, and reference() takes and returns one part's arrays. A program takes and returns all parts, laid end to end along the dimension named above; an argument that names none is the same for every part. Nothing has to cross between parts.
Inputs may be any that keep to these rules, and one draw needn't show every extreme that they name: `obs_count`: the counts of all tiles sum to 192 times the number of tiles, and some tile has 480. `obs_index`: the 480 entries of one tile are distinct; the first obs_count of them are the observed columns.
All inputs are finite; a program needn't handle non-finite values.
Results may differ from the reference program's by a relative error of at most 0.0055.
Values may be sent and summed in bfloat16 or wider, within the bound.
No kernel may reach another device: no remote copies, remote signals or barrier semaphores. Data moves between devices by JAX's collectives and lax.ppermute only.
A program may use at most 64 MiB of HBM per device.

```python
import math
import jax
import jax.numpy as jnp
from jax import lax

K = 1024
H = 1024
CH = 1024
LAT_DEV = 4
LON = 128
STEPS = 4
NLAT = 64
LOAD = 192
F_MAX = 96
OBS_MAX = 480
N_LAT = 16


def draw_obs_count(key, part):
    group_key, heavy_key = jax.random.split(jax.random.fold_in(key, 7))
    group_total = N_LAT // 4
    extra_obs = jax.random.randint(group_key, (group_total,), 0, F_MAX + 1)
    extra_obs = extra_obs.at[0].set(F_MAX)
    heavy_slot = jax.random.randint(heavy_key, (group_total,), 0, 4)
    member_ids = jnp.arange(4, dtype=jnp.int32)
    tile_counts = jnp.where(member_ids[None, :] == heavy_slot[:, None], LOAD + 3 * extra_obs[:, None], LOAD - extra_obs[:, None])
    return tile_counts.reshape(N_LAT).astype(jnp.int32)


def draw_obs_index(key, part):
    tile_keys = jax.random.split(jax.random.fold_in(key, 11), N_LAT)
    chosen = jax.vmap(lambda tile_key: jax.random.permutation(tile_key, LAT_DEV * LON)[:OBS_MAX])(tile_keys)
    return chosen.astype(jnp.int32)


def plant(entries, own_key, smallest, largest):
    index_at = [jax.random.randint(jax.random.fold_in(own_key, axis), (), 0, length) for axis, length in enumerate(entries.shape)]
    widest = entries.shape.index(max(entries.shape))
    beside = index_at[:widest] + [(index_at[widest] + 1) % entries.shape[widest]] + index_at[widest + 1:]
    return entries.at[tuple(index_at)].set(smallest).at[tuple(beside)].set(largest)


def level_of(rng, dims, shards, smallest, high):
    factor_of, own = 1.0, jax.random.fold_in(rng, 6)
    for axis_at, shards_of in shards:
        draws = jnp.exp(jax.random.uniform(jax.random.fold_in(own, axis_at), (shards_of,), jnp.float32, smallest / len(shards), high / len(shards)))
        factor_of = factor_of * jnp.repeat(draws, dims[axis_at] // shards_of).reshape([-1 if axis == axis_at else 1 for axis in range(len(dims))])
    return factor_of


def scatter_about(key, dims, scale, bound, cuts=(), held_as=jnp.bfloat16):
    result = scale * jax.random.normal(key, dims, jnp.float32)
    if cuts:
        result = result * level_of(key, dims, cuts, -0.22, 0.18)
    return jnp.clip(result, -bound, bound).astype(held_as)


def setup_inputs(seed: int = 0, part: int = 0) -> dict:
    arg_keys = jax.random.split(jax.random.key(seed), 12)
    own_keys = jax.random.split(jax.random.fold_in(arg_keys[11], part), 12)
    return {
        "tangent": scatter_about(own_keys[0], (NLAT, LON, K), 1.0, 6.0, ((0, 16),), jnp.float32),
        "wind_code": plant(jax.random.randint(own_keys[1], (STEPS, NLAT, LON), 0, 15), jax.random.fold_in(own_keys[1], 1), 0, 14).astype(jnp.int32),
        "courant": jnp.clip(jax.random.uniform(arg_keys[2], (K,), jnp.float32, 0.2, 0.8), 0.2, 0.8),
        "obs_index": draw_obs_index(jax.random.fold_in(jax.random.fold_in(arg_keys[11], part), 71), part),
        "obs_count": draw_obs_count(jax.random.fold_in(jax.random.fold_in(arg_keys[11], part), 71), part),
        "obs_quality": jnp.clip(jnp.exp(math.log(3.0) - 2.306499 * jax.random.uniform(own_keys[5], (N_LAT, OBS_MAX), jnp.float32) ** level_of(own_keys[5], (N_LAT, OBS_MAX), ((0, 16),), -0.2, 0.2)), 0.29882812, 3.0).astype(jnp.bfloat16),
        "background": scatter_about(own_keys[6], (N_LAT, OBS_MAX, K), 1.0, 6.0, ((0, 16),)),
        "w_first": scatter_about(arg_keys[7], (K, H), K ** -0.5, 0.1875),
        "w_second": scatter_about(arg_keys[8], (H, H), H ** -0.5, 0.1875),
        "w_third": scatter_about(arg_keys[9], (H, CH), H ** -0.5, 0.1875),
        "chan_weight": jnp.clip(jnp.exp(jax.random.uniform(arg_keys[10], (CH,), jnp.float32, math.log(0.3), math.log(3.0))), 0.3, 3.0),
    }


def source_cells(wind_step):
    lat_shift = wind_step // 5 - 1
    lon_shift = wind_step % 5 - 2
    row_grid = lax.broadcasted_iota(jnp.int32, wind_step.shape, 0) - lat_shift
    col_grid = (lax.broadcasted_iota(jnp.int32, wind_step.shape, 1) - lon_shift) % wind_step.shape[1]
    return row_grid, col_grid


def advect_forward(state_now, wind_step, courant):
    row_grid, col_grid = source_cells(wind_step)
    row_total = state_now.shape[0]
    inside = ((row_grid >= 0) & (row_grid < row_total)).astype(jnp.float32)
    upstream = state_now[jnp.clip(row_grid, 0, row_total - 1), col_grid] * inside[:, :, None]
    return (1.0 - courant) * state_now + courant * upstream


def advect_adjoint(adj_now, wind_step, courant):
    row_grid, col_grid = source_cells(wind_step)
    row_total = adj_now.shape[0]
    inside = ((row_grid >= 0) & (row_grid < row_total)).astype(jnp.float32)
    result_adj = (1.0 - courant) * adj_now
    return result_adj.at[jnp.clip(row_grid, 0, row_total - 1), col_grid].add(courant * adj_now * inside[:, :, None])


def product_t(left, right):
    return lax.dot_general(left, right, (((1,), (1,)), ((), ())), preferred_element_type=jnp.float32)


def radiance_adjoint(tangent_cols, back_cols, quality_cols, w_first, w_second, w_third, chan_weight):
    first_tanh = jnp.tanh(jnp.dot(back_cols, w_first, preferred_element_type=jnp.float32))
    hidden_one = first_tanh.astype(jnp.bfloat16)
    slope_one = 1.0 - first_tanh * first_tanh
    second_tanh = jnp.tanh(jnp.dot(hidden_one, w_second, preferred_element_type=jnp.float32))
    slope_two = 1.0 - second_tanh * second_tanh
    tangent_one = (slope_one * jnp.dot(tangent_cols, w_first, preferred_element_type=jnp.float32)).astype(jnp.bfloat16)
    tangent_two = (slope_two * jnp.dot(tangent_one, w_second, preferred_element_type=jnp.float32)).astype(jnp.bfloat16)
    radiance_tangent = jnp.dot(tangent_two, w_third, preferred_element_type=jnp.float32)
    weighted = (quality_cols.astype(jnp.float32)[:, None] * chan_weight[None, :] * radiance_tangent).astype(jnp.bfloat16)
    adjoint_two = (slope_two * product_t(weighted, w_third)).astype(jnp.bfloat16)
    adjoint_one = (slope_one * product_t(adjoint_two, w_second)).astype(jnp.bfloat16)
    return product_t(adjoint_one, w_first).astype(jnp.bfloat16)


def reference(tangent, wind_code, courant, obs_index, obs_count, obs_quality, background, w_first, w_second, w_third, chan_weight):
    state_now = tangent
    for step_index in range(STEPS):
        state_now = advect_forward(state_now, wind_code[step_index], courant)
    tile_cols = state_now.reshape(N_LAT, LAT_DEV * LON, K)
    slot_ids = jnp.arange(OBS_MAX, dtype=jnp.int32)
    observed = slot_ids[None, :] < obs_count[:, None]
    picked = jax.vmap(lambda cols_all, where_cols: jnp.take(cols_all, where_cols, axis=0))(tile_cols, obs_index)
    column_values = jnp.where(observed[:, :, None], picked, 0.0).astype(jnp.bfloat16)
    live_quality = jnp.where(observed, obs_quality, jnp.zeros_like(obs_quality))

    def one_tile(pieces):
        return radiance_adjoint(pieces[0], pieces[1], pieces[2], w_first, w_second, w_third, chan_weight)

    column_adjoint = lax.map(one_tile, (column_values, background, live_quality))

    def place_tile(ret_cols, where_cols):
        return jnp.zeros((LAT_DEV * LON, K), jnp.float32).at[where_cols].add(ret_cols.astype(jnp.float32))

    adj_now = jax.vmap(place_tile)(column_adjoint, obs_index).reshape(NLAT, LON, K)
    for step_index in reversed(range(STEPS)):
        adj_now = advect_adjoint(adj_now, wind_code[step_index], courant)
    return adj_now
```

```python
import functools

import jax
import jax.numpy as jnp
from jax import lax
from jax.experimental import pallas as pl
from jax.experimental.pallas import tpu as pltpu
from jax.sharding import PartitionSpec as P

F32 = jnp.float32
BF16 = jnp.bfloat16
LANE = 256
ANY = pl.BlockSpec(memory_space=pl.ANY)
VMEM = pl.BlockSpec(memory_space=pltpu.VMEM)
SMEM = pl.BlockSpec(memory_space=pltpu.SMEM)
VMEM_LIMIT = 56 * 1024 * 1024


def dot_t(left, right):
    return lax.dot_general(left, right, (((1,), (1,)), ((), ())), preferred_element_type=F32)


def dot(left, right):
    return jnp.dot(left, right, preferred_element_type=F32)


def store_sources(table, slot, codes, mirrored, sign, lon, rows):
    code = codes.astype(F32) - 1.0
    lat_q = jnp.where(code >= 5.0, 1.0, 0.0) + jnp.where(code >= 10.0, 1.0, 0.0)
    lon_step = code - 5.0 * lat_q - 2.0
    col = lax.broadcasted_iota(jnp.int32, code.shape, 1).astype(F32) - lon_step
    col = jnp.where(col < 0.0, col + lon, jnp.where(col >= lon, col - lon, col))
    stored = lax.broadcasted_iota(jnp.int32, code.shape, 0) & (rows - 1)
    row = (rows - 1 - stored) if mirrored else stored
    row = (row + slot * rows).astype(F32)
    src = (row - sign * (lat_q - 1.0)) * lon + col
    table[slot * code.shape[0] : (slot + 1) * code.shape[0], :] = jnp.where(code < 0.0, -65536.0, src)


def table_row(step, ext, rows):
    slot, at = ext // rows, ext % rows
    return slot * rows * rows + step * rows + (at if slot == 1 else rows - 1 - at)


def pull_matrix(out, turned, step, ext, lon, rows):
    span = 4 * lon
    lanes = lax.broadcasted_iota(jnp.int32, (lon, span), 1).astype(F32) + float((ext - 1) * lon)
    for half in range(2):
        k = table_row(step, ext + half, rows)
        column = turned[:, k : k + 1]
        out[half * lon : (half + 1) * lon, :] = jnp.where(column == lanes, 1.0, 0.0).astype(BF16)


def push_matrix(out, table, step, ext, lon, rows):
    dest = lax.broadcasted_iota(jnp.int32, (2 * lon, lon), 0).astype(F32) + float(ext * lon)
    for part in range(4):
        k = table_row(step, ext - 1 + part, rows)
        line = table[k : k + 1, :]
        out[:, part * lon : (part + 1) * lon] = jnp.where(line == dest, 1.0, 0.0).astype(BF16)


def pack_kernel(flip, tangent, codes, out, buf, sem):
    rows, lon = tangent.shape[0], tangent.shape[1]
    copies = []
    for j in range(rows):
        at = jnp.where(flip[0] == 1, rows - 1 - j, j)
        copies.append(pltpu.make_async_copy(tangent.at[at], buf.at[j], sem.at[j]))
        copies[-1].start()
    pad = jnp.zeros((codes.shape[0], out.shape[1] - lon), BF16)
    out[rows * lon :, :] = jnp.concatenate([codes[...].astype(F32).astype(BF16), pad], axis=1)
    for j in range(rows):
        copies[j].wait()
        out[j * lon : (j + 1) * lon, :] = buf[j].astype(BF16)


def near_steps(mats, start_b, start_f, c_ref, outs, mid_b, mid_f, lon, cs):
    c = c_ref[0:1, cs]
    blocks = ((5, 7, 9), (6, 8), (7,))
    read_b, read_f, first = start_b, start_f, 4
    k = 0
    for step, exts in enumerate(blocks):
        for ext in exts:
            at = (ext - 1 - first) * lon
            pulled = dot(mats[k], read_b(at, 4 * lon))
            value = (1.0 - c) * read_f(at + lon, 2 * lon) + c * pulled
            k += 1
            if ext == exts[0]:
                outs[step][:, cs] = value
            if step < 2:
                to = (ext - exts[0]) * lon
                mid_f[step, to : to + 2 * lon, :] = value
                mid_b[step, to : to + 2 * lon, :] = value.astype(BF16)
        first = exts[0]
        read_b = functools.partial(lambda s, a, n: mid_b[s, a : a + n, :], step)
        read_f = functools.partial(lambda s, a, n: mid_f[s, a : a + n, :], step)


def far_steps(mats, start_b, start_f, c_ref, kept, mid_b, mid_f, lon, cs):
    c = c_ref[0:1, cs]
    k = 0
    done = []
    for step in range(4):
        for half in range(2):
            at = 2 * half * lon
            if step == 0:
                window, own = start_b(at, 4 * lon), start_f(at + lon, 2 * lon)
            else:
                window = mid_b[step - 1, at : at + 4 * lon, :]
                own = mid_f[step - 1, at + lon : at + 3 * lon, :]
            value = (1.0 - c) * own + c * dot(mats[k], window)
            k += 1
            if step < 3:
                mid_f[step, at : at + 2 * lon, :] = value
                mid_b[step, at : at + 2 * lon, :] = value.astype(BF16)
            else:
                done.append(value)
        if step < 3:
            carried = kept[step][:, cs]
            mid_f[step, 4 * lon :, :] = carried
            mid_b[step, 4 * lon :, :] = carried.astype(BF16)
    return done


def near_kernel(
    flip, tangent, own, near, courant, background, w_first, w_second,
    slope_one, slope_two, kept_a, kept_b, kept_c,
    table, mats, cells_f, cells_b, mid_b, mid_f, back, w_one, w_two, hidden, s_one, s_two, sem,
):
    rows, lon = tangent.shape[0], tangent.shape[1]
    levels = tangent.shape[2]
    loads = [
        pltpu.make_async_copy(background, back, sem.at[0]),
        pltpu.make_async_copy(w_first, w_one, sem.at[1]),
        pltpu.make_async_copy(w_second, w_two, sem.at[2]),
    ]
    for copy in loads:
        copy.start()
    cell_copies = []
    for j in range(rows):
        at = jnp.where(flip[0] == 1, rows - 1 - j, j)
        cell_copies.append(pltpu.make_async_copy(tangent.at[at], cells_f.at[j], sem.at[5 + j]))
        cell_copies[-1].start()

    sign = jnp.where(flip[0] == 1, -1.0, 1.0)
    cells = rows * lon
    table[...] = jnp.zeros_like(table)
    store_sources(table, 1, own[cells:, 0:lon], False, sign, lon, rows)
    store_sources(table, 2, near[cells:, 0:lon], True, sign, lon, rows)
    turned = table[...].T
    k = 0
    for step, exts in enumerate(((5, 7, 9), (6, 8), (7,))):
        for ext in exts:
            pull_matrix(mats.at[k], turned, step, ext, lon, rows)
            k += 1
    cells_b[0:cells, :] = own[0:cells, :]
    for j in range(rows):
        cells_b[(rows + j) * lon : (rows + j + 1) * lon, :] = near[(rows - 1 - j) * lon : (rows - j) * lon, :]
    for copy in cell_copies:
        copy.wait()

    @pl.loop(0, levels // LANE)
    def _(i):
        cs = pl.ds(pl.multiple_of(i * LANE, LANE), LANE)

        def start_f(at, size):
            pieces = []
            for row in range(at // lon, (at + size) // lon):
                if row < rows:
                    pieces.append(cells_f[row, :, cs])
                else:
                    pieces.append(cells_b[row * lon : (row + 1) * lon, cs].astype(F32))
            return jnp.concatenate(pieces, axis=0)

        near_steps(
            mats, lambda at, size: cells_b[at : at + size, cs], start_f, courant,
            (kept_a, kept_b, kept_c), mid_b, mid_f, lon, cs,
        )

    loads[0].wait()
    loads[1].wait()

    @pl.loop(0, levels // LANE)
    def _(i):
        cs = pl.ds(pl.multiple_of(i * LANE, LANE), LANE)
        first_tanh = jnp.tanh(dot(back[...], w_one[:, cs]))
        hidden[:, cs] = first_tanh.astype(BF16)
        s_one[:, cs] = 1.0 - first_tanh * first_tanh

    keep_one = pltpu.make_async_copy(s_one, slope_one, sem.at[3])
    keep_one.start()
    loads[2].wait()

    @pl.loop(0, levels // LANE)
    def _(i):
        cs = pl.ds(pl.multiple_of(i * LANE, LANE), LANE)
        second_tanh = jnp.tanh(dot(hidden[...], w_two[:, cs]))
        s_two[:, cs] = 1.0 - second_tanh * second_tanh

    keep_two = pltpu.make_async_copy(s_two, slope_two, sem.at[4])
    keep_two.start()
    keep_one.wait()
    keep_two.wait()


def observe_kernel(
    flip, tangent, own, near, far, courant, slope_one, slope_two, kept_a, kept_b, kept_c,
    w_first, w_second, w_third, where_col, where_row, quality, chan_weight,
    out,
    table, mats, row_f, cells_b, mid_b, mid_f, last_b, w_one, w_two, w_three, s_one, s_two,
    pick, place, one_b, two_b, sem,
):
    rows, lon = tangent.shape[0], tangent.shape[1]
    levels = tangent.shape[2]
    loads = [
        pltpu.make_async_copy(w_first, w_one, sem.at[0]),
        pltpu.make_async_copy(slope_one, s_one, sem.at[1]),
        pltpu.make_async_copy(w_second, w_two, sem.at[2]),
        pltpu.make_async_copy(slope_two, s_two, sem.at[3]),
        pltpu.make_async_copy(w_third, w_three, sem.at[4]),
    ]
    at0 = jnp.where(flip[0] == 1, rows - 1, 0)
    row_copy = pltpu.make_async_copy(tangent.at[at0], row_f, sem.at[5])
    row_copy.start()
    for copy in loads:
        copy.start()

    sign = jnp.where(flip[0] == 1, -1.0, 1.0)
    cells = rows * lon
    table[...] = jnp.zeros_like(table)
    store_sources(table, 0, far[cells:, 0:lon], True, sign, lon, rows)
    store_sources(table, 1, own[cells:, 0:lon], False, sign, lon, rows)
    turned = table[...].T
    for step in range(4):
        for half in range(2):
            pull_matrix(mats.at[2 * step + half], turned, step, step + 1 + 2 * half, lon, rows)
    for j in range(rows):
        cells_b[j * lon : (j + 1) * lon, :] = far[(rows - 1 - j) * lon : (rows - j) * lon, :]
    cells_b[cells:, :] = own[0 : 2 * lon, :]
    slots = where_col.shape[0]
    pick[...] = jnp.where(
        where_col[...] == lax.broadcasted_iota(jnp.int32, (slots, cells), 1), 1.0, 0.0
    ).astype(BF16)
    place[...] = jnp.where(
        where_row[...] == lax.broadcasted_iota(jnp.int32, (cells, slots), 0), 1.0, 0.0
    ).astype(BF16)
    row_copy.wait()

    @pl.loop(0, levels // LANE)
    def _(i):
        cs = pl.ds(pl.multiple_of(i * LANE, LANE), LANE)

        def start_f(at, size):
            pieces = []
            for row in range(at // lon, (at + size) // lon):
                if row == rows:
                    pieces.append(row_f[:, cs])
                else:
                    pieces.append(cells_b[row * lon : (row + 1) * lon, cs].astype(F32))
            return jnp.concatenate(pieces, axis=0)

        done = far_steps(
            mats, lambda at, size: cells_b[at : at + size, cs], start_f, courant,
            (kept_a, kept_b, kept_c), mid_b, mid_f, lon, cs,
        )
        for half in range(2):
            last_b[2 * half * lon : 2 * (half + 1) * lon, :] = done[half].astype(BF16)
        one_b[:, cs] = dot(pick[...], last_b[...]).astype(BF16)

    def layer(body):
        @pl.loop(0, levels // LANE)
        def _(i):
            body(pl.ds(pl.multiple_of(i * LANE, LANE), LANE))

    loads[0].wait()
    loads[1].wait()

    def tangent_one(cs):
        two_b[:, cs] = (s_one[:, cs] * dot(one_b[...], w_one[:, cs])).astype(BF16)

    layer(tangent_one)
    loads[2].wait()
    loads[3].wait()

    def tangent_two(cs):
        one_b[:, cs] = (s_two[:, cs] * dot(two_b[...], w_two[:, cs])).astype(BF16)

    layer(tangent_two)
    loads[4].wait()

    def weighted(cs):
        scale = quality[...] * chan_weight[0:1, cs]
        two_b[:, cs] = (scale * dot(one_b[...], w_three[:, cs])).astype(BF16)

    layer(weighted)

    def adjoint_two(cs):
        one_b[:, cs] = (s_two[:, cs] * dot_t(two_b[...], w_three[cs, :])).astype(BF16)

    layer(adjoint_two)

    def adjoint_one(cs):
        two_b[:, cs] = (s_one[:, cs] * dot_t(one_b[...], w_two[cs, :])).astype(BF16)

    layer(adjoint_one)

    def adjoint_cells(cs):
        column = dot_t(two_b[...], w_one[cs, :]).astype(BF16)
        out[:, cs] = dot(place[...], column).astype(BF16)

    layer(adjoint_cells)


def near_adjoint_kernel(
    flip, cells_own, cells_near, own, near, courant,
    kept_a, kept_b, kept_c,
    table, mats, cells_b, mid_b, mid_f,
):
    levels = cells_own.shape[1]
    rows, lon = 4, table.shape[1]
    cells = rows * lon
    sign = jnp.where(flip[0] == 1, -1.0, 1.0)
    store_sources(table, 1, own[cells:, 0:lon], False, sign, lon, rows)
    store_sources(table, 2, near[cells:, 0:lon], True, sign, lon, rows)
    k = 0
    for order, exts in enumerate(((5, 7, 9), (6, 8), (7,))):
        for ext in exts:
            push_matrix(mats.at[k], table, 3 - order, ext, lon, rows)
            k += 1
    cells_b[0:cells, :] = cells_own[...]
    for j in range(rows):
        cells_b[(rows + j) * lon : (rows + j + 1) * lon, :] = cells_near[
            (rows - 1 - j) * lon : (rows - j) * lon, :
        ]

    @pl.loop(0, levels // LANE)
    def _(i):
        cs = pl.ds(pl.multiple_of(i * LANE, LANE), LANE)
        near_steps(
            mats, lambda at, size: cells_b[at : at + size, cs],
            lambda at, size: cells_b[at : at + size, cs].astype(F32), courant,
            (kept_a, kept_b, kept_c), mid_b, mid_f, lon, cs,
        )


def far_adjoint_kernel(
    flip, cells_own, cells_far, own, far, courant, kept_a, kept_b, kept_c,
    out,
    table, mats, cells_b, mid_b, mid_f, result, sem,
):
    levels = cells_own.shape[1]
    rows, lon = 4, table.shape[1]
    cells = rows * lon
    sign = jnp.where(flip[0] == 1, -1.0, 1.0)
    store_sources(table, 0, far[cells:, 0:lon], True, sign, lon, rows)
    store_sources(table, 1, own[cells:, 0:lon], False, sign, lon, rows)
    for order in range(4):
        for half in range(2):
            push_matrix(mats.at[2 * order + half], table, 3 - order, order + 1 + 2 * half, lon, rows)
    for j in range(rows):
        cells_b[j * lon : (j + 1) * lon, :] = cells_far[(rows - 1 - j) * lon : (rows - j) * lon, :]
    cells_b[cells:, :] = cells_own[0 : 2 * lon, :]

    @pl.loop(0, levels // LANE)
    def _(i):
        cs = pl.ds(pl.multiple_of(i * LANE, LANE), LANE)
        done = far_steps(
            mats, lambda at, size: cells_b[at : at + size, cs],
            lambda at, size: cells_b[at : at + size, cs].astype(F32), courant,
            (kept_a, kept_b, kept_c), mid_b, mid_f, lon, cs,
        )
        for half in range(2):
            for part in range(2):
                result[2 * half + part, :, cs] = done[half][part * lon : (part + 1) * lon, :]

    copies = []
    for j in range(rows):
        at = jnp.where(flip[0] == 1, rows - 1 - j, j)
        copies.append(pltpu.make_async_copy(result.at[j], out.at[at], sem.at[j]))
        copies[-1].start()
    for copy in copies:
        copy.wait()


def params():
    return pltpu.CompilerParams(vmem_limit_bytes=VMEM_LIMIT)


def local(
    tangent,
    wind_code,
    courant,
    obs_index,
    obs_count,
    obs_quality,
    background,
    w_first,
    w_second,
    w_third,
    chan_weight,
):
    rows, lon, levels = tangent.shape
    steps = wind_code.shape[0]
    cells = rows * lon
    slots = obs_index.shape[1]
    hidden_size = w_first.shape[1]
    count = lax.axis_size("lat")
    here = lax.axis_index("lat")
    odd = (here % 2).astype(jnp.int32)
    flip = odd.reshape(1)
    pairs = [(i, i ^ 1) for i in range(count)]
    links = [(i, i + 1) for i in range(1, count - 1, 2)]
    links = links + [(b, a) for a, b in links]

    codes = jnp.where(odd == 1, wind_code[:, ::-1], wind_code) + 1
    codes = codes.reshape(steps * rows, lon)
    own = pl.pallas_call(
        pack_kernel,
        out_shape=jax.ShapeDtypeStruct((cells + steps * rows, levels), BF16),
        in_specs=[SMEM, ANY, VMEM],
        out_specs=VMEM,
        scratch_shapes=[pltpu.VMEM((rows, lon, levels), F32), pltpu.SemaphoreType.DMA((rows,))],
        compiler_params=params(),
        name="pack",
    )(flip, tangent, codes)

    near = lax.ppermute(own, "lat", pairs)
    far = lax.ppermute(own, "lat", links)

    c_row = courant.reshape(1, levels)
    slot_ids = jnp.arange(slots, dtype=jnp.int32)
    observed = slot_ids < obs_count[0]
    where_at = obs_index[0]
    where_at = jnp.where(odd == 1, where_at + (rows - 1 - 2 * (where_at // lon)) * lon, where_at)
    where_at = jnp.where(observed, where_at, -1)
    quality = jnp.where(observed, obs_quality[0].astype(F32), 0.0)

    kept_shape = [jax.ShapeDtypeStruct((2 * lon, levels), F32)] * 3
    slope_shape = jax.ShapeDtypeStruct((slots, hidden_size), F32)
    slope_one, slope_two, kept_a, kept_b, kept_c = pl.pallas_call(
        near_kernel,
        out_shape=[slope_shape, slope_shape] + kept_shape,
        in_specs=[SMEM, ANY, VMEM, VMEM, VMEM, ANY, ANY, ANY],
        out_specs=[ANY, ANY, VMEM, VMEM, VMEM],
        scratch_shapes=[
            pltpu.VMEM((lon, lon), F32),
            pltpu.VMEM((6, 2 * lon, 4 * lon), BF16),
            pltpu.VMEM((rows, lon, levels), F32),
            pltpu.VMEM((2 * cells, levels), BF16),
            pltpu.VMEM((2, 6 * lon, LANE), BF16),
            pltpu.VMEM((2, 6 * lon, LANE), F32),
            pltpu.VMEM((slots, levels), BF16),
            pltpu.VMEM(w_first.shape, BF16),
            pltpu.VMEM(w_second.shape, BF16),
            pltpu.VMEM((slots, hidden_size), BF16),
            pltpu.VMEM((slots, hidden_size), F32),
            pltpu.VMEM((slots, hidden_size), F32),
            pltpu.SemaphoreType.DMA((5 + rows,)),
        ],
        compiler_params=params(),
        cost_estimate=pl.CostEstimate(flops=4_000_000_000, bytes_accessed=16_000_000, transcendentals=1_000_000),
        name="near",
    )(flip, tangent, own, near, c_row, background[0], w_first, w_second)

    cells_own = pl.pallas_call(
        observe_kernel,
        out_shape=jax.ShapeDtypeStruct((cells, levels), BF16),
        in_specs=[SMEM, ANY, VMEM, VMEM, VMEM, VMEM, ANY, ANY, VMEM, VMEM, VMEM, ANY, ANY, ANY]
        + [VMEM] * 4,
        out_specs=VMEM,
        scratch_shapes=[
            pltpu.VMEM((lon, lon), F32),
            pltpu.VMEM((8, 2 * lon, 4 * lon), BF16),
            pltpu.VMEM((lon, levels), F32),
            pltpu.VMEM((6 * lon, levels), BF16),
            pltpu.VMEM((3, 6 * lon, LANE), BF16),
            pltpu.VMEM((3, 6 * lon, LANE), F32),
            pltpu.VMEM((cells, LANE), BF16),
            pltpu.VMEM(w_first.shape, BF16),
            pltpu.VMEM(w_second.shape, BF16),
            pltpu.VMEM(w_third.shape, BF16),
            pltpu.VMEM((slots, hidden_size), F32),
            pltpu.VMEM((slots, hidden_size), F32),
            pltpu.VMEM((slots, cells), BF16),
            pltpu.VMEM((cells, slots), BF16),
            pltpu.VMEM((slots, levels), BF16),
            pltpu.VMEM((slots, levels), BF16),
            pltpu.SemaphoreType.DMA((6,)),
        ],
        compiler_params=params(),
        name="observe",
    )(
        flip, tangent, own, near, far, c_row, slope_one, slope_two, kept_a, kept_b, kept_c,
        w_first, w_second, w_third, where_at.reshape(slots, 1), where_at.reshape(1, slots),
        quality.reshape(slots, 1), chan_weight.reshape(1, -1),
    )

    cells_near = lax.ppermute(cells_own, "lat", pairs)
    cells_far = lax.ppermute(cells_own, "lat", links)

    kept_a, kept_b, kept_c = pl.pallas_call(
        near_adjoint_kernel,
        out_shape=kept_shape,
        in_specs=[SMEM] + [VMEM] * 5,
        out_specs=[VMEM] * 3,
        scratch_shapes=[
            pltpu.VMEM((lon, lon), F32),
            pltpu.VMEM((6, 2 * lon, 4 * lon), BF16),
            pltpu.VMEM((2 * cells, levels), BF16),
            pltpu.VMEM((2, 6 * lon, LANE), BF16),
            pltpu.VMEM((2, 6 * lon, LANE), F32),
        ],
        compiler_params=params(),
        cost_estimate=pl.CostEstimate(flops=2_000_000_000, bytes_accessed=8_000_000, transcendentals=0),
        name="near_adjoint",
    )(flip, cells_own, cells_near, own, near, c_row)

    return pl.pallas_call(
        far_adjoint_kernel,
        out_shape=jax.ShapeDtypeStruct((rows, lon, levels), F32),
        in_specs=[SMEM] + [VMEM] * 8,
        out_specs=ANY,
        scratch_shapes=[
            pltpu.VMEM((lon, lon), F32),
            pltpu.VMEM((8, 2 * lon, 4 * lon), BF16),
            pltpu.VMEM((6 * lon, levels), BF16),
            pltpu.VMEM((3, 6 * lon, LANE), BF16),
            pltpu.VMEM((3, 6 * lon, LANE), F32),
            pltpu.VMEM((rows, lon, levels), F32),
            pltpu.SemaphoreType.DMA((rows,)),
        ],
        compiler_params=params(),
        name="far_adjoint",
    )(flip, cells_own, cells_far, own, far, c_row, kept_a, kept_b, kept_c)


def solution(mesh):
    placed = (
        P(("groups", "lat"), None, None),
        P(None, ("groups", "lat"), None),
        P(),
        P(("groups", "lat"), None),
        P(("groups", "lat")),
        P(("groups", "lat"), None),
        P(("groups", "lat"), None, None),
        P(),
        P(),
        P(),
        P(),
    )
    return jax.shard_map(
        local,
        mesh=mesh,
        in_specs=placed,
        out_specs=P(("groups", "lat"), None, None),
        check_vma=False,
    )
```

```python
import functools

import jax
import jax.numpy as jnp
from jax import lax
from jax.experimental import pallas as pl
from jax.experimental.pallas import tpu as pltpu
from jax.sharding import PartitionSpec as P

F32 = jnp.float32
BF16 = jnp.bfloat16
FAR_CELLS = 304
FAR_COLUMNS = 272
ANY = pl.BlockSpec(memory_space=pl.ANY)
VMEM = pl.BlockSpec(memory_space=pltpu.VMEM)
HBM = pl.BlockSpec(memory_space=pltpu.HBM)
SMEM = pl.BlockSpec(memory_space=pltpu.SMEM)
VMEM_LIMIT = 28 * 1024 * 1024


def dot_t(left, right):
    return lax.dot_general(left, right, (((1,), (1,)), ((), ())), preferred_element_type=F32)


def dot(left, right):
    return jnp.dot(left, right, preferred_element_type=F32)


def store_sources(table, slot, codes, mirrored, sign, lon, rows):
    code = codes.astype(F32) - 1.0
    lat_q = jnp.where(code >= 5.0, 1.0, 0.0) + jnp.where(code >= 10.0, 1.0, 0.0)
    lon_step = code - 5.0 * lat_q - 2.0
    col = lax.broadcasted_iota(jnp.int32, code.shape, 1).astype(F32) - lon_step
    col = jnp.where(col < 0.0, col + lon, jnp.where(col >= lon, col - lon, col))
    stored = lax.broadcasted_iota(jnp.int32, code.shape, 0) & (rows - 1)
    row = (rows - 1 - stored) if mirrored else stored
    row = (row + slot * rows).astype(F32)
    src = (row - sign * (lat_q - 1.0)) * lon + col
    table[slot * code.shape[0] : (slot + 1) * code.shape[0], :] = jnp.where(code < 0.0, -65536.0, src)


def table_row(step, ext, rows):
    slot, at = ext // rows, ext % rows
    return slot * rows * rows + step * rows + (at if slot == 1 else rows - 1 - at)


def pull_matrix(out, turned, step, ext, lon, rows):
    span = 4 * lon
    lanes = lax.broadcasted_iota(jnp.int32, (lon, span), 1).astype(F32) + float((ext - 1) * lon)
    for half in range(2):
        k = table_row(step, ext + half, rows)
        column = turned[:, k : k + 1]
        out[half * lon : (half + 1) * lon, :] = jnp.where(column == lanes, 1.0, 0.0).astype(BF16)


def push_matrix(out, table, step, ext, lon, rows):
    dest = lax.broadcasted_iota(jnp.int32, (2 * lon, lon), 0).astype(F32) + float(ext * lon)
    for part in range(4):
        k = table_row(step, ext - 1 + part, rows)
        line = table[k : k + 1, :]
        out[:, part * lon : (part + 1) * lon] = jnp.where(line == dest, 1.0, 0.0).astype(BF16)


def wind_fields(codes, sign, rows):
    code = codes.astype(F32) - 1.0
    lat_q = jnp.where(code >= 5.0, 1.0, 0.0) + jnp.where(code >= 10.0, 1.0, 0.0)
    lat = jnp.where(code < 0.0, 9.0, sign * (lat_q - 1.0))
    lon = code - 5.0 * lat_q - 2.0
    fill = jnp.full((8 - rows, code.shape[1]), 9.0, F32)
    fields = []
    for step in range(code.shape[0] // rows):
        at = slice(step * rows, (step + 1) * rows)
        fields.append((jnp.concatenate([lat[at], fill], axis=0), jnp.concatenate([lon[at], fill], axis=0)))
    return fields


def shift_rows(mask, by):
    blank = jnp.zeros((1, mask.shape[1]), F32)
    if by == 1:
        return jnp.concatenate([blank, mask[:-1]], axis=0)
    if by == -1:
        return jnp.concatenate([mask[1:], blank], axis=0)
    return mask


def cells_pulled(fields, rows):
    lon = fields[0][0].shape[1]
    row = lax.broadcasted_iota(jnp.int32, (8, lon), 0)
    mask = jnp.where(row == 0, 1.0, 0.0)
    for lat, east in reversed(fields[: len(fields) - 1]):
        new = mask
        for a in (-1, 0, 1):
            total = jnp.zeros_like(mask)
            for b in range(-2, 3):
                hit = jnp.where((lat == float(a)) & (east == float(b)), mask, 0.0)
                total = jnp.maximum(total, hit if b == 0 else pltpu.roll(hit, (-b) % lon, 1))
            new = jnp.maximum(new, shift_rows(total, -a))
        mask = jnp.where(row < rows, new, 0.0)
    return mask


def cells_reached(fields, rows):
    lon = fields[0][0].shape[1]
    row = lax.broadcasted_iota(jnp.int32, (8, lon), 0)
    mask = jnp.zeros((8, lon), F32)
    for lat, east in fields:
        new = mask
        for a in (-1, 0, 1):
            source = shift_rows(mask, a)
            if a == 1:
                source = jnp.where(row == 0, 1.0, source)
            for b in range(-2, 3):
                seen = source if b == 0 else pltpu.roll(source, b % lon, 1)
                new = jnp.maximum(new, jnp.where((lat == float(a)) & (east == float(b)), seen, 0.0))
        mask = jnp.where(row < rows, new, 0.0)
    return mask


def slot_of(mask):
    lon = mask.shape[1]
    before = lax.broadcasted_iota(jnp.int32, (lon, lon), 0) < lax.broadcasted_iota(jnp.int32, (lon, lon), 1)
    place = dot(mask.astype(BF16), jnp.where(before, 1.0, 0.0).astype(BF16))
    totals = jnp.sum(mask, axis=1, keepdims=True)
    ahead = jnp.zeros((1, 1), F32)
    lines = []
    for j in range(mask.shape[0]):
        lines.append(place[j : j + 1] + ahead)
        ahead = ahead + totals[j : j + 1]
    return jnp.where(mask > 0.0, jnp.concatenate(lines, axis=0), -1.0), ahead


def choose_matrix(slots, size, rows, first=0):
    lon = slots.shape[1]
    at = lax.broadcasted_iota(jnp.int32, (size, lon), 0).astype(F32) + float(first)
    parts = [jnp.where(slots[j : j + 1] == at, 1.0, 0.0) for j in range(rows)]
    return jnp.concatenate(parts, axis=1).astype(BF16)


def spread_matrix(turned, row, size, first=0):
    at = lax.broadcasted_iota(jnp.int32, (turned.shape[0], size), 1).astype(F32) + float(first)
    return jnp.where(turned[:, row : row + 1] == at, 1.0, 0.0).astype(BF16)


def turn(slots):
    lon = slots.shape[1]
    return jnp.concatenate([slots, jnp.full((lon - slots.shape[0], lon), -1.0, F32)], axis=0).T


def sign_of(flip):
    return jnp.where(flip[0] == 1, -1.0, 1.0)


def pack_kernel(flip, tangent, wind, own, sent, slots, over, buf, codes, sem):
    rows, lon = tangent.shape[0], tangent.shape[1]
    cells = rows * lon
    copies = []
    for j in range(rows):
        at = jnp.where(flip[0] == 1, rows - 1 - j, j)
        copies.append(pltpu.make_async_copy(tangent.at[at], buf.at[j], sem.at[j]))
        copies[-1].start()
    for step in range(wind.shape[0]):
        for j in range(rows):
            code = jnp.where(flip[0] == 1, wind[step, rows - 1 - j : rows - j, :], wind[step, j : j + 1, :])
            codes[step * rows + j : step * rows + j + 1, :] = code.astype(F32) + 1.0
    mask = cells_pulled(wind_fields(codes[...], sign_of(flip), rows), rows)
    where, total = slot_of(mask)
    slots[...] = where
    capacity = sent.shape[0] - codes.shape[0]
    flag = jnp.where(total > float(capacity), 1.0, 0.0)
    over[...] = jnp.broadcast_to(flag, over.shape)
    head = codes.shape[0]
    tall = jnp.concatenate([mask, jnp.zeros((head - mask.shape[0], lon), F32)], axis=0)
    notes = jnp.concatenate(
        [codes[...], tall, jnp.broadcast_to(flag, (head, lon)), jnp.zeros((head, own.shape[1] - 3 * lon), F32)], axis=1
    ).astype(BF16)
    own[cells:, :] = notes
    sent[capacity:, :] = notes
    choose = choose_matrix(where, capacity, rows)
    for j in range(rows):
        copies[j].wait()
        own[j * lon : (j + 1) * lon, :] = buf[j].astype(BF16)
    sent[0:capacity, :] = dot(choose, own[0:cells, :]).astype(BF16)


def rest_kernel(first, slots, dense, out):
    rows = dense.shape[0] // slots.shape[1]
    cells = rows * slots.shape[1]
    choose = choose_matrix(slots[...], out.shape[0], rows, first)
    out[...] = dot(choose, dense[0:cells, :]).astype(BF16)


def blank_kernel(out):
    pass


def near_steps(mats, start_b, start_f, c_ref, outs, mid_b, mid_f, lon):
    c = c_ref[0:1, :]
    blocks = ((5, 7, 9), (6, 8), (7,))
    read_b, read_f, first = start_b, start_f, 4
    k = 0
    for step, exts in enumerate(blocks):
        for ext in exts:
            at = (ext - 1 - first) * lon
            pulled = dot(mats[k], read_b(at, 4 * lon))
            value = (1.0 - c) * read_f(at + lon, 2 * lon) + c * pulled
            k += 1
            if ext == exts[0]:
                outs[step][...] = value
            if step < 2:
                to = (ext - exts[0]) * lon
                mid_f[step, to : to + 2 * lon, :] = value
                mid_b[step, to : to + 2 * lon, :] = value.astype(BF16)
        first = exts[0]
        read_b = functools.partial(lambda s, a, n: mid_b[s, a : a + n, :], step)
        read_f = functools.partial(lambda s, a, n: mid_f[s, a : a + n, :], step)


def far_steps(mats, start_b, start_f, c_ref, kept, mid_b, mid_f, lon, finish):
    c = c_ref[0:1, :]
    k = 0
    for step in range(4):
        now, last = step % 2, (step + 1) % 2
        for half in range(2):
            at = 2 * half * lon
            if step == 0:
                window, own = start_b(at, 4 * lon), start_f(at + lon, 2 * lon)
            else:
                window = mid_b[last, at : at + 4 * lon, :]
                own = mid_f[last, at + lon : at + 3 * lon, :]
            value = (1.0 - c) * own + c * dot(mats[k], window)
            k += 1
            if step < 3:
                mid_f[now, at : at + 2 * lon, :] = value
                mid_b[now, at : at + 2 * lon, :] = value.astype(BF16)
            else:
                finish(half, value)
        if step < 3:
            carried = kept[step][...]
            mid_f[now, 4 * lon :, :] = carried
            mid_b[now, 4 * lon :, :] = carried.astype(BF16)


def near_kernel(
    flip, tangent, own, near, courant, background, w_first, w_second, where_col, where_row,
    slope_one, slope_two, kept_a, kept_b, kept_c, pick, place, place_far, slots,
    table, mats, cells_b, mid_b, mid_f, hidden,
):
    rows, lon = tangent.shape[0], tangent.shape[1]
    cells = rows * lon
    sign = sign_of(flip)
    table[...] = jnp.zeros_like(table)
    store_sources(table, 1, own[cells:, 0:lon], False, sign, lon, rows)
    store_sources(table, 2, near[cells:, 0:lon], True, sign, lon, rows)
    turned = table[...].T
    k = 0
    for step, exts in enumerate(((5, 7, 9), (6, 8), (7,))):
        for ext in exts:
            pull_matrix(mats.at[k], turned, step, ext, lon, rows)
            k += 1
    cells_b[0:cells, :] = own[0:cells, :]
    for j in range(rows):
        cells_b[(rows + j) * lon : (rows + j + 1) * lon, :] = near[(rows - 1 - j) * lon : (rows - j) * lon, :]

    def start_f(at, size):
        pieces = []
        for row in range(at // lon, (at + size) // lon):
            if row < rows:
                pieces.append(tangent[jnp.where(flip[0] == 1, rows - 1 - row, row)])
            else:
                pieces.append(cells_b[row * lon : (row + 1) * lon, :].astype(F32))
        return jnp.concatenate(pieces, axis=0)

    near_steps(
        mats, lambda at, size: cells_b[at : at + size, :], start_f, courant,
        (kept_a, kept_b, kept_c), mid_b, mid_f, lon,
    )

    first_tanh = jnp.tanh(dot(background[...], w_first[...]))
    hidden[...] = first_tanh.astype(BF16)
    slope_one[...] = 1.0 - first_tanh * first_tanh
    second_tanh = jnp.tanh(dot(hidden[...], w_second[...]))
    slope_two[...] = 1.0 - second_tanh * second_tanh

    count = where_col.shape[0]
    pick[...] = jnp.where(
        where_col[...] == lax.broadcasted_iota(jnp.int32, (count, cells), 1), 1.0, 0.0
    ).astype(BF16)
    place[...] = jnp.where(
        where_row[...] == lax.broadcasted_iota(jnp.int32, (cells, count), 0), 1.0, 0.0
    ).astype(BF16)
    where, _ = slot_of(cells_reached(wind_fields(own[cells:, 0:lon], sign, rows), rows))
    slots[...] = where
    place_far[...] = dot(choose_matrix(where, place_far.shape[0], rows), place[...]).astype(BF16)


def observe_kernel(
    flip, flag, tangent, own, far, rest, courant, slope_one, slope_two, kept_a, kept_b, kept_c,
    w_first, w_second, w_third, pick, place, place_far, quality, chan_weight,
    out, sent,
    table, mats, cells_b, mid_b, mid_f, last_b, one_b, two_b, rest_b, sem,
):
    rows, lon = tangent.shape[0], tangent.shape[1]
    cells = rows * lon
    sign = sign_of(flip)
    capacity = far.shape[0] - (own.shape[0] - cells)
    table[...] = jnp.zeros_like(table)
    store_sources(table, 0, far[capacity:, 0:lon], True, sign, lon, rows)
    store_sources(table, 1, own[cells:, 0:lon], False, sign, lon, rows)
    turned = table[...].T
    for step in range(4):
        for half in range(2):
            pull_matrix(mats.at[2 * step + half], turned, step, step + 1 + 2 * half, lon, rows)
    where, _ = slot_of(far[capacity:, lon : 2 * lon].astype(F32)[0:8])
    where = turn(where)
    for j in range(rows):
        value = dot(spread_matrix(where, j, capacity), far[0:capacity, :])
        cells_b[(rows - 1 - j) * lon : (rows - j) * lon, :] = value.astype(BF16)
    cells_b[cells:, :] = own[0 : 2 * lon, :]

    @pl.when(flag[0] > 0)
    def _():
        copy = pltpu.make_async_copy(rest, rest_b, sem.at[0])
        copy.start()
        copy.wait()
        for j in range(rows):
            value = dot(spread_matrix(where, j, rest_b.shape[0], capacity), rest_b[...])
            at = slice((rows - 1 - j) * lon, (rows - j) * lon)
            cells_b[at, :] = (cells_b[at, :].astype(F32) + value).astype(BF16)

    def start_f(at, size):
        pieces = []
        for row in range(at // lon, (at + size) // lon):
            if row == rows:
                pieces.append(tangent[jnp.where(flip[0] == 1, rows - 1, 0)])
            else:
                pieces.append(cells_b[row * lon : (row + 1) * lon, :].astype(F32))
        return jnp.concatenate(pieces, axis=0)

    def finish(half, value):
        last_b[2 * half * lon : 2 * (half + 1) * lon, :] = value.astype(BF16)

    far_steps(
        mats, lambda at, size: cells_b[at : at + size, :], start_f, courant,
        (kept_a, kept_b, kept_c), mid_b, mid_f, lon, finish,
    )
    one_b[...] = dot(pick[...], last_b[...]).astype(BF16)
    two_b[...] = (slope_one[...] * dot(one_b[...], w_first[...])).astype(BF16)
    one_b[...] = (slope_two[...] * dot(two_b[...], w_second[...])).astype(BF16)
    scale = quality[...] * chan_weight[0:1, :]
    two_b[...] = (scale * dot(one_b[...], w_third[...])).astype(BF16)
    one_b[...] = (slope_two[...] * dot_t(two_b[...], w_third[...])).astype(BF16)
    two_b[...] = (slope_one[...] * dot_t(one_b[...], w_second[...])).astype(BF16)
    one_b[...] = dot_t(two_b[...], w_first[...]).astype(BF16)
    sent[...] = dot(place_far[...], one_b[...]).astype(BF16)
    out[...] = dot(place[...], one_b[...]).astype(BF16)


def near_adjoint_kernel(
    flip, cells_own, cells_near, own, near, far, own_slots, courant,
    kept_a, kept_b, kept_c, far_mats, spread, far_slots, over,
    table, mats, cells_b, mid_b, mid_f,
):
    rows, lon = 4, table.shape[1]
    cells = rows * lon
    sign = sign_of(flip)
    head = own.shape[0] - cells
    far_codes = far[far.shape[0] - head :, 0:lon]
    store_sources(table, 0, far_codes, True, sign, lon, rows)
    store_sources(table, 1, own[cells:, 0:lon], False, sign, lon, rows)
    store_sources(table, 2, near[cells:, 0:lon], True, sign, lon, rows)
    k = 0
    for order, exts in enumerate(((5, 7, 9), (6, 8), (7,))):
        for ext in exts:
            push_matrix(mats.at[k], table, 3 - order, ext, lon, rows)
            k += 1
    cells_b[0:cells, :] = cells_own[...]
    for j in range(rows):
        cells_b[(rows + j) * lon : (rows + j + 1) * lon, :] = cells_near[
            (rows - 1 - j) * lon : (rows - j) * lon, :
        ]
    near_steps(
        mats, lambda at, size: cells_b[at : at + size, :],
        lambda at, size: cells_b[at : at + size, :].astype(F32), courant,
        (kept_a, kept_b, kept_c), mid_b, mid_f, lon,
    )
    for order in range(4):
        for half in range(2):
            push_matrix(far_mats.at[2 * order + half], table, 3 - order, order + 1 + 2 * half, lon, rows)
    where, total = slot_of(cells_reached(wind_fields(far_codes, -sign, rows), rows))
    far_slots[...] = where
    where = turn(where)
    capacity = spread.shape[1]
    for j in range(rows):
        spread[j * lon : (j + 1) * lon, :] = spread_matrix(where, j, capacity)
    most = jnp.maximum(jnp.max(own_slots[...], axis=(0, 1), keepdims=True) + 1.0, total)
    over[...] = jnp.broadcast_to(jnp.where(most > float(capacity), 1.0, 0.0), over.shape)


def far_adjoint_kernel(
    flip, flag, cells_own, far, rest, courant, kept_a, kept_b, kept_c, mats, spread, far_slots,
    out,
    cells_b, mid_b, mid_f, result, rest_b, sem,
):
    rows, lon = out.shape[0], out.shape[1]
    cells = rows * lon
    for j in range(rows):
        value = dot(spread[j * lon : (j + 1) * lon, :], far[...])
        cells_b[(rows - 1 - j) * lon : (rows - j) * lon, :] = value.astype(BF16)
    cells_b[cells:, :] = cells_own[0 : 2 * lon, :]

    @pl.when(flag[0] > 0)
    def _():
        copy = pltpu.make_async_copy(rest, rest_b, sem.at[rows])
        copy.start()
        copy.wait()
        where = turn(far_slots[...])
        for j in range(rows):
            value = dot(spread_matrix(where, j, rest_b.shape[0], spread.shape[1]), rest_b[...])
            at = slice((rows - 1 - j) * lon, (rows - j) * lon)
            cells_b[at, :] = (cells_b[at, :].astype(F32) + value).astype(BF16)

    copies = []

    def finish(half, value):
        for part in range(2):
            j = 2 * half + part
            result[j] = value[part * lon : (part + 1) * lon, :]
            at = jnp.where(flip[0] == 1, rows - 1 - j, j)
            copies.append(pltpu.make_async_copy(result.at[j], out.at[at], sem.at[j]))
            copies[-1].start()

    far_steps(
        mats, lambda at, size: cells_b[at : at + size, :],
        lambda at, size: cells_b[at : at + size, :].astype(F32), courant,
        (kept_a, kept_b, kept_c), mid_b, mid_f, lon, finish,
    )
    for copy in copies:
        copy.wait()


def params():
    return pltpu.CompilerParams(vmem_limit_bytes=VMEM_LIMIT)


def shape(dims, dtype):
    return jax.ShapeDtypeStruct(dims, dtype)


def second_exchange(flag, first, slots, dense, size, links):
    out = shape((size, dense.shape[1]), BF16)

    def send():
        rest = pl.pallas_call(
            functools.partial(rest_kernel, first),
            out_shape=out,
            in_specs=[VMEM, VMEM],
            out_specs=VMEM,
            compiler_params=params(),
            name="rest",
        )(slots, dense)
        return lax.ppermute(rest, "lat", links)

    def skip():
        return pl.pallas_call(blank_kernel, out_shape=out, out_specs=ANY, name="blank")()

    return lax.cond(flag, send, skip)


def local(
    tangent,
    wind_code,
    courant,
    obs_index,
    obs_count,
    obs_quality,
    background,
    w_first,
    w_second,
    w_third,
    chan_weight,
):
    rows, lon, levels = tangent.shape
    cells = rows * lon
    head = wind_code.shape[0] * rows
    listed = obs_index.shape[1]
    hidden_size = w_first.shape[1]
    count = lax.axis_size("lat")
    here = lax.axis_index("lat")
    odd = (here % 2).astype(jnp.int32)
    flip = odd.reshape(1)
    linked = (here > 0) & (here < count - 1)
    pairs = [(i, i ^ 1) for i in range(count)]
    links = [(i, i + 1) for i in range(1, count - 1, 2)]
    links = links + [(b, a) for a, b in links]

    own, sent, slots, over = pl.pallas_call(
        pack_kernel,
        out_shape=[
            shape((cells + head, levels), BF16),
            shape((FAR_CELLS + head, levels), BF16),
            shape((8, lon), F32),
            shape((8, lon), F32),
        ],
        in_specs=[SMEM, HBM, VMEM],
        out_specs=[VMEM] * 4,
        scratch_shapes=[
            pltpu.VMEM((rows, lon, levels), F32),
            pltpu.VMEM((head, lon), F32),
            pltpu.SemaphoreType.DMA((rows,)),
        ],
        compiler_params=params(),
        name="pack",
    )(flip, tangent, wind_code)

    far = lax.ppermute(sent, "lat", links)
    near = lax.ppermute(own, "lat", pairs)

    c_row = courant.reshape(1, levels)
    slot_ids = jnp.arange(listed, dtype=jnp.int32)
    observed = slot_ids < obs_count[0]
    where_at = obs_index[0]
    where_at = jnp.where(odd == 1, where_at + (rows - 1 - 2 * (where_at // lon)) * lon, where_at)
    where_at = jnp.where(observed, where_at, -1)
    quality = jnp.where(observed, obs_quality[0].astype(F32), 0.0)

    kept_shape = [shape((2 * lon, levels), F32)] * 3
    slope_shape = shape((listed, hidden_size), F32)
    slope_one, slope_two, kept_a, kept_b, kept_c, pick, place, place_far, own_slots = pl.pallas_call(
        near_kernel,
        out_shape=[slope_shape, slope_shape]
        + kept_shape
        + [
            shape((listed, cells), BF16),
            shape((cells, listed), BF16),
            shape((FAR_COLUMNS, listed), BF16),
            shape((8, lon), F32),
        ],
        in_specs=[SMEM] + [VMEM] * 9,
        out_specs=[VMEM] * 9,
        scratch_shapes=[
            pltpu.VMEM((lon, lon), F32),
            pltpu.VMEM((6, 2 * lon, 4 * lon), BF16),
            pltpu.VMEM((2 * cells, levels), BF16),
            pltpu.VMEM((2, 6 * lon, levels), BF16),
            pltpu.VMEM((2, 6 * lon, levels), F32),
            pltpu.VMEM((listed, hidden_size), BF16),
        ],
        compiler_params=params(),
        cost_estimate=pl.CostEstimate(flops=4_000_000_000, bytes_accessed=16_000_000, transcendentals=1_000_000),
        name="near",
    )(
        flip, tangent, own, near, c_row, background[0], w_first, w_second,
        where_at.reshape(listed, 1), where_at.reshape(1, listed),
    )

    flag = linked & ((over[0, 0] > 0.0) | (far[FAR_CELLS, 2 * lon] > 0.0))
    rest = second_exchange(flag, FAR_CELLS, slots, own, cells - FAR_CELLS, links)
    cells_own, sent = pl.pallas_call(
        observe_kernel,
        out_shape=[shape((cells, levels), BF16), shape((FAR_COLUMNS, levels), BF16)],
        in_specs=[SMEM, SMEM, VMEM, VMEM, VMEM, ANY] + [VMEM] * 14,
        out_specs=[VMEM] * 2,
        scratch_shapes=[
            pltpu.VMEM((lon, lon), F32),
            pltpu.VMEM((8, 2 * lon, 4 * lon), BF16),
            pltpu.VMEM((6 * lon, levels), BF16),
            pltpu.VMEM((2, 6 * lon, levels), BF16),
            pltpu.VMEM((2, 6 * lon, levels), F32),
            pltpu.VMEM((cells, levels), BF16),
            pltpu.VMEM((listed, levels), BF16),
            pltpu.VMEM((listed, levels), BF16),
            pltpu.VMEM((cells - FAR_CELLS, levels), BF16),
            pltpu.SemaphoreType.DMA((1,)),
        ],
        compiler_params=params(),
        name="observe",
    )(
        flip, flag.astype(jnp.int32).reshape(1), tangent, own, far, rest, c_row,
        slope_one, slope_two, kept_a, kept_b, kept_c, w_first, w_second, w_third,
        pick, place, place_far, quality.reshape(listed, 1), chan_weight.reshape(1, -1),
    )

    columns_far = lax.ppermute(sent, "lat", links)
    cells_near = lax.ppermute(cells_own, "lat", pairs)

    kept_a, kept_b, kept_c, mats, spread, far_slots, over = pl.pallas_call(
        near_adjoint_kernel,
        out_shape=kept_shape
        + [
            shape((8, 2 * lon, 4 * lon), BF16),
            shape((cells, FAR_COLUMNS), BF16),
            shape((8, lon), F32),
            shape((8, lon), F32),
        ],
        in_specs=[SMEM] + [VMEM] * 7,
        out_specs=[VMEM] * 7,
        scratch_shapes=[
            pltpu.VMEM((lon, lon), F32),
            pltpu.VMEM((6, 2 * lon, 4 * lon), BF16),
            pltpu.VMEM((2 * cells, levels), BF16),
            pltpu.VMEM((2, 6 * lon, levels), BF16),
            pltpu.VMEM((2, 6 * lon, levels), F32),
        ],
        compiler_params=params(),
        cost_estimate=pl.CostEstimate(flops=2_000_000_000, bytes_accessed=8_000_000, transcendentals=0),
        name="near_adjoint",
    )(flip, cells_own, cells_near, own, near, far, own_slots, c_row)

    flag = linked & (over[0, 0] > 0.0)
    rest = second_exchange(flag, FAR_COLUMNS, own_slots, cells_own, cells - FAR_COLUMNS, links)
    return pl.pallas_call(
        far_adjoint_kernel,
        out_shape=shape((rows, lon, levels), F32),
        in_specs=[SMEM, SMEM, VMEM, VMEM, ANY] + [VMEM] * 7,
        out_specs=HBM,
        scratch_shapes=[
            pltpu.VMEM((6 * lon, levels), BF16),
            pltpu.VMEM((2, 6 * lon, levels), BF16),
            pltpu.VMEM((2, 6 * lon, levels), F32),
            pltpu.VMEM((rows, lon, levels), F32),
            pltpu.VMEM((cells - FAR_COLUMNS, levels), BF16),
            pltpu.SemaphoreType.DMA((rows + 1,)),
        ],
        compiler_params=params(),
        name="far_adjoint",
    )(
        flip, flag.astype(jnp.int32).reshape(1), cells_own, columns_far, rest, c_row,
        kept_a, kept_b, kept_c, mats, spread, far_slots,
    )


def solution(mesh):
    placed = (
        P(("groups", "lat"), None, None),
        P(None, ("groups", "lat"), None),
        P(),
        P(("groups", "lat"), None),
        P(("groups", "lat")),
        P(("groups", "lat"), None),
        P(("groups", "lat"), None, None),
        P(),
        P(),
        P(),
        P(),
    )
    return jax.shard_map(
        local,
        mesh=mesh,
        in_specs=placed,
        out_specs=P(("groups", "lat"), None, None),
        check_vma=False,
    )
```

```python
import functools

import jax
import jax.numpy as jnp
from jax import lax
from jax.experimental import pallas as pl
from jax.experimental.pallas import tpu as pltpu
from jax.sharding import PartitionSpec as P

F32 = jnp.float32
BF16 = jnp.bfloat16
FAR_CELLS = 304
FAR_COLUMNS = 272
ANY = pl.BlockSpec(memory_space=pl.ANY)
VMEM = pl.BlockSpec(memory_space=pltpu.VMEM)
HBM = pl.BlockSpec(memory_space=pltpu.HBM)
SMEM = pl.BlockSpec(memory_space=pltpu.SMEM)
VMEM_LIMIT = 28 * 1024 * 1024
PACK_LIMIT = 60 * 1024 * 1024


def dot_t(left, right):
    return lax.dot_general(left, right, (((1,), (1,)), ((), ())), preferred_element_type=F32)


def dot(left, right):
    return jnp.dot(left, right, preferred_element_type=F32)


def store_sources(table, slot, codes, mirrored, sign, lon, rows):
    code = codes.astype(F32) - 1.0
    lat_q = jnp.where(code >= 5.0, 1.0, 0.0) + jnp.where(code >= 10.0, 1.0, 0.0)
    lon_step = code - 5.0 * lat_q - 2.0
    col = lax.broadcasted_iota(jnp.int32, code.shape, 1).astype(F32) - lon_step
    col = jnp.where(col < 0.0, col + lon, jnp.where(col >= lon, col - lon, col))
    stored = lax.broadcasted_iota(jnp.int32, code.shape, 0) & (rows - 1)
    row = (rows - 1 - stored) if mirrored else stored
    row = (row + slot * rows).astype(F32)
    src = (row - sign * (lat_q - 1.0)) * lon + col
    table[slot * code.shape[0] : (slot + 1) * code.shape[0], :] = jnp.where(code < 0.0, -65536.0, src)


def table_row(step, ext, rows):
    slot, at = ext // rows, ext % rows
    return slot * rows * rows + step * rows + (at if slot == 1 else rows - 1 - at)


def pull_matrix(out, turned, step, ext, lon, rows):
    span = 4 * lon
    lanes = lax.broadcasted_iota(jnp.int32, (lon, span), 1).astype(F32) + float((ext - 1) * lon)
    for half in range(2):
        k = table_row(step, ext + half, rows)
        column = turned[:, k : k + 1]
        out[half * lon : (half + 1) * lon, :] = jnp.where(column == lanes, 1.0, 0.0).astype(BF16)


def push_matrix(out, table, step, ext, lon, rows):
    dest = lax.broadcasted_iota(jnp.int32, (2 * lon, lon), 0).astype(F32) + float(ext * lon)
    for part in range(4):
        k = table_row(step, ext - 1 + part, rows)
        line = table[k : k + 1, :]
        out[:, part * lon : (part + 1) * lon] = jnp.where(line == dest, 1.0, 0.0).astype(BF16)


def wind_fields(codes, sign, rows):
    code = codes.astype(F32) - 1.0
    lat_q = jnp.where(code >= 5.0, 1.0, 0.0) + jnp.where(code >= 10.0, 1.0, 0.0)
    lat = jnp.where(code < 0.0, 9.0, sign * (lat_q - 1.0))
    lon = code - 5.0 * lat_q - 2.0
    fill = jnp.full((8 - rows, code.shape[1]), 9.0, F32)
    fields = []
    for step in range(code.shape[0] // rows):
        at = slice(step * rows, (step + 1) * rows)
        fields.append((jnp.concatenate([lat[at], fill], axis=0), jnp.concatenate([lon[at], fill], axis=0)))
    return fields


def shift_rows(mask, by):
    blank = jnp.zeros((1, mask.shape[1]), F32)
    if by == 1:
        return jnp.concatenate([blank, mask[:-1]], axis=0)
    if by == -1:
        return jnp.concatenate([mask[1:], blank], axis=0)
    return mask


def cells_pulled(fields, rows):
    lon = fields[0][0].shape[1]
    row = lax.broadcasted_iota(jnp.int32, (8, lon), 0)
    mask = jnp.where(row == 0, 1.0, 0.0)
    for lat, east in reversed(fields[: len(fields) - 1]):
        new = mask
        for a in (-1, 0, 1):
            total = jnp.zeros_like(mask)
            for b in range(-2, 3):
                hit = jnp.where((lat == float(a)) & (east == float(b)), mask, 0.0)
                total = jnp.maximum(total, hit if b == 0 else pltpu.roll(hit, (-b) % lon, 1))
            new = jnp.maximum(new, shift_rows(total, -a))
        mask = jnp.where(row < rows, new, 0.0)
    return mask


def cells_reached(fields, rows):
    lon = fields[0][0].shape[1]
    row = lax.broadcasted_iota(jnp.int32, (8, lon), 0)
    mask = jnp.zeros((8, lon), F32)
    for lat, east in fields:
        new = mask
        for a in (-1, 0, 1):
            source = shift_rows(mask, a)
            if a == 1:
                source = jnp.where(row == 0, 1.0, source)
            for b in range(-2, 3):
                seen = source if b == 0 else pltpu.roll(source, b % lon, 1)
                new = jnp.maximum(new, jnp.where((lat == float(a)) & (east == float(b)), seen, 0.0))
        mask = jnp.where(row < rows, new, 0.0)
    return mask


def slot_of(mask):
    lon = mask.shape[1]
    before = lax.broadcasted_iota(jnp.int32, (lon, lon), 0) < lax.broadcasted_iota(jnp.int32, (lon, lon), 1)
    place = dot(mask.astype(BF16), jnp.where(before, 1.0, 0.0).astype(BF16))
    totals = jnp.sum(mask, axis=1, keepdims=True)
    ahead = jnp.zeros((1, 1), F32)
    lines = []
    for j in range(mask.shape[0]):
        lines.append(place[j : j + 1] + ahead)
        ahead = ahead + totals[j : j + 1]
    return jnp.where(mask > 0.0, jnp.concatenate(lines, axis=0), -1.0), ahead


def choose_matrix(slots, size, rows, first=0):
    lon = slots.shape[1]
    at = lax.broadcasted_iota(jnp.int32, (size, lon), 0).astype(F32) + float(first)
    parts = [jnp.where(slots[j : j + 1] == at, 1.0, 0.0) for j in range(rows)]
    return jnp.concatenate(parts, axis=1).astype(BF16)


def spread_matrix(turned, row, size, first=0):
    at = lax.broadcasted_iota(jnp.int32, (turned.shape[0], size), 1).astype(F32) + float(first)
    return jnp.where(turned[:, row : row + 1] == at, 1.0, 0.0).astype(BF16)


def turn(slots):
    lon = slots.shape[1]
    return jnp.concatenate([slots, jnp.full((lon - slots.shape[0], lon), -1.0, F32)], axis=0).T


def sign_of(flip):
    return jnp.where(flip[0] == 1, -1.0, 1.0)


def pack_kernel(flip, tangent, wind, own, sent, codes, slots, buf, wind_b, sem):
    rows, lon = tangent.shape[0], tangent.shape[1]
    cells = rows * lon
    wind_copy = pltpu.make_async_copy(wind, wind_b, sem.at[rows])
    wind_copy.start()
    copies = []
    for j in range(rows):
        at = jnp.where(flip[0] == 1, rows - 1 - j, j)
        copies.append(pltpu.make_async_copy(tangent.at[at], buf.at[j], sem.at[j]))
        copies[-1].start()
    wind_copy.wait()
    for step in range(wind_b.shape[0]):
        for j in range(rows):
            code = jnp.where(flip[0] == 1, wind_b[step, rows - 1 - j : rows - j, :], wind_b[step, j : j + 1, :])
            codes[step * rows + j : step * rows + j + 1, :] = code.astype(F32) + 1.0
    mask = cells_pulled(wind_fields(codes[...], sign_of(flip), rows), rows)
    where, _ = slot_of(mask)
    slots[...] = where
    head = codes.shape[0]
    capacity = sent.shape[0] - head
    tall = jnp.concatenate([mask, jnp.zeros((head - mask.shape[0], lon), F32)], axis=0)
    notes = jnp.concatenate([codes[...], tall, jnp.zeros((head, own.shape[1] - 2 * lon), F32)], axis=1)
    notes = notes.astype(BF16)
    own[cells:, :] = notes
    sent[capacity:, :] = notes
    choose = choose_matrix(where, capacity, rows)
    for j in range(rows):
        copies[j].wait()
        own[j * lon : (j + 1) * lon, :] = buf[j].astype(BF16)
    sent[0:capacity, :] = dot(choose, own[0:cells, :]).astype(BF16)


def reach_kernel(flip, after, codes, pulled_slots, slots, over):
    rows = 4
    where, total = slot_of(cells_reached(wind_fields(codes[...], sign_of(flip), rows), rows))
    slots[...] = where
    pulled = jnp.max(pulled_slots[...], axis=(0, 1), keepdims=True) + 1.0
    line = lax.broadcasted_iota(jnp.int32, over.shape, 1)
    first = jnp.where(pulled > float(FAR_CELLS), 1.0, 0.0)
    second = jnp.where(total > float(FAR_COLUMNS), 1.0, 0.0)
    over[...] = jnp.where(line == 0, first, jnp.where(line == 1, second, 0.0))


def rest_kernel(first, slots, dense, out):
    rows = dense.shape[0] // slots.shape[1]
    cells = rows * slots.shape[1]
    choose = choose_matrix(slots[...], out.shape[0], rows, first)
    out[...] = dot(choose, dense[0:cells, :]).astype(BF16)


def blank_kernel(out):
    pass


def near_steps(mats, start_b, start_f, c_ref, outs, mid_b, mid_f, lon):
    c = c_ref[0:1, :]
    blocks = ((5, 7, 9), (6, 8), (7,))
    read_b, read_f, first = start_b, start_f, 4
    k = 0
    for step, exts in enumerate(blocks):
        for ext in exts:
            at = (ext - 1 - first) * lon
            pulled = dot(mats[k], read_b(at, 4 * lon))
            value = (1.0 - c) * read_f(at + lon, 2 * lon) + c * pulled
            k += 1
            if ext == exts[0]:
                outs[step][...] = value
            if step < 2:
                to = (ext - exts[0]) * lon
                mid_f[step, to : to + 2 * lon, :] = value
                mid_b[step, to : to + 2 * lon, :] = value.astype(BF16)
        first = exts[0]
        read_b = functools.partial(lambda s, a, n: mid_b[s, a : a + n, :], step)
        read_f = functools.partial(lambda s, a, n: mid_f[s, a : a + n, :], step)


def far_steps(mats, start_b, start_f, c_ref, kept, mid_b, mid_f, lon, finish):
    c = c_ref[0:1, :]
    k = 0
    for step in range(4):
        now, last = step % 2, (step + 1) % 2
        for half in range(2):
            at = 2 * half * lon
            if step == 0:
                window, own = start_b(at, 4 * lon), start_f(at + lon, 2 * lon)
            else:
                window = mid_b[last, at : at + 4 * lon, :]
                own = mid_f[last, at + lon : at + 3 * lon, :]
            value = (1.0 - c) * own + c * dot(mats[k], window)
            k += 1
            if step < 3:
                mid_f[now, at : at + 2 * lon, :] = value
                mid_b[now, at : at + 2 * lon, :] = value.astype(BF16)
            else:
                finish(half, value)
        if step < 3:
            carried = kept[step][...]
            mid_f[now, 4 * lon :, :] = carried
            mid_b[now, 4 * lon :, :] = carried.astype(BF16)


def near_kernel(
    flip, rest, tangent, codes, near, courant, background, w_first, w_second, where_col, where_row, slots,
    slope_one, slope_two, kept_a, kept_b, kept_c, pick, place, place_far, near_codes,
    table, mats, cells_b, mid_b, mid_f, hidden,
):
    rows, lon = tangent.shape[0], tangent.shape[1]
    cells = rows * lon
    sign = sign_of(flip)
    table[...] = jnp.zeros_like(table)
    near_codes[...] = near[cells:, 0:lon].astype(F32)
    store_sources(table, 1, codes[...], False, sign, lon, rows)
    store_sources(table, 2, near_codes[...], True, sign, lon, rows)
    turned = table[...].T
    k = 0
    for step, exts in enumerate(((5, 7, 9), (6, 8), (7,))):
        for ext in exts:
            pull_matrix(mats.at[k], turned, step, ext, lon, rows)
            k += 1
    for j in range(rows):
        row = tangent[jnp.where(flip[0] == 1, rows - 1 - j, j)]
        cells_b[j * lon : (j + 1) * lon, :] = row.astype(BF16)
        cells_b[(rows + j) * lon : (rows + j + 1) * lon, :] = near[(rows - 1 - j) * lon : (rows - j) * lon, :]

    def start_f(at, size):
        pieces = []
        for row in range(at // lon, (at + size) // lon):
            if row < rows:
                pieces.append(tangent[jnp.where(flip[0] == 1, rows - 1 - row, row)])
            else:
                pieces.append(cells_b[row * lon : (row + 1) * lon, :].astype(F32))
        return jnp.concatenate(pieces, axis=0)

    near_steps(
        mats, lambda at, size: cells_b[at : at + size, :], start_f, courant,
        (kept_a, kept_b, kept_c), mid_b, mid_f, lon,
    )

    first_tanh = jnp.tanh(dot(background[...], w_first[...]))
    hidden[...] = first_tanh.astype(BF16)
    slope_one[...] = 1.0 - first_tanh * first_tanh
    second_tanh = jnp.tanh(dot(hidden[...], w_second[...]))
    slope_two[...] = 1.0 - second_tanh * second_tanh

    count = where_col.shape[0]
    pick[...] = jnp.where(
        where_col[...] == lax.broadcasted_iota(jnp.int32, (count, cells), 1), 1.0, 0.0
    ).astype(BF16)
    place[...] = jnp.where(
        where_row[...] == lax.broadcasted_iota(jnp.int32, (cells, count), 0), 1.0, 0.0
    ).astype(BF16)
    place_far[...] = dot(choose_matrix(slots[...], place_far.shape[0], rows), place[...]).astype(BF16)


def observe_kernel(
    flip, flag, tangent, codes, far, rest, courant, slope_one, slope_two, kept_a, kept_b, kept_c,
    w_first, w_second, w_third, pick, place, place_far, quality, chan_weight,
    out, sent, far_codes,
    table, mats, cells_b, mid_b, mid_f, last_b, one_b, two_b, rest_b, sem,
):
    rows, lon = tangent.shape[0], tangent.shape[1]
    cells = rows * lon
    sign = sign_of(flip)
    capacity = far.shape[0] - codes.shape[0]
    table[...] = jnp.zeros_like(table)
    far_codes[...] = far[capacity:, 0:lon].astype(F32)
    store_sources(table, 0, far_codes[...], True, sign, lon, rows)
    store_sources(table, 1, codes[...], False, sign, lon, rows)
    turned = table[...].T
    for step in range(4):
        for half in range(2):
            pull_matrix(mats.at[2 * step + half], turned, step, step + 1 + 2 * half, lon, rows)
    where, _ = slot_of(far[capacity:, lon : 2 * lon].astype(F32)[0:8])
    where = turn(where)
    for j in range(rows):
        value = dot(spread_matrix(where, j, capacity), far[0:capacity, :])
        cells_b[(rows - 1 - j) * lon : (rows - j) * lon, :] = value.astype(BF16)
    for j in range(2):
        row = tangent[jnp.where(flip[0] == 1, rows - 1 - j, j)]
        cells_b[(rows + j) * lon : (rows + j + 1) * lon, :] = row.astype(BF16)

    @pl.when(flag[0] > 0)
    def _():
        copy = pltpu.make_async_copy(rest, rest_b, sem.at[0])
        copy.start()
        copy.wait()
        for j in range(rows):
            value = dot(spread_matrix(where, j, rest_b.shape[0], capacity), rest_b[...])
            at = slice((rows - 1 - j) * lon, (rows - j) * lon)
            cells_b[at, :] = (cells_b[at, :].astype(F32) + value).astype(BF16)

    def start_f(at, size):
        pieces = []
        for row in range(at // lon, (at + size) // lon):
            if row == rows:
                pieces.append(tangent[jnp.where(flip[0] == 1, rows - 1, 0)])
            else:
                pieces.append(cells_b[row * lon : (row + 1) * lon, :].astype(F32))
        return jnp.concatenate(pieces, axis=0)

    def finish(half, value):
        last_b[2 * half * lon : 2 * (half + 1) * lon, :] = value.astype(BF16)

    far_steps(
        mats, lambda at, size: cells_b[at : at + size, :], start_f, courant,
        (kept_a, kept_b, kept_c), mid_b, mid_f, lon, finish,
    )
    one_b[...] = dot(pick[...], last_b[...]).astype(BF16)
    two_b[...] = (slope_one[...] * dot(one_b[...], w_first[...])).astype(BF16)
    one_b[...] = (slope_two[...] * dot(two_b[...], w_second[...])).astype(BF16)
    scale = quality[...] * chan_weight[0:1, :]
    two_b[...] = (scale * dot(one_b[...], w_third[...])).astype(BF16)
    one_b[...] = (slope_two[...] * dot_t(two_b[...], w_third[...])).astype(BF16)
    two_b[...] = (slope_one[...] * dot_t(one_b[...], w_second[...])).astype(BF16)
    one_b[...] = dot_t(two_b[...], w_first[...]).astype(BF16)
    sent[...] = dot(place_far[...], one_b[...]).astype(BF16)
    out[...] = dot(place[...], one_b[...]).astype(BF16)


def near_adjoint_kernel(
    flip, rest, cells_own, cells_near, codes, near_codes, far_codes, courant,
    kept_a, kept_b, kept_c, far_mats, spread, far_slots,
    table, mats, cells_b, mid_b, mid_f,
):
    rows, lon = 4, table.shape[1]
    cells = rows * lon
    sign = sign_of(flip)
    store_sources(table, 0, far_codes[...], True, sign, lon, rows)
    store_sources(table, 1, codes[...], False, sign, lon, rows)
    store_sources(table, 2, near_codes[...], True, sign, lon, rows)
    k = 0
    for order, exts in enumerate(((5, 7, 9), (6, 8), (7,))):
        for ext in exts:
            push_matrix(mats.at[k], table, 3 - order, ext, lon, rows)
            k += 1
    cells_b[0:cells, :] = cells_own[...]
    for j in range(rows):
        cells_b[(rows + j) * lon : (rows + j + 1) * lon, :] = cells_near[
            (rows - 1 - j) * lon : (rows - j) * lon, :
        ]
    near_steps(
        mats, lambda at, size: cells_b[at : at + size, :],
        lambda at, size: cells_b[at : at + size, :].astype(F32), courant,
        (kept_a, kept_b, kept_c), mid_b, mid_f, lon,
    )
    for order in range(4):
        for half in range(2):
            push_matrix(far_mats.at[2 * order + half], table, 3 - order, order + 1 + 2 * half, lon, rows)
    where, _ = slot_of(cells_reached(wind_fields(far_codes[...], -sign, rows), rows))
    far_slots[...] = where
    where = turn(where)
    capacity = spread.shape[1]
    for j in range(rows):
        spread[j * lon : (j + 1) * lon, :] = spread_matrix(where, j, capacity)


def far_adjoint_kernel(
    flip, flag, cells_own, far, rest, courant, kept_a, kept_b, kept_c, mats, spread, far_slots,
    out,
    cells_b, mid_b, mid_f, result, rest_b, sem,
):
    rows, lon = out.shape[0], out.shape[1]
    cells = rows * lon
    for j in range(rows):
        value = dot(spread[j * lon : (j + 1) * lon, :], far[...])
        cells_b[(rows - 1 - j) * lon : (rows - j) * lon, :] = value.astype(BF16)
    cells_b[cells:, :] = cells_own[0 : 2 * lon, :]

    @pl.when(flag[0] > 0)
    def _():
        copy = pltpu.make_async_copy(rest, rest_b, sem.at[rows])
        copy.start()
        copy.wait()
        where = turn(far_slots[...])
        for j in range(rows):
            value = dot(spread_matrix(where, j, rest_b.shape[0], spread.shape[1]), rest_b[...])
            at = slice((rows - 1 - j) * lon, (rows - j) * lon)
            cells_b[at, :] = (cells_b[at, :].astype(F32) + value).astype(BF16)

    copies = []

    def finish(half, value):
        for part in range(2):
            j = 2 * half + part
            result[j] = value[part * lon : (part + 1) * lon, :]
            at = jnp.where(flip[0] == 1, rows - 1 - j, j)
            copies.append(pltpu.make_async_copy(result.at[j], out.at[at], sem.at[j]))
            copies[-1].start()

    far_steps(
        mats, lambda at, size: cells_b[at : at + size, :],
        lambda at, size: cells_b[at : at + size, :].astype(F32), courant,
        (kept_a, kept_b, kept_c), mid_b, mid_f, lon, finish,
    )
    for copy in copies:
        copy.wait()


def params():
    return pltpu.CompilerParams(vmem_limit_bytes=VMEM_LIMIT)


def shape(dims, dtype):
    return jax.ShapeDtypeStruct(dims, dtype)


def second_exchange(flag, first, slots, dense, size, links):
    out = shape((size, dense.shape[1]), BF16)

    def send():
        rest = pl.pallas_call(
            functools.partial(rest_kernel, first),
            out_shape=out,
            in_specs=[VMEM, VMEM],
            out_specs=VMEM,
            name="rest",
        )(slots, dense)
        return lax.ppermute(rest, "lat", links)

    def skip():
        return pl.pallas_call(blank_kernel, out_shape=out, out_specs=ANY, name="blank")()

    return lax.cond(flag, send, skip)


def local(
    tangent,
    wind_code,
    courant,
    obs_index,
    obs_count,
    obs_quality,
    background,
    w_first,
    w_second,
    w_third,
    chan_weight,
):
    rows, lon, levels = tangent.shape
    cells = rows * lon
    head = wind_code.shape[0] * rows
    listed = obs_index.shape[1]
    hidden_size = w_first.shape[1]
    count = lax.axis_size("lat")
    here = lax.axis_index("lat")
    odd = (here % 2).astype(jnp.int32)
    flip = odd.reshape(1)
    linked = (here > 0) & (here < count - 1)
    pairs = [(i, i ^ 1) for i in range(count)]
    links = [(i, i + 1) for i in range(1, count - 1, 2)]
    links = links + [(b, a) for a, b in links]

    own, sent, codes, slots = pl.pallas_call(
        pack_kernel,
        out_shape=[
            shape((cells + head, levels), BF16),
            shape((FAR_CELLS + head, levels), BF16),
            shape((head, lon), F32),
            shape((8, lon), F32),
        ],
        in_specs=[SMEM, HBM, HBM],
        out_specs=[VMEM] * 4,
        scratch_shapes=[
            pltpu.VMEM((rows, lon, levels), F32),
            pltpu.VMEM(wind_code.shape, jnp.int32),
            pltpu.SemaphoreType.DMA((rows + 1,)),
        ],
        compiler_params=pltpu.CompilerParams(vmem_limit_bytes=PACK_LIMIT),
        name="pack",
    )(flip, tangent, wind_code)

    far = lax.ppermute(sent, "lat", links)
    near = lax.ppermute(own, "lat", pairs)

    own_slots, over = pl.pallas_call(
        reach_kernel,
        out_shape=[shape((8, lon), F32)] * 2,
        in_specs=[SMEM, ANY, VMEM, VMEM],
        out_specs=[VMEM] * 2,
        name="reach",
    )(flip, near, codes, slots)
    over = jnp.maximum(over, lax.ppermute(over, "lat", links))
    first_over = linked & (over[0, 0] > 0.0)
    second_over = linked & (over[0, 1] > 0.0)
    rest = second_exchange(first_over, FAR_CELLS, slots, own, cells - FAR_CELLS, links)

    c_row = courant.reshape(1, levels)
    slot_ids = jnp.arange(listed, dtype=jnp.int32)
    observed = slot_ids < obs_count[0]
    where_at = obs_index[0]
    where_at = jnp.where(odd == 1, where_at + (rows - 1 - 2 * (where_at // lon)) * lon, where_at)
    where_at = jnp.where(observed, where_at, -1)
    quality = jnp.where(observed, obs_quality[0].astype(F32), 0.0)

    kept_shape = [shape((2 * lon, levels), F32)] * 3
    slope_shape = shape((listed, hidden_size), F32)
    slope_one, slope_two, kept_a, kept_b, kept_c, pick, place, place_far, near_codes = pl.pallas_call(
        near_kernel,
        out_shape=[slope_shape, slope_shape]
        + kept_shape
        + [
            shape((listed, cells), BF16),
            shape((cells, listed), BF16),
            shape((FAR_COLUMNS, listed), BF16),
            shape((head, lon), F32),
        ],
        in_specs=[SMEM, ANY] + [VMEM] * 10,
        out_specs=[VMEM] * 9,
        scratch_shapes=[
            pltpu.VMEM((lon, lon), F32),
            pltpu.VMEM((6, 2 * lon, 4 * lon), BF16),
            pltpu.VMEM((2 * cells, levels), BF16),
            pltpu.VMEM((2, 6 * lon, levels), BF16),
            pltpu.VMEM((2, 6 * lon, levels), F32),
            pltpu.VMEM((listed, hidden_size), BF16),
        ],
        compiler_params=params(),
        cost_estimate=pl.CostEstimate(flops=4_000_000_000, bytes_accessed=16_000_000, transcendentals=1_000_000),
        name="near",
    )(
        flip, rest, tangent, codes, near, c_row, background[0], w_first, w_second,
        where_at.reshape(listed, 1), where_at.reshape(1, listed), own_slots,
    )

    cells_own, sent, far_codes = pl.pallas_call(
        observe_kernel,
        out_shape=[
            shape((cells, levels), BF16),
            shape((FAR_COLUMNS, levels), BF16),
            shape((head, lon), F32),
        ],
        in_specs=[SMEM, SMEM, VMEM, VMEM, VMEM, ANY] + [VMEM] * 14,
        out_specs=[VMEM] * 3,
        scratch_shapes=[
            pltpu.VMEM((lon, lon), F32),
            pltpu.VMEM((8, 2 * lon, 4 * lon), BF16),
            pltpu.VMEM((6 * lon, levels), BF16),
            pltpu.VMEM((2, 6 * lon, levels), BF16),
            pltpu.VMEM((2, 6 * lon, levels), F32),
            pltpu.VMEM((cells, levels), BF16),
            pltpu.VMEM((listed, levels), BF16),
            pltpu.VMEM((listed, levels), BF16),
            pltpu.VMEM((cells - FAR_CELLS, levels), BF16),
            pltpu.SemaphoreType.DMA((1,)),
        ],
        compiler_params=params(),
        name="observe",
    )(
        flip, first_over.astype(jnp.int32).reshape(1), tangent, codes, far, rest, c_row,
        slope_one, slope_two, kept_a, kept_b, kept_c, w_first, w_second, w_third,
        pick, place, place_far, quality.reshape(listed, 1), chan_weight.reshape(1, -1),
    )

    columns_far = lax.ppermute(sent, "lat", links)
    cells_near = lax.ppermute(cells_own, "lat", pairs)

    rest = second_exchange(second_over, FAR_COLUMNS, own_slots, cells_own, cells - FAR_COLUMNS, links)
    kept_a, kept_b, kept_c, mats, spread, far_slots = pl.pallas_call(
        near_adjoint_kernel,
        out_shape=kept_shape
        + [
            shape((8, 2 * lon, 4 * lon), BF16),
            shape((cells, FAR_COLUMNS), BF16),
            shape((8, lon), F32),
        ],
        in_specs=[SMEM, ANY] + [VMEM] * 6,
        out_specs=[VMEM] * 6,
        scratch_shapes=[
            pltpu.VMEM((lon, lon), F32),
            pltpu.VMEM((6, 2 * lon, 4 * lon), BF16),
            pltpu.VMEM((2 * cells, levels), BF16),
            pltpu.VMEM((2, 6 * lon, levels), BF16),
            pltpu.VMEM((2, 6 * lon, levels), F32),
        ],
        compiler_params=params(),
        cost_estimate=pl.CostEstimate(flops=2_000_000_000, bytes_accessed=8_000_000, transcendentals=0),
        name="near_adjoint",
    )(flip, rest, cells_own, cells_near, codes, near_codes, far_codes, c_row)

    return pl.pallas_call(
        far_adjoint_kernel,
        out_shape=shape((rows, lon, levels), F32),
        in_specs=[SMEM, SMEM, VMEM, VMEM, ANY] + [VMEM] * 7,
        out_specs=HBM,
        scratch_shapes=[
            pltpu.VMEM((6 * lon, levels), BF16),
            pltpu.VMEM((2, 6 * lon, levels), BF16),
            pltpu.VMEM((2, 6 * lon, levels), F32),
            pltpu.VMEM((rows, lon, levels), F32),
            pltpu.VMEM((cells - FAR_COLUMNS, levels), BF16),
            pltpu.SemaphoreType.DMA((rows + 1,)),
        ],
        compiler_params=params(),
        name="far_adjoint",
    )(
        flip, second_over.astype(jnp.int32).reshape(1), cells_own, columns_far, rest, c_row,
        kept_a, kept_b, kept_c, mats, spread, far_slots,
    )


def solution(mesh):
    placed = (
        P(("groups", "lat"), None, None),
        P(None, ("groups", "lat"), None),
        P(),
        P(("groups", "lat"), None),
        P(("groups", "lat")),
        P(("groups", "lat"), None),
        P(("groups", "lat"), None, None),
        P(),
        P(),
        P(),
        P(),
    )
    return jax.shard_map(
        local,
        mesh=mesh,
        in_specs=placed,
        out_specs=P(("groups", "lat"), None, None),
        check_vma=False,
    )
```

```python
import functools

import jax
import jax.numpy as jnp
from jax import lax
from jax.experimental import pallas as pl
from jax.experimental.pallas import tpu as pltpu
from jax.sharding import PartitionSpec as P

F32 = jnp.float32
BF16 = jnp.bfloat16
FAR_CELLS = 304
FAR_COLUMNS = 272
ANY = pl.BlockSpec(memory_space=pl.ANY)
VMEM = pl.BlockSpec(memory_space=pltpu.VMEM)
HBM = pl.BlockSpec(memory_space=pltpu.HBM)
SMEM = pl.BlockSpec(memory_space=pltpu.SMEM)
VMEM_LIMIT = 28 * 1024 * 1024
PACK_LIMIT = 60 * 1024 * 1024


def dot_t(left, right):
    return lax.dot_general(left, right, (((1,), (1,)), ((), ())), preferred_element_type=F32)


def dot(left, right):
    return jnp.dot(left, right, preferred_element_type=F32)


def store_sources(table, slot, codes, mirrored, sign, lon, rows):
    code = codes.astype(F32) - 1.0
    lat_q = jnp.where(code >= 5.0, 1.0, 0.0) + jnp.where(code >= 10.0, 1.0, 0.0)
    lon_step = code - 5.0 * lat_q - 2.0
    col = lax.broadcasted_iota(jnp.int32, code.shape, 1).astype(F32) - lon_step
    col = jnp.where(col < 0.0, col + lon, jnp.where(col >= lon, col - lon, col))
    stored = lax.broadcasted_iota(jnp.int32, code.shape, 0) & (rows - 1)
    row = (rows - 1 - stored) if mirrored else stored
    row = (row + slot * rows).astype(F32)
    src = (row - sign * (lat_q - 1.0)) * lon + col
    table[slot * code.shape[0] : (slot + 1) * code.shape[0], :] = jnp.where(code < 0.0, -65536.0, src)


def table_row(step, ext, rows):
    slot, at = ext // rows, ext % rows
    return slot * rows * rows + step * rows + (at if slot == 1 else rows - 1 - at)


def pull_matrix(out, turned, step, ext, lon, rows):
    span = 4 * lon
    lanes = lax.broadcasted_iota(jnp.int32, (lon, span), 1).astype(F32) + float((ext - 1) * lon)
    for half in range(2):
        k = table_row(step, ext + half, rows)
        column = turned[:, k : k + 1]
        out[half * lon : (half + 1) * lon, :] = jnp.where(column == lanes, 1.0, 0.0).astype(BF16)


def push_matrix(out, table, step, ext, lon, rows):
    dest = lax.broadcasted_iota(jnp.int32, (2 * lon, lon), 0).astype(F32) + float(ext * lon)
    for part in range(4):
        k = table_row(step, ext - 1 + part, rows)
        line = table[k : k + 1, :]
        out[:, part * lon : (part + 1) * lon] = jnp.where(line == dest, 1.0, 0.0).astype(BF16)


def wind_fields(codes, sign, rows):
    code = codes.astype(F32) - 1.0
    lat_q = jnp.where(code >= 5.0, 1.0, 0.0) + jnp.where(code >= 10.0, 1.0, 0.0)
    lat = jnp.where(code < 0.0, 9.0, sign * (lat_q - 1.0))
    lon = code - 5.0 * lat_q - 2.0
    fill = jnp.full((8 - rows, code.shape[1]), 9.0, F32)
    fields = []
    for step in range(code.shape[0] // rows):
        at = slice(step * rows, (step + 1) * rows)
        fields.append((jnp.concatenate([lat[at], fill], axis=0), jnp.concatenate([lon[at], fill], axis=0)))
    return fields


def shift_rows(mask, by):
    blank = jnp.zeros((1, mask.shape[1]), F32)
    if by == 1:
        return jnp.concatenate([blank, mask[:-1]], axis=0)
    if by == -1:
        return jnp.concatenate([mask[1:], blank], axis=0)
    return mask


def cells_pulled(fields, rows):
    lon = fields[0][0].shape[1]
    row = lax.broadcasted_iota(jnp.int32, (8, lon), 0)
    mask = jnp.where(row == 0, 1.0, 0.0)
    for lat, east in reversed(fields[: len(fields) - 1]):
        new = mask
        for a in (-1, 0, 1):
            total = jnp.zeros_like(mask)
            for b in range(-2, 3):
                hit = jnp.where((lat == float(a)) & (east == float(b)), mask, 0.0)
                total = jnp.maximum(total, hit if b == 0 else pltpu.roll(hit, (-b) % lon, 1))
            new = jnp.maximum(new, shift_rows(total, -a))
        mask = jnp.where(row < rows, new, 0.0)
    return mask


def cells_reached(fields, rows):
    lon = fields[0][0].shape[1]
    row = lax.broadcasted_iota(jnp.int32, (8, lon), 0)
    mask = jnp.zeros((8, lon), F32)
    for lat, east in fields:
        new = mask
        for a in (-1, 0, 1):
            source = shift_rows(mask, a)
            if a == 1:
                source = jnp.where(row == 0, 1.0, source)
            for b in range(-2, 3):
                seen = source if b == 0 else pltpu.roll(source, b % lon, 1)
                new = jnp.maximum(new, jnp.where((lat == float(a)) & (east == float(b)), seen, 0.0))
        mask = jnp.where(row < rows, new, 0.0)
    return mask


def slot_of(mask):
    lon = mask.shape[1]
    before = lax.broadcasted_iota(jnp.int32, (lon, lon), 0) < lax.broadcasted_iota(jnp.int32, (lon, lon), 1)
    place = dot(mask.astype(BF16), jnp.where(before, 1.0, 0.0).astype(BF16))
    totals = jnp.sum(mask, axis=1, keepdims=True)
    ahead = jnp.zeros((1, 1), F32)
    lines = []
    for j in range(mask.shape[0]):
        lines.append(place[j : j + 1] + ahead)
        ahead = ahead + totals[j : j + 1]
    return jnp.where(mask > 0.0, jnp.concatenate(lines, axis=0), -1.0), ahead


def choose_matrix(slots, size, rows, first=0):
    lon = slots.shape[1]
    at = lax.broadcasted_iota(jnp.int32, (size, lon), 0).astype(F32) + float(first)
    parts = [jnp.where(slots[j : j + 1] == at, 1.0, 0.0) for j in range(rows)]
    return jnp.concatenate(parts, axis=1).astype(BF16)


def spread_matrix(turned, row, size, first=0):
    at = lax.broadcasted_iota(jnp.int32, (turned.shape[0], size), 1).astype(F32) + float(first)
    return jnp.where(turned[:, row : row + 1] == at, 1.0, 0.0).astype(BF16)


def turn(slots):
    lon = slots.shape[1]
    return jnp.concatenate([slots, jnp.full((lon - slots.shape[0], lon), -1.0, F32)], axis=0).T


def sign_of(flip):
    return jnp.where(flip[0] == 1, -1.0, 1.0)


def pack_kernel(flip, tangent, wind, own, sent, codes, slots, buf, wind_b, sem):
    rows, lon = tangent.shape[0], tangent.shape[1]
    cells = rows * lon
    wind_copy = pltpu.make_async_copy(wind, wind_b, sem.at[rows])
    wind_copy.start()
    copies = []
    for j in range(rows):
        at = jnp.where(flip[0] == 1, rows - 1 - j, j)
        copies.append(pltpu.make_async_copy(tangent.at[at], buf.at[j], sem.at[j]))
        copies[-1].start()
    wind_copy.wait()
    for step in range(wind_b.shape[0]):
        for j in range(rows):
            code = jnp.where(flip[0] == 1, wind_b[step, rows - 1 - j : rows - j, :], wind_b[step, j : j + 1, :])
            codes[step * rows + j : step * rows + j + 1, :] = code.astype(F32) + 1.0
    mask = cells_pulled(wind_fields(codes[...], sign_of(flip), rows), rows)
    where, total = slot_of(mask)
    slots[...] = where
    head = codes.shape[0]
    capacity = sent.shape[0] - head
    tall = jnp.concatenate([mask, jnp.zeros((head - mask.shape[0], lon), F32)], axis=0)
    flag = jnp.broadcast_to(jnp.where(total > float(capacity), 1.0, 0.0), (head, lon))
    notes = jnp.concatenate([codes[...], tall, flag, jnp.zeros((head, own.shape[1] - 3 * lon), F32)], axis=1)
    notes = notes.astype(BF16)
    own[cells:, :] = notes
    sent[capacity:, :] = notes
    choose = choose_matrix(where, capacity, rows)
    for j in range(rows):
        copies[j].wait()
        own[j * lon : (j + 1) * lon, :] = buf[j].astype(BF16)
    sent[0:capacity, :] = dot(choose, own[0:cells, :]).astype(BF16)


def reach_kernel(flip, linked, own_slots, far_codes, far_slots, over):
    where, total = slot_of(cells_reached(wind_fields(far_codes[...], -sign_of(flip), 4), 4))
    far_slots[...] = where
    most = jnp.maximum(total, jnp.max(own_slots[...], axis=(0, 1), keepdims=True) + 1.0)
    over[0] = jnp.where(jnp.max(most) > float(FAR_COLUMNS), linked[0], 0)


def choose_kernel(flag, _one, _two, redone_one, redone_two, one, two, sem):
    @pl.when(flag[0] > 0)
    def _():
        copies = [
            pltpu.make_async_copy(redone_one, one, sem.at[0]),
            pltpu.make_async_copy(redone_two, two, sem.at[1]),
        ]
        for copy in copies:
            copy.start()
        for copy in copies:
            copy.wait()


def rest_kernel(first, slots, dense, out):
    rows = dense.shape[0] // slots.shape[1]
    cells = rows * slots.shape[1]
    choose = choose_matrix(slots[...], out.shape[0], rows, first)
    out[...] = dot(choose, dense[0:cells, :]).astype(BF16)


def blank_kernel(*outs):
    pass


def near_steps(mats, start_b, start_f, c_ref, outs, mid_b, mid_f, lon):
    c = c_ref[0:1, :]
    blocks = ((5, 7, 9), (6, 8), (7,))
    read_b, read_f, first = start_b, start_f, 4
    k = 0
    for step, exts in enumerate(blocks):
        for ext in exts:
            at = (ext - 1 - first) * lon
            pulled = dot(mats[k], read_b(at, 4 * lon))
            value = (1.0 - c) * read_f(at + lon, 2 * lon) + c * pulled
            k += 1
            if ext == exts[0]:
                outs[step][...] = value
            if step < 2:
                to = (ext - exts[0]) * lon
                mid_f[step, to : to + 2 * lon, :] = value
                mid_b[step, to : to + 2 * lon, :] = value.astype(BF16)
        first = exts[0]
        read_b = functools.partial(lambda s, a, n: mid_b[s, a : a + n, :], step)
        read_f = functools.partial(lambda s, a, n: mid_f[s, a : a + n, :], step)


def far_steps(mats, start_b, start_f, c_ref, kept, mid_b, mid_f, lon, finish):
    c = c_ref[0:1, :]
    k = 0
    for step in range(4):
        now, last = step % 2, (step + 1) % 2
        for half in range(2):
            at = 2 * half * lon
            if step == 0:
                window, own = start_b(at, 4 * lon), start_f(at + lon, 2 * lon)
            else:
                window = mid_b[last, at : at + 4 * lon, :]
                own = mid_f[last, at + lon : at + 3 * lon, :]
            value = (1.0 - c) * own + c * dot(mats[k], window)
            k += 1
            if step < 3:
                mid_f[now, at : at + 2 * lon, :] = value
                mid_b[now, at : at + 2 * lon, :] = value.astype(BF16)
            else:
                finish(half, value)
        if step < 3:
            carried = kept[step][...]
            mid_f[now, 4 * lon :, :] = carried
            mid_b[now, 4 * lon :, :] = carried.astype(BF16)


def near_kernel(
    flip, obs_count, tangent, codes, near, courant, background, w_first, w_second, obs_index, obs_quality,
    slope_one, slope_two, kept_a, kept_b, kept_c, pick, place, place_far, near_codes, quality, slots,
    table, mats, cells_b, mid_b, mid_f, hidden,
):
    rows, lon = tangent.shape[0], tangent.shape[1]
    cells = rows * lon
    sign = sign_of(flip)
    table[...] = jnp.zeros_like(table)
    near_codes[...] = near[cells:, 0:lon].astype(F32)
    store_sources(table, 1, codes[...], False, sign, lon, rows)
    store_sources(table, 2, near_codes[...], True, sign, lon, rows)
    turned = table[...].T
    k = 0
    for step, exts in enumerate(((5, 7, 9), (6, 8), (7,))):
        for ext in exts:
            pull_matrix(mats.at[k], turned, step, ext, lon, rows)
            k += 1
    for j in range(rows):
        row = tangent[jnp.where(flip[0] == 1, rows - 1 - j, j)]
        cells_b[j * lon : (j + 1) * lon, :] = row.astype(BF16)
        cells_b[(rows + j) * lon : (rows + j + 1) * lon, :] = near[(rows - 1 - j) * lon : (rows - j) * lon, :]

    def start_f(at, size):
        pieces = []
        for row in range(at // lon, (at + size) // lon):
            if row < rows:
                pieces.append(tangent[jnp.where(flip[0] == 1, rows - 1 - row, row)])
            else:
                pieces.append(cells_b[row * lon : (row + 1) * lon, :].astype(F32))
        return jnp.concatenate(pieces, axis=0)

    near_steps(
        mats, lambda at, size: cells_b[at : at + size, :], start_f, courant,
        (kept_a, kept_b, kept_c), mid_b, mid_f, lon,
    )

    first_tanh = jnp.tanh(dot(background[...], w_first[...]))
    hidden[...] = first_tanh.astype(BF16)
    slope_one[...] = 1.0 - first_tanh * first_tanh
    second_tanh = jnp.tanh(dot(hidden[...], w_second[...]))
    slope_two[...] = 1.0 - second_tanh * second_tanh

    count = obs_index.shape[1]
    at = obs_index[...]
    at = jnp.where(flip[0] == 1, at + (rows - 1 - 2 * lax.div(at, lon)) * lon, at)
    live = lax.broadcasted_iota(jnp.int32, at.shape, 1) < obs_count[0]
    at = jnp.where(live, at, -1)
    chosen = at == lax.broadcasted_iota(jnp.int32, (cells, count), 0)
    place[...] = jnp.where(chosen, 1.0, 0.0).astype(BF16)
    lines = jnp.concatenate([at.astype(F32), jnp.where(live, obs_quality[...].astype(F32), 0.0)], axis=0)
    lines = jnp.concatenate([lines, jnp.zeros((6, count), F32)], axis=0)
    lines = jnp.concatenate([lines, jnp.zeros((8, cells - count), F32)], axis=1).T
    quality[...] = lines[0:count, 1:2]
    columns = lax.broadcasted_iota(jnp.int32, (count, cells), 1).astype(F32)
    pick[...] = jnp.where(lines[0:count, 0:1] == columns, 1.0, 0.0).astype(BF16)
    where, _ = slot_of(cells_reached(wind_fields(codes[...], sign, rows), rows))
    slots[...] = where
    place_far[...] = dot(choose_matrix(slots[...], place_far.shape[0], rows), place[...]).astype(BF16)


def observe_kernel(
    redo, flip, linked, slots, tangent, codes, far, rest, courant, slope_one, slope_two, kept_a, kept_b, kept_c,
    w_first, w_second, w_third, pick, place, place_far, quality, chan_weight,
    out, sent, far_codes, over,
    table, mats, cells_b, mid_b, mid_f, last_b, one_b, two_b, rest_b, sem,
):
    rows, lon = tangent.shape[0], tangent.shape[1]
    cells = rows * lon
    sign = sign_of(flip)
    capacity = far.shape[0] - codes.shape[0]
    table[...] = jnp.zeros_like(table)
    far_codes[...] = far[capacity:, 0:lon].astype(F32)
    store_sources(table, 0, far_codes[...], True, sign, lon, rows)
    store_sources(table, 1, codes[...], False, sign, lon, rows)
    turned = table[...].T
    for step in range(4):
        for half in range(2):
            pull_matrix(mats.at[2 * step + half], turned, step, step + 1 + 2 * half, lon, rows)
    where, _ = slot_of(far[capacity:, lon : 2 * lon].astype(F32)[0:8])
    where = turn(where)
    most = jnp.maximum(jnp.max(far[capacity:, 2 * lon : 3 * lon].astype(F32)), jnp.where(jnp.max(slots[...]) >= float(capacity), 1.0, 0.0))
    over[0] = jnp.where(most > 0.0, linked[0], 0)
    for j in range(rows):
        value = dot(spread_matrix(where, j, capacity), far[0:capacity, :])
        cells_b[(rows - 1 - j) * lon : (rows - j) * lon, :] = value.astype(BF16)
    for j in range(2):
        row = tangent[jnp.where(flip[0] == 1, rows - 1 - j, j)]
        cells_b[(rows + j) * lon : (rows + j + 1) * lon, :] = row.astype(BF16)

    if redo:
        copy = pltpu.make_async_copy(rest, rest_b, sem.at[0])
        copy.start()
        copy.wait()
        for j in range(rows):
            value = dot(spread_matrix(where, j, rest_b.shape[0], capacity), rest_b[...])
            at = slice((rows - 1 - j) * lon, (rows - j) * lon)
            cells_b[at, :] = (cells_b[at, :].astype(F32) + value).astype(BF16)

    def start_f(at, size):
        pieces = []
        for row in range(at // lon, (at + size) // lon):
            if row == rows:
                pieces.append(tangent[jnp.where(flip[0] == 1, rows - 1, 0)])
            else:
                pieces.append(cells_b[row * lon : (row + 1) * lon, :].astype(F32))
        return jnp.concatenate(pieces, axis=0)

    def finish(half, value):
        last_b[2 * half * lon : 2 * (half + 1) * lon, :] = value.astype(BF16)

    far_steps(
        mats, lambda at, size: cells_b[at : at + size, :], start_f, courant,
        (kept_a, kept_b, kept_c), mid_b, mid_f, lon, finish,
    )
    one_b[...] = dot(pick[...], last_b[...]).astype(BF16)
    two_b[...] = (slope_one[...] * dot(one_b[...], w_first[...])).astype(BF16)
    one_b[...] = (slope_two[...] * dot(two_b[...], w_second[...])).astype(BF16)
    scale = quality[...] * chan_weight[0:1, :]
    two_b[...] = (scale * dot(one_b[...], w_third[...])).astype(BF16)
    one_b[...] = (slope_two[...] * dot_t(two_b[...], w_third[...])).astype(BF16)
    two_b[...] = (slope_one[...] * dot_t(one_b[...], w_second[...])).astype(BF16)
    one_b[...] = dot_t(two_b[...], w_first[...]).astype(BF16)
    sent[...] = dot(place_far[...], one_b[...]).astype(BF16)
    out[...] = dot(place[...], one_b[...]).astype(BF16)


def near_adjoint_kernel(
    flip, rest, cells_own, cells_near, codes, near_codes, far_codes, far_slots, courant,
    kept_a, kept_b, kept_c, far_mats, spread,
    table, mats, cells_b, mid_b, mid_f,
):
    rows, lon = 4, table.shape[1]
    cells = rows * lon
    sign = sign_of(flip)
    store_sources(table, 0, far_codes[...], True, sign, lon, rows)
    store_sources(table, 1, codes[...], False, sign, lon, rows)
    store_sources(table, 2, near_codes[...], True, sign, lon, rows)
    k = 0
    for order, exts in enumerate(((5, 7, 9), (6, 8), (7,))):
        for ext in exts:
            push_matrix(mats.at[k], table, 3 - order, ext, lon, rows)
            k += 1
    cells_b[0:cells, :] = cells_own[...]
    for j in range(rows):
        cells_b[(rows + j) * lon : (rows + j + 1) * lon, :] = cells_near[
            (rows - 1 - j) * lon : (rows - j) * lon, :
        ]
    near_steps(
        mats, lambda at, size: cells_b[at : at + size, :],
        lambda at, size: cells_b[at : at + size, :].astype(F32), courant,
        (kept_a, kept_b, kept_c), mid_b, mid_f, lon,
    )
    for order in range(4):
        for half in range(2):
            push_matrix(far_mats.at[2 * order + half], table, 3 - order, order + 1 + 2 * half, lon, rows)
    where = turn(far_slots[...])
    capacity = spread.shape[1]
    for j in range(rows):
        spread[j * lon : (j + 1) * lon, :] = spread_matrix(where, j, capacity)


def far_adjoint_kernel(
    flip, flag, cells_own, far, rest, courant, kept_a, kept_b, kept_c, mats, spread, far_slots,
    out,
    cells_b, mid_b, mid_f, result, rest_b, sem,
):
    rows, lon = out.shape[0], out.shape[1]
    cells = rows * lon
    for j in range(rows):
        value = dot(spread[j * lon : (j + 1) * lon, :], far[...])
        cells_b[(rows - 1 - j) * lon : (rows - j) * lon, :] = value.astype(BF16)
    cells_b[cells:, :] = cells_own[0 : 2 * lon, :]

    @pl.when(flag[0] > 0)
    def _():
        copy = pltpu.make_async_copy(rest, rest_b, sem.at[rows])
        copy.start()
        copy.wait()
        where = turn(far_slots[...])
        for j in range(rows):
            value = dot(spread_matrix(where, j, rest_b.shape[0], spread.shape[1]), rest_b[...])
            at = slice((rows - 1 - j) * lon, (rows - j) * lon)
            cells_b[at, :] = (cells_b[at, :].astype(F32) + value).astype(BF16)

    copies = []

    def finish(half, value):
        for part in range(2):
            j = 2 * half + part
            result[j] = value[part * lon : (part + 1) * lon, :]
            at = jnp.where(flip[0] == 1, rows - 1 - j, j)
            copies.append(pltpu.make_async_copy(result.at[j], out.at[at], sem.at[j]))
            copies[-1].start()

    far_steps(
        mats, lambda at, size: cells_b[at : at + size, :],
        lambda at, size: cells_b[at : at + size, :].astype(F32), courant,
        (kept_a, kept_b, kept_c), mid_b, mid_f, lon, finish,
    )
    for copy in copies:
        copy.wait()


def params():
    return pltpu.CompilerParams(vmem_limit_bytes=VMEM_LIMIT)


def shape(dims, dtype):
    return jax.ShapeDtypeStruct(dims, dtype)


def send_rest(first, slots, dense, size, links):
    rest = pl.pallas_call(
        functools.partial(rest_kernel, first),
        out_shape=shape((size, dense.shape[1]), BF16),
        in_specs=[VMEM, VMEM],
        out_specs=VMEM,
        name="rest",
    )(slots, dense)
    return lax.ppermute(rest, "lat", links)


def blank(outs):
    return pl.pallas_call(blank_kernel, out_shape=outs, out_specs=[ANY] * len(outs), name="blank")()


def local(
    tangent,
    wind_code,
    courant,
    obs_index,
    obs_count,
    obs_quality,
    background,
    w_first,
    w_second,
    w_third,
    chan_weight,
):
    rows, lon, levels = tangent.shape
    cells = rows * lon
    head = wind_code.shape[0] * rows
    listed = obs_index.shape[1]
    hidden_size = w_first.shape[1]
    count = lax.axis_size("lat")
    here = lax.axis_index("lat")
    odd = (here % 2).astype(jnp.int32)
    flip = odd.reshape(1)
    linked = ((here > 0) & (here < count - 1)).astype(jnp.int32).reshape(1)
    pairs = [(i, i ^ 1) for i in range(count)]
    links = [(i, i + 1) for i in range(1, count - 1, 2)]
    links = links + [(b, a) for a, b in links]

    own, sent, codes, slots = pl.pallas_call(
        pack_kernel,
        out_shape=[
            shape((cells + head, levels), BF16),
            shape((FAR_CELLS + head, levels), BF16),
            shape((head, lon), F32),
            shape((8, lon), F32),
        ],
        in_specs=[SMEM, HBM, HBM],
        out_specs=[VMEM] * 4,
        scratch_shapes=[
            pltpu.VMEM((rows, lon, levels), F32),
            pltpu.VMEM(wind_code.shape, jnp.int32),
            pltpu.SemaphoreType.DMA((rows + 1,)),
        ],
        compiler_params=pltpu.CompilerParams(vmem_limit_bytes=PACK_LIMIT),
        name="pack",
    )(flip, tangent, wind_code)

    far = lax.ppermute(sent, "lat", links)
    near = lax.ppermute(own, "lat", pairs)

    c_row = courant.reshape(1, levels)
    kept_shape = [shape((2 * lon, levels), F32)] * 3
    slope_shape = shape((listed, hidden_size), F32)

    def run_near():
        return pl.pallas_call(
            near_kernel,
            out_shape=[slope_shape, slope_shape]
            + kept_shape
            + [
                shape((listed, cells), BF16),
                shape((cells, listed), BF16),
                shape((FAR_COLUMNS, listed), BF16),
                shape((head, lon), F32),
                shape((listed, 1), F32),
                shape((8, lon), F32),
            ],
            in_specs=[SMEM, SMEM] + [VMEM] * 9,
            out_specs=[VMEM] * 11,
            scratch_shapes=[
                pltpu.VMEM((lon, lon), F32),
                pltpu.VMEM((6, 2 * lon, 4 * lon), BF16),
                pltpu.VMEM((2 * cells, levels), BF16),
                pltpu.VMEM((2, 6 * lon, levels), BF16),
                pltpu.VMEM((2, 6 * lon, levels), F32),
                pltpu.VMEM((listed, hidden_size), BF16),
            ],
            compiler_params=params(),
            cost_estimate=pl.CostEstimate(flops=4_000_000_000, bytes_accessed=16_000_000, transcendentals=1_000_000),
            name="near",
        )(
            flip, obs_count, tangent, codes, near, c_row, background[0], w_first, w_second, obs_index, obs_quality,
        )

    column_shape = [shape((cells, levels), BF16), shape((FAR_COLUMNS, levels), BF16)]

    def run_observe(redo, parts, rest):
        slope_one, slope_two, kept_a, kept_b, kept_c, pick, place, place_far, _, quality, _ = parts
        rest_specs = [ANY] if redo else []
        body = functools.partial(observe_kernel, redo)
        rest_args = [rest] if redo else []
        rest_scratch = [pltpu.VMEM((cells - FAR_CELLS, levels), BF16), pltpu.SemaphoreType.DMA((1,))]

        def kernel(*refs):
            refs = list(refs)
            if not redo:
                refs.insert(6, None)
                refs = refs + [None, None]
            body(*refs)

        return pl.pallas_call(
            kernel,
            out_shape=column_shape + [shape((head, lon), F32), shape((1,), jnp.int32)],
            in_specs=[SMEM, SMEM] + [VMEM] * 4 + rest_specs + [VMEM] * 14,
            out_specs=[VMEM] * 3 + [SMEM],
            scratch_shapes=[
                pltpu.VMEM((lon, lon), F32),
                pltpu.VMEM((8, 2 * lon, 4 * lon), BF16),
                pltpu.VMEM((6 * lon, levels), BF16),
                pltpu.VMEM((2, 6 * lon, levels), BF16),
                pltpu.VMEM((2, 6 * lon, levels), F32),
                pltpu.VMEM((cells, levels), BF16),
                pltpu.VMEM((listed, levels), BF16),
                pltpu.VMEM((listed, levels), BF16),
            ]
            + (rest_scratch if redo else []),
            compiler_params=params(),
            name="observe",
        )(
            flip, linked, slots, tangent, codes, far, *rest_args, c_row,
            slope_one, slope_two, kept_a, kept_b, kept_c, w_first, w_second, w_third,
            pick, place, place_far, quality, chan_weight.reshape(1, -1),
        )

    parts = run_near()
    near_codes, own_slots = parts[8], parts[10]
    cells_own, sent, far_codes, over = run_observe(False, parts, None)

    def observe_again():
        rest = send_rest(FAR_CELLS, slots, own, cells - FAR_CELLS, links)
        return run_observe(True, run_near(), rest)[:2]

    redone = lax.cond(over[0] > 0, observe_again, lambda: blank(column_shape))
    cells_own, sent = pl.pallas_call(
        choose_kernel,
        out_shape=column_shape,
        in_specs=[SMEM] + [ANY] * 4,
        out_specs=[ANY] * 2,
        scratch_shapes=[pltpu.SemaphoreType.DMA((2,))],
        input_output_aliases={1: 0, 2: 1},
        name="choose",
    )(over, cells_own, sent, *redone)

    columns_far = lax.ppermute(sent, "lat", links)
    cells_near = lax.ppermute(cells_own, "lat", pairs)

    far_slots, over = pl.pallas_call(
        reach_kernel,
        out_shape=[shape((8, lon), F32), shape((1,), jnp.int32)],
        in_specs=[SMEM, SMEM, VMEM, VMEM],
        out_specs=[VMEM, SMEM],
        name="reach",
    )(flip, linked, own_slots, far_codes)
    left = cells - FAR_COLUMNS
    rest = lax.cond(
        over[0] > 0,
        lambda: send_rest(FAR_COLUMNS, own_slots, cells_own, left, links),
        lambda: blank([shape((left, levels), BF16)])[0],
    )
    kept_a, kept_b, kept_c, mats, spread = pl.pallas_call(
        near_adjoint_kernel,
        out_shape=kept_shape
        + [
            shape((8, 2 * lon, 4 * lon), BF16),
            shape((cells, FAR_COLUMNS), BF16),
        ],
        in_specs=[SMEM, ANY] + [VMEM] * 7,
        out_specs=[VMEM] * 5,
        scratch_shapes=[
            pltpu.VMEM((lon, lon), F32),
            pltpu.VMEM((6, 2 * lon, 4 * lon), BF16),
            pltpu.VMEM((2 * cells, levels), BF16),
            pltpu.VMEM((2, 6 * lon, levels), BF16),
            pltpu.VMEM((2, 6 * lon, levels), F32),
        ],
        compiler_params=params(),
        cost_estimate=pl.CostEstimate(flops=2_000_000_000, bytes_accessed=8_000_000, transcendentals=0),
        name="near_adjoint",
    )(flip, rest, cells_own, cells_near, codes, near_codes, far_codes, far_slots, c_row)

    return pl.pallas_call(
        far_adjoint_kernel,
        out_shape=shape((rows, lon, levels), F32),
        in_specs=[SMEM, SMEM, VMEM, VMEM, ANY] + [VMEM] * 7,
        out_specs=HBM,
        scratch_shapes=[
            pltpu.VMEM((6 * lon, levels), BF16),
            pltpu.VMEM((2, 6 * lon, levels), BF16),
            pltpu.VMEM((2, 6 * lon, levels), F32),
            pltpu.VMEM((rows, lon, levels), F32),
            pltpu.VMEM((cells - FAR_COLUMNS, levels), BF16),
            pltpu.SemaphoreType.DMA((rows + 1,)),
        ],
        compiler_params=params(),
        name="far_adjoint",
    )(
        flip, over, cells_own, columns_far, rest, c_row,
        kept_a, kept_b, kept_c, mats, spread, far_slots,
    )


def solution(mesh):
    placed = (
        P(("groups", "lat"), None, None),
        P(None, ("groups", "lat"), None),
        P(),
        P(("groups", "lat"), None),
        P(("groups", "lat")),
        P(("groups", "lat"), None),
        P(("groups", "lat"), None, None),
        P(),
        P(),
        P(),
        P(),
    )
    return jax.shard_map(
        local,
        mesh=mesh,
        in_specs=placed,
        out_specs=P(("groups", "lat"), None, None),
        check_vma=False,
    )
```

```python
import functools

import jax
import jax.numpy as jnp
from jax import lax
from jax.experimental import pallas as pl
from jax.experimental.pallas import tpu as pltpu
from jax.sharding import PartitionSpec as P

F32 = jnp.float32
BF16 = jnp.bfloat16
FAR_CELLS = 304
FAR_COLUMNS = 272
ANY = pl.BlockSpec(memory_space=pl.ANY)
VMEM = pl.BlockSpec(memory_space=pltpu.VMEM)
HBM = pl.BlockSpec(memory_space=pltpu.HBM)
SMEM = pl.BlockSpec(memory_space=pltpu.SMEM)
VMEM_LIMIT = 32 * 1024 * 1024
PACK_LIMIT = 60 * 1024 * 1024

OWN_BLOCKS = ((1, 1), (2, 1), (3, 0), (3, 1))
FAR_BLOCKS = ((0, 0), (0, 1), (1, 0), (2, 0))


def dot_t(left, right):
    return lax.dot_general(left, right, (((1,), (1,)), ((), ())), preferred_element_type=F32)


def dot(left, right):
    return jnp.dot(left, right, preferred_element_type=F32)


def store_sources(table, slot, codes, mirrored, sign, lon, rows):
    code = codes.astype(F32) - 1.0
    lat_q = jnp.where(code >= 5.0, 1.0, 0.0) + jnp.where(code >= 10.0, 1.0, 0.0)
    lon_step = code - 5.0 * lat_q - 2.0
    col = lax.broadcasted_iota(jnp.int32, code.shape, 1).astype(F32) - lon_step
    col = jnp.where(col < 0.0, col + lon, jnp.where(col >= lon, col - lon, col))
    stored = lax.broadcasted_iota(jnp.int32, code.shape, 0) & (rows - 1)
    row = (rows - 1 - stored) if mirrored else stored
    row = (row + slot * rows).astype(F32)
    src = (row - sign * (lat_q - 1.0)) * lon + col
    table[slot * code.shape[0] : (slot + 1) * code.shape[0], :] = jnp.where(code < 0.0, -65536.0, src)


def table_row(step, ext, rows):
    slot, at = ext // rows, ext % rows
    return slot * rows * rows + step * rows + (at if slot == 1 else rows - 1 - at)


def pull_matrix(out, turned, step, ext, lon, rows):
    span = 4 * lon
    lanes = lax.broadcasted_iota(jnp.int32, (lon, span), 1).astype(F32) + float((ext - 1) * lon)
    for half in range(2):
        k = table_row(step, ext + half, rows)
        column = turned[:, k : k + 1]
        out[half * lon : (half + 1) * lon, :] = jnp.where(column == lanes, 1.0, 0.0).astype(BF16)


def push_matrix(out, table, step, ext, lon, rows):
    dest = lax.broadcasted_iota(jnp.int32, (2 * lon, lon), 0).astype(F32) + float(ext * lon)
    for part in range(4):
        k = table_row(step, ext - 1 + part, rows)
        line = table[k : k + 1, :]
        out[:, part * lon : (part + 1) * lon] = jnp.where(line == dest, 1.0, 0.0).astype(BF16)


def wind_fields(codes, sign, rows):
    code = codes.astype(F32) - 1.0
    lat_q = jnp.where(code >= 5.0, 1.0, 0.0) + jnp.where(code >= 10.0, 1.0, 0.0)
    lat = jnp.where(code < 0.0, 9.0, sign * (lat_q - 1.0))
    lon = code - 5.0 * lat_q - 2.0
    fill = jnp.full((8 - rows, code.shape[1]), 9.0, F32)
    fields = []
    for step in range(code.shape[0] // rows):
        at = slice(step * rows, (step + 1) * rows)
        fields.append((jnp.concatenate([lat[at], fill], axis=0), jnp.concatenate([lon[at], fill], axis=0)))
    return fields


def shift_rows(mask, by):
    blank = jnp.zeros((1, mask.shape[1]), F32)
    if by == 1:
        return jnp.concatenate([blank, mask[:-1]], axis=0)
    if by == -1:
        return jnp.concatenate([mask[1:], blank], axis=0)
    return mask


def cells_pulled(fields, rows):
    lon = fields[0][0].shape[1]
    row = lax.broadcasted_iota(jnp.int32, (8, lon), 0)
    mask = jnp.where(row == 0, 1.0, 0.0)
    for lat, east in reversed(fields[: len(fields) - 1]):
        new = mask
        for a in (-1, 0, 1):
            total = jnp.zeros_like(mask)
            for b in range(-2, 3):
                hit = jnp.where((lat == float(a)) & (east == float(b)), mask, 0.0)
                total = jnp.maximum(total, hit if b == 0 else pltpu.roll(hit, (-b) % lon, 1))
            new = jnp.maximum(new, shift_rows(total, -a))
        mask = jnp.where(row < rows, new, 0.0)
    return mask


def cells_reached(fields, rows):
    lon = fields[0][0].shape[1]
    row = lax.broadcasted_iota(jnp.int32, (8, lon), 0)
    mask = jnp.zeros((8, lon), F32)
    for lat, east in fields:
        new = mask
        for a in (-1, 0, 1):
            source = shift_rows(mask, a)
            if a == 1:
                source = jnp.where(row == 0, 1.0, source)
            for b in range(-2, 3):
                seen = source if b == 0 else pltpu.roll(source, b % lon, 1)
                new = jnp.maximum(new, jnp.where((lat == float(a)) & (east == float(b)), seen, 0.0))
        mask = jnp.where(row < rows, new, 0.0)
    return mask


def slot_of(mask):
    lon = mask.shape[1]
    before = lax.broadcasted_iota(jnp.int32, (lon, lon), 0) < lax.broadcasted_iota(jnp.int32, (lon, lon), 1)
    place = dot(mask.astype(BF16), jnp.where(before, 1.0, 0.0).astype(BF16))
    totals = jnp.sum(mask, axis=1, keepdims=True)
    ahead = jnp.zeros((1, 1), F32)
    lines = []
    for j in range(mask.shape[0]):
        lines.append(place[j : j + 1] + ahead)
        ahead = ahead + totals[j : j + 1]
    return jnp.where(mask > 0.0, jnp.concatenate(lines, axis=0), -1.0), ahead


def choose_matrix(slots, size, rows, first=0):
    lon = slots.shape[1]
    at = lax.broadcasted_iota(jnp.int32, (size, lon), 0).astype(F32) + float(first)
    parts = [jnp.where(slots[j : j + 1] == at, 1.0, 0.0) for j in range(rows)]
    return jnp.concatenate(parts, axis=1).astype(BF16)


def spread_matrix(turned, row, size, first=0):
    at = lax.broadcasted_iota(jnp.int32, (turned.shape[0], size), 1).astype(F32) + float(first)
    return jnp.where(turned[:, row : row + 1] == at, 1.0, 0.0).astype(BF16)


def turn(slots):
    lon = slots.shape[1]
    return jnp.concatenate([slots, jnp.full((lon - slots.shape[0], lon), -1.0, F32)], axis=0).T


def sign_of(flip):
    return jnp.where(flip[0] == 1, -1.0, 1.0)


def pack_kernel(flip, tangent, wind, own, sent, codes, slots, buf, wind_b, sem):
    rows, lon = tangent.shape[0], tangent.shape[1]
    cells = rows * lon
    wind_copy = pltpu.make_async_copy(wind, wind_b, sem.at[rows])
    wind_copy.start()
    copies = []
    for j in range(rows):
        at = jnp.where(flip[0] == 1, rows - 1 - j, j)
        copies.append(pltpu.make_async_copy(tangent.at[at], buf.at[j], sem.at[j]))
        copies[-1].start()
    wind_copy.wait()
    for step in range(wind_b.shape[0]):
        for j in range(rows):
            code = jnp.where(flip[0] == 1, wind_b[step, rows - 1 - j : rows - j, :], wind_b[step, j : j + 1, :])
            codes[step * rows + j : step * rows + j + 1, :] = code.astype(F32) + 1.0
    mask = cells_pulled(wind_fields(codes[...], sign_of(flip), rows), rows)
    where, total = slot_of(mask)
    slots[...] = where
    head = codes.shape[0]
    capacity = sent.shape[0] - head
    tall = jnp.concatenate([mask, jnp.zeros((head - mask.shape[0], lon), F32)], axis=0)
    flag = jnp.broadcast_to(jnp.where(total > float(capacity), 1.0, 0.0), (head, lon))
    notes = jnp.concatenate([codes[...], tall, flag, jnp.zeros((head, own.shape[1] - 3 * lon), F32)], axis=1)
    notes = notes.astype(BF16)
    own[cells:, :] = notes
    sent[capacity:, :] = notes
    choose = choose_matrix(where, capacity, rows)
    for j in range(rows):
        copies[j].wait()
        own[j * lon : (j + 1) * lon, :] = buf[j].astype(BF16)
    sent[0:capacity, :] = dot(choose, own[0:cells, :]).astype(BF16)


def reach_kernel(flip, linked, own_slots, far_codes, far_slots, over):
    where, total = slot_of(cells_reached(wind_fields(far_codes[...], -sign_of(flip), 4), 4))
    far_slots[...] = where
    most = jnp.maximum(total, jnp.max(own_slots[...], axis=(0, 1), keepdims=True) + 1.0)
    over[0] = jnp.where(jnp.max(most) > float(FAR_COLUMNS), linked[0], 0)


def choose_kernel(flag, _one, _two, redone_one, redone_two, one, two, sem):
    @pl.when(flag[0] > 0)
    def _():
        copies = [
            pltpu.make_async_copy(redone_one, one, sem.at[0]),
            pltpu.make_async_copy(redone_two, two, sem.at[1]),
        ]
        for copy in copies:
            copy.start()
        for copy in copies:
            copy.wait()


def rest_kernel(first, slots, dense, out):
    rows = dense.shape[0] // slots.shape[1]
    cells = rows * slots.shape[1]
    choose = choose_matrix(slots[...], out.shape[0], rows, first)
    out[...] = dot(choose, dense[0:cells, :]).astype(BF16)


def blank_kernel(*outs):
    pass


def near_steps(mats, start_b, start_f, c_ref, outs, mid_b, mid_f, lon):
    c = c_ref[0:1, :]
    blocks = ((5, 7, 9), (6, 8), (7,))
    read_b, read_f, first = start_b, start_f, 4
    k = 0
    for step, exts in enumerate(blocks):
        for ext in exts:
            at = (ext - 1 - first) * lon
            pulled = dot(mats[k], read_b(at, 4 * lon))
            value = (1.0 - c) * read_f(at + lon, 2 * lon) + c * pulled
            k += 1
            if ext == exts[0]:
                outs[step][...] = value
            if step < 2:
                to = (ext - exts[0]) * lon
                mid_f[step, to : to + 2 * lon, :] = value
                mid_b[step, to : to + 2 * lon, :] = value.astype(BF16)
        first = exts[0]
        read_b = functools.partial(lambda s, a, n: mid_b[s, a : a + n, :], step)
        read_f = functools.partial(lambda s, a, n: mid_f[s, a : a + n, :], step)


def far_steps(mats, start_b, start_f, c_ref, kept, mid_b, mid_f, lon, finish):
    c = c_ref[0:1, :]
    k = 0
    for step in range(4):
        now, last = step % 2, (step + 1) % 2
        for half in range(2):
            at = 2 * half * lon
            if step == 0:
                window, own = start_b(at, 4 * lon), start_f(at + lon, 2 * lon)
            else:
                window = mid_b[last, at : at + 4 * lon, :]
                own = mid_f[last, at + lon : at + 3 * lon, :]
            value = (1.0 - c) * own + c * dot(mats[k][...], window)
            k += 1
            if step < 3:
                mid_f[now, at : at + 2 * lon, :] = value
                mid_b[now, at : at + 2 * lon, :] = value.astype(BF16)
            else:
                finish(half, value)
        if step < 3:
            carried = kept[step][...]
            mid_f[now, 4 * lon :, :] = carried
            mid_b[now, 4 * lon :, :] = carried.astype(BF16)


def near_kernel(
    flip, obs_count, tangent, codes, near, courant, background, w_first, w_second, obs_index, obs_quality,
    slope_one, slope_two, kept_a, kept_b, kept_c, pick, place, place_far, near_codes, quality, slots, own_mats, own_f, own_b,
    table, mats, cells_b, mid_b, mid_f, hidden,
):
    rows, lon = tangent.shape[0], tangent.shape[1]
    cells = rows * lon
    sign = sign_of(flip)
    table[...] = jnp.zeros_like(table)
    near_codes[...] = near[cells:, 0:lon].astype(F32)
    store_sources(table, 1, codes[...], False, sign, lon, rows)
    store_sources(table, 2, near_codes[...], True, sign, lon, rows)
    turned = table[...].T
    k = 0
    for step, exts in enumerate(((5, 7, 9), (6, 8), (7,))):
        for ext in exts:
            pull_matrix(mats.at[k], turned, step, ext, lon, rows)
            k += 1
    for k, (step, half) in enumerate(OWN_BLOCKS):
        pull_matrix(own_mats.at[k], turned, step, step + 1 + 2 * half, lon, rows)
    for j in range(rows):
        row = tangent[jnp.where(flip[0] == 1, rows - 1 - j, j)]
        cells_b[j * lon : (j + 1) * lon, :] = row.astype(BF16)
        cells_b[(rows + j) * lon : (rows + j + 1) * lon, :] = near[(rows - 1 - j) * lon : (rows - j) * lon, :]

    own_f[...] = tangent[jnp.where(flip[0] == 1, rows - 1, 0)]
    own_b[...] = cells_b[0 : 2 * lon, :]

    def start_f(at, size):
        pieces = []
        for row in range(at // lon, (at + size) // lon):
            if row < rows:
                pieces.append(tangent[jnp.where(flip[0] == 1, rows - 1 - row, row)])
            else:
                pieces.append(cells_b[row * lon : (row + 1) * lon, :].astype(F32))
        return jnp.concatenate(pieces, axis=0)

    near_steps(
        mats, lambda at, size: cells_b[at : at + size, :], start_f, courant,
        (kept_a, kept_b, kept_c), mid_b, mid_f, lon,
    )

    first_tanh = jnp.tanh(dot(background[...], w_first[...]))
    hidden[...] = first_tanh.astype(BF16)
    slope_one[...] = 1.0 - first_tanh * first_tanh
    second_tanh = jnp.tanh(dot(hidden[...], w_second[...]))
    slope_two[...] = 1.0 - second_tanh * second_tanh

    count = obs_index.shape[1]
    at = obs_index[...]
    at = jnp.where(flip[0] == 1, at + (rows - 1 - 2 * lax.div(at, lon)) * lon, at)
    live = lax.broadcasted_iota(jnp.int32, at.shape, 1) < obs_count[0]
    at = jnp.where(live, at, -1)
    chosen = at == lax.broadcasted_iota(jnp.int32, (cells, count), 0)
    place[...] = jnp.where(chosen, 1.0, 0.0).astype(BF16)
    lines = jnp.concatenate([at.astype(F32), jnp.where(live, obs_quality[...].astype(F32), 0.0)], axis=0)
    lines = jnp.concatenate([lines, jnp.zeros((6, count), F32)], axis=0)
    lines = jnp.concatenate([lines, jnp.zeros((8, cells - count), F32)], axis=1).T
    quality[...] = lines[0:count, 1:2]
    columns = lax.broadcasted_iota(jnp.int32, (count, cells), 1).astype(F32)
    pick[...] = jnp.where(lines[0:count, 0:1] == columns, 1.0, 0.0).astype(BF16)
    where, _ = slot_of(cells_reached(wind_fields(codes[...], sign, rows), rows))
    slots[...] = where
    place_far[...] = dot(choose_matrix(slots[...], place_far.shape[0], rows), place[...]).astype(BF16)


def observe_kernel(
    redo, flip, linked, slots, own_f, own_b, codes, far, rest, courant, slope_one, slope_two, kept_a, kept_b, kept_c,
    hbm_first, hbm_second, hbm_third, pick, place, place_far, quality, chan_weight, own_mats,
    hbm_out, hbm_sent, hbm_codes, over,
    table, mats, cells_b, mid_b, mid_f, last_b, one_b, two_b, w_first, w_second, w_third, out, sent, far_codes, sem,
    rest_b,
):
    rows, lon = 4, own_f.shape[0]
    cells = rows * lon
    sign = sign_of(flip)
    capacity = far.shape[0] - codes.shape[0]
    loads = [
        pltpu.make_async_copy(hbm_first, w_first, sem.at[0]),
        pltpu.make_async_copy(hbm_second, w_second, sem.at[1]),
        pltpu.make_async_copy(hbm_third, w_third, sem.at[2]),
    ]
    for copy in loads:
        copy.start()
    table[...] = jnp.zeros_like(table)
    far_codes[...] = far[capacity:, 0:lon].astype(F32)
    store_sources(table, 0, far_codes[...], True, sign, lon, rows)
    store_sources(table, 1, codes[...], False, sign, lon, rows)
    turned = table[...].T
    keep_codes = pltpu.make_async_copy(far_codes, hbm_codes, sem.at[3])
    keep_codes.start()
    chosen = [None] * 8
    for k, (step, half) in enumerate(OWN_BLOCKS):
        chosen[2 * step + half] = own_mats.at[k]
    for k, (step, half) in enumerate(FAR_BLOCKS):
        pull_matrix(mats.at[k], turned, step, step + 1 + 2 * half, lon, rows)
        chosen[2 * step + half] = mats.at[k]
    where, _ = slot_of(far[capacity:, lon : 2 * lon].astype(F32)[0:8])
    where = turn(where)
    most = jnp.maximum(jnp.max(far[capacity:, 2 * lon : 3 * lon].astype(F32)), jnp.where(jnp.max(slots[...]) >= float(capacity), 1.0, 0.0))
    over[0] = jnp.where(most > 0.0, linked[0], 0)
    for j in range(rows):
        value = dot(spread_matrix(where, j, capacity), far[0:capacity, :])
        cells_b[(rows - 1 - j) * lon : (rows - j) * lon, :] = value.astype(BF16)
    cells_b[cells:, :] = own_b[...]

    if redo:
        copy = pltpu.make_async_copy(rest, rest_b, sem.at[5])
        copy.start()
        copy.wait()
        for j in range(rows):
            value = dot(spread_matrix(where, j, rest_b.shape[0], capacity), rest_b[...])
            at = slice((rows - 1 - j) * lon, (rows - j) * lon)
            cells_b[at, :] = (cells_b[at, :].astype(F32) + value).astype(BF16)

    def start_f(at, size):
        pieces = []
        for row in range(at // lon, (at + size) // lon):
            if row == rows:
                pieces.append(own_f[...])
            else:
                pieces.append(cells_b[row * lon : (row + 1) * lon, :].astype(F32))
        return jnp.concatenate(pieces, axis=0)

    def finish(half, value):
        last_b[2 * half * lon : 2 * (half + 1) * lon, :] = value.astype(BF16)

    far_steps(
        chosen, lambda at, size: cells_b[at : at + size, :], start_f, courant,
        (kept_a, kept_b, kept_c), mid_b, mid_f, lon, finish,
    )
    one_b[...] = dot(pick[...], last_b[...]).astype(BF16)
    loads[0].wait()
    two_b[...] = (slope_one[...] * dot(one_b[...], w_first[...])).astype(BF16)
    loads[1].wait()
    one_b[...] = (slope_two[...] * dot(two_b[...], w_second[...])).astype(BF16)
    loads[2].wait()
    scale = quality[...] * chan_weight[0:1, :]
    two_b[...] = (scale * dot(one_b[...], w_third[...])).astype(BF16)
    one_b[...] = (slope_two[...] * dot_t(two_b[...], w_third[...])).astype(BF16)
    two_b[...] = (slope_one[...] * dot_t(one_b[...], w_second[...])).astype(BF16)
    one_b[...] = dot_t(two_b[...], w_first[...]).astype(BF16)
    sent[...] = dot(place_far[...], one_b[...]).astype(BF16)
    keep_sent = pltpu.make_async_copy(sent, hbm_sent, sem.at[4])
    keep_sent.start()
    out[...] = dot(place[...], one_b[...]).astype(BF16)
    keep_out = pltpu.make_async_copy(out, hbm_out, sem.at[0])
    keep_out.start()
    keep_codes.wait()
    keep_sent.wait()
    keep_out.wait()


def near_adjoint_kernel(
    flip, rest, cells_own, cells_near, codes, near_codes, far_codes, far_slots, courant,
    kept_a, kept_b, kept_c, far_mats, spread,
    table, mats, cells_b, mid_b, mid_f,
):
    rows, lon = 4, table.shape[1]
    cells = rows * lon
    sign = sign_of(flip)
    store_sources(table, 0, far_codes[...], True, sign, lon, rows)
    store_sources(table, 1, codes[...], False, sign, lon, rows)
    store_sources(table, 2, near_codes[...], True, sign, lon, rows)
    k = 0
    for order, exts in enumerate(((5, 7, 9), (6, 8), (7,))):
        for ext in exts:
            push_matrix(mats.at[k], table, 3 - order, ext, lon, rows)
            k += 1
    cells_b[0:cells, :] = cells_own[...]
    for j in range(rows):
        cells_b[(rows + j) * lon : (rows + j + 1) * lon, :] = cells_near[
            (rows - 1 - j) * lon : (rows - j) * lon, :
        ]
    near_steps(
        mats, lambda at, size: cells_b[at : at + size, :],
        lambda at, size: cells_b[at : at + size, :].astype(F32), courant,
        (kept_a, kept_b, kept_c), mid_b, mid_f, lon,
    )
    for order in range(4):
        for half in range(2):
            push_matrix(far_mats.at[2 * order + half], table, 3 - order, order + 1 + 2 * half, lon, rows)
    where = turn(far_slots[...])
    capacity = spread.shape[1]
    for j in range(rows):
        spread[j * lon : (j + 1) * lon, :] = spread_matrix(where, j, capacity)


def far_adjoint_kernel(
    flip, flag, cells_own, far, rest, courant, kept_a, kept_b, kept_c, mats, spread, far_slots,
    out,
    cells_b, mid_b, mid_f, result, rest_b, sem,
):
    rows, lon = out.shape[0], out.shape[1]
    cells = rows * lon
    for j in range(rows):
        value = dot(spread[j * lon : (j + 1) * lon, :], far[...])
        cells_b[(rows - 1 - j) * lon : (rows - j) * lon, :] = value.astype(BF16)
    cells_b[cells:, :] = cells_own[0 : 2 * lon, :]

    @pl.when(flag[0] > 0)
    def _():
        copy = pltpu.make_async_copy(rest, rest_b, sem.at[rows])
        copy.start()
        copy.wait()
        where = turn(far_slots[...])
        for j in range(rows):
            value = dot(spread_matrix(where, j, rest_b.shape[0], spread.shape[1]), rest_b[...])
            at = slice((rows - 1 - j) * lon, (rows - j) * lon)
            cells_b[at, :] = (cells_b[at, :].astype(F32) + value).astype(BF16)

    copies = []

    def finish(half, value):
        for part in range(2):
            j = 2 * half + part
            result[j] = value[part * lon : (part + 1) * lon, :]
            at = jnp.where(flip[0] == 1, rows - 1 - j, j)
            copies.append(pltpu.make_async_copy(result.at[j], out.at[at], sem.at[j]))
            copies[-1].start()

    far_steps(
        [mats.at[k] for k in range(8)], lambda at, size: cells_b[at : at + size, :],
        lambda at, size: cells_b[at : at + size, :].astype(F32), courant,
        (kept_a, kept_b, kept_c), mid_b, mid_f, lon, finish,
    )
    for copy in copies:
        copy.wait()


def params():
    return pltpu.CompilerParams(vmem_limit_bytes=VMEM_LIMIT)


def shape(dims, dtype):
    return jax.ShapeDtypeStruct(dims, dtype)


def send_rest(first, slots, dense, size, links):
    rest = pl.pallas_call(
        functools.partial(rest_kernel, first),
        out_shape=shape((size, dense.shape[1]), BF16),
        in_specs=[VMEM, VMEM],
        out_specs=VMEM,
        name="rest",
    )(slots, dense)
    return lax.ppermute(rest, "lat", links)


def blank(outs):
    return pl.pallas_call(blank_kernel, out_shape=outs, out_specs=[ANY] * len(outs), name="blank")()


def local(
    tangent,
    wind_code,
    courant,
    obs_index,
    obs_count,
    obs_quality,
    background,
    w_first,
    w_second,
    w_third,
    chan_weight,
):
    rows, lon, levels = tangent.shape
    cells = rows * lon
    head = wind_code.shape[0] * rows
    listed = obs_index.shape[1]
    hidden_size = w_first.shape[1]
    count = lax.axis_size("lat")
    here = lax.axis_index("lat")
    odd = (here % 2).astype(jnp.int32)
    flip = odd.reshape(1)
    linked = ((here > 0) & (here < count - 1)).astype(jnp.int32).reshape(1)
    pairs = [(i, i ^ 1) for i in range(count)]
    links = [(i, i + 1) for i in range(1, count - 1, 2)]
    links = links + [(b, a) for a, b in links]

    own, sent, codes, slots = pl.pallas_call(
        pack_kernel,
        out_shape=[
            shape((cells + head, levels), BF16),
            shape((FAR_CELLS + head, levels), BF16),
            shape((head, lon), F32),
            shape((8, lon), F32),
        ],
        in_specs=[SMEM, HBM, HBM],
        out_specs=[VMEM] * 4,
        scratch_shapes=[
            pltpu.VMEM((rows, lon, levels), F32),
            pltpu.VMEM(wind_code.shape, jnp.int32),
            pltpu.SemaphoreType.DMA((rows + 1,)),
        ],
        compiler_params=pltpu.CompilerParams(vmem_limit_bytes=PACK_LIMIT),
        name="pack",
    )(flip, tangent, wind_code)

    far = lax.ppermute(sent, "lat", links)
    near = lax.ppermute(own, "lat", pairs)

    c_row = courant.reshape(1, levels)
    kept_shape = [shape((2 * lon, levels), F32)] * 3
    slope_shape = shape((listed, hidden_size), F32)

    def run_near():
        return pl.pallas_call(
            near_kernel,
            out_shape=[slope_shape, slope_shape]
            + kept_shape
            + [
                shape((listed, cells), BF16),
                shape((cells, listed), BF16),
                shape((FAR_COLUMNS, listed), BF16),
                shape((head, lon), F32),
                shape((listed, 1), F32),
                shape((8, lon), F32),
                shape((4, 2 * lon, 4 * lon), BF16),
                shape((lon, levels), F32),
                shape((2 * lon, levels), BF16),
            ],
            in_specs=[SMEM, SMEM] + [VMEM] * 9,
            out_specs=[VMEM] * 14,
            scratch_shapes=[
                pltpu.VMEM((lon, lon), F32),
                pltpu.VMEM((6, 2 * lon, 4 * lon), BF16),
                pltpu.VMEM((2 * cells, levels), BF16),
                pltpu.VMEM((2, 6 * lon, levels), BF16),
                pltpu.VMEM((2, 6 * lon, levels), F32),
                pltpu.VMEM((listed, hidden_size), BF16),
            ],
            compiler_params=params(),
            cost_estimate=pl.CostEstimate(flops=4_000_000_000, bytes_accessed=16_000_000, transcendentals=1_000_000),
            name="near",
        )(
            flip, obs_count, tangent, codes, near, c_row, background[0], w_first, w_second, obs_index, obs_quality,
        )

    column_shape = [pltpu.HBM((cells, levels), BF16), pltpu.HBM((FAR_COLUMNS, levels), BF16)]

    def run_observe(redo, parts, rest):
        slope_one, slope_two, kept_a, kept_b, kept_c, pick, place, place_far = parts[:8]
        quality, _, own_mats, own_f, own_b = parts[9:]
        rest_specs = [ANY] if redo else []
        body = functools.partial(observe_kernel, redo)
        rest_args = [rest] if redo else []
        rest_scratch = [pltpu.VMEM((cells - FAR_CELLS, levels), BF16)]

        def kernel(*refs):
            refs = list(refs)
            if not redo:
                refs.insert(7, None)
                refs.append(None)
            body(*refs)

        return pl.pallas_call(
            kernel,
            out_shape=column_shape + [pltpu.HBM((head, lon), F32), shape((1,), jnp.int32)],
            in_specs=[SMEM, SMEM] + [VMEM] * 5 + rest_specs + [VMEM] * 6 + [ANY] * 3 + [VMEM] * 6,
            out_specs=[HBM] * 3 + [SMEM],
            scratch_shapes=[
                pltpu.VMEM((lon, lon), F32),
                pltpu.VMEM((4, 2 * lon, 4 * lon), BF16),
                pltpu.VMEM((6 * lon, levels), BF16),
                pltpu.VMEM((2, 6 * lon, levels), BF16),
                pltpu.VMEM((2, 6 * lon, levels), F32),
                pltpu.VMEM((cells, levels), BF16),
                pltpu.VMEM((listed, levels), BF16),
                pltpu.VMEM((listed, levels), BF16),
                pltpu.VMEM(w_first.shape, BF16),
                pltpu.VMEM(w_second.shape, BF16),
                pltpu.VMEM(w_third.shape, BF16),
                pltpu.VMEM((cells, levels), BF16),
                pltpu.VMEM((FAR_COLUMNS, levels), BF16),
                pltpu.VMEM((head, lon), F32),
                pltpu.SemaphoreType.DMA((6,)),
            ]
            + (rest_scratch if redo else []),
            compiler_params=params(),
            name="observe",
        )(
            flip, linked, slots, own_f, own_b, codes, far, *rest_args, c_row,
            slope_one, slope_two, kept_a, kept_b, kept_c, w_first, w_second, w_third,
            pick, place, place_far, quality, chan_weight.reshape(1, -1), own_mats,
        )

    parts = run_near()
    near_codes, own_slots = parts[8], parts[10]
    cells_own, sent, far_codes, over = run_observe(False, parts, None)

    def observe_again():
        rest = send_rest(FAR_CELLS, slots, own, cells - FAR_CELLS, links)
        return run_observe(True, run_near(), rest)[:2]

    redone = lax.cond(over[0] > 0, observe_again, lambda: blank(column_shape))
    cells_own, sent = pl.pallas_call(
        choose_kernel,
        out_shape=column_shape,
        in_specs=[SMEM] + [HBM] * 4,
        out_specs=[HBM] * 2,
        scratch_shapes=[pltpu.SemaphoreType.DMA((2,))],
        input_output_aliases={1: 0, 2: 1},
        name="choose",
    )(over, cells_own, sent, *redone)

    columns_far = lax.ppermute(sent, "lat", links)
    cells_near = lax.ppermute(cells_own, "lat", pairs)

    far_slots, over = pl.pallas_call(
        reach_kernel,
        out_shape=[shape((8, lon), F32), shape((1,), jnp.int32)],
        in_specs=[SMEM, SMEM, VMEM, VMEM],
        out_specs=[VMEM, SMEM],
        name="reach",
    )(flip, linked, own_slots, far_codes)
    left = cells - FAR_COLUMNS
    rest = lax.cond(
        over[0] > 0,
        lambda: send_rest(FAR_COLUMNS, own_slots, cells_own, left, links),
        lambda: blank([shape((left, levels), BF16)])[0],
    )
    kept_a, kept_b, kept_c, mats, spread = pl.pallas_call(
        near_adjoint_kernel,
        out_shape=kept_shape
        + [
            shape((8, 2 * lon, 4 * lon), BF16),
            shape((cells, FAR_COLUMNS), BF16),
        ],
        in_specs=[SMEM, ANY] + [VMEM] * 7,
        out_specs=[VMEM] * 5,
        scratch_shapes=[
            pltpu.VMEM((lon, lon), F32),
            pltpu.VMEM((6, 2 * lon, 4 * lon), BF16),
            pltpu.VMEM((2 * cells, levels), BF16),
            pltpu.VMEM((2, 6 * lon, levels), BF16),
            pltpu.VMEM((2, 6 * lon, levels), F32),
        ],
        compiler_params=params(),
        cost_estimate=pl.CostEstimate(flops=2_000_000_000, bytes_accessed=8_000_000, transcendentals=0),
        name="near_adjoint",
    )(flip, rest, cells_own, cells_near, codes, near_codes, far_codes, far_slots, c_row)

    return pl.pallas_call(
        far_adjoint_kernel,
        out_shape=shape((rows, lon, levels), F32),
        in_specs=[SMEM, SMEM, VMEM, VMEM, ANY] + [VMEM] * 7,
        out_specs=HBM,
        scratch_shapes=[
            pltpu.VMEM((6 * lon, levels), BF16),
            pltpu.VMEM((2, 6 * lon, levels), BF16),
            pltpu.VMEM((2, 6 * lon, levels), F32),
            pltpu.VMEM((rows, lon, levels), F32),
            pltpu.VMEM((cells - FAR_COLUMNS, levels), BF16),
            pltpu.SemaphoreType.DMA((rows + 1,)),
        ],
        compiler_params=params(),
        name="far_adjoint",
    )(
        flip, over, cells_own, columns_far, rest, c_row,
        kept_a, kept_b, kept_c, mats, spread, far_slots,
    )


def solution(mesh):
    placed = (
        P(("groups", "lat"), None, None),
        P(None, ("groups", "lat"), None),
        P(),
        P(("groups", "lat"), None),
        P(("groups", "lat")),
        P(("groups", "lat"), None),
        P(("groups", "lat"), None, None),
        P(),
        P(),
        P(),
        P(),
    )
    return jax.shard_map(
        local,
        mesh=mesh,
        in_specs=placed,
        out_specs=P(("groups", "lat"), None, None),
        check_vma=False,
    )
```

```python
import functools

import jax
import jax.numpy as jnp
from jax import lax
from jax.experimental import pallas as pl
from jax.experimental.pallas import tpu as pltpu
from jax.sharding import PartitionSpec as P

F32 = jnp.float32
BF16 = jnp.bfloat16
PART = 512
FAR_CELLS = 304
FAR_COLUMNS = 272
ANY = pl.BlockSpec(memory_space=pl.ANY)
VMEM = pl.BlockSpec(memory_space=pltpu.VMEM)
HBM = pl.BlockSpec(memory_space=pltpu.HBM)
SMEM = pl.BlockSpec(memory_space=pltpu.SMEM)
VMEM_LIMIT = 32 * 1024 * 1024
PACK_LIMIT = 60 * 1024 * 1024

OWN_BLOCKS = ((1, 1), (2, 1), (3, 0), (3, 1))
FAR_BLOCKS = ((0, 0), (0, 1), (1, 0), (2, 0))


def dot_t(left, right):
    return lax.dot_general(left, right, (((1,), (1,)), ((), ())), preferred_element_type=F32)


def dot(left, right):
    return jnp.dot(left, right, preferred_element_type=F32)


def store_sources(table, slot, codes, mirrored, sign, lon, rows):
    code = codes.astype(F32) - 1.0
    lat_q = jnp.where(code >= 5.0, 1.0, 0.0) + jnp.where(code >= 10.0, 1.0, 0.0)
    lon_step = code - 5.0 * lat_q - 2.0
    col = lax.broadcasted_iota(jnp.int32, code.shape, 1).astype(F32) - lon_step
    col = jnp.where(col < 0.0, col + lon, jnp.where(col >= lon, col - lon, col))
    stored = lax.broadcasted_iota(jnp.int32, code.shape, 0) & (rows - 1)
    row = (rows - 1 - stored) if mirrored else stored
    row = (row + slot * rows).astype(F32)
    src = (row - sign * (lat_q - 1.0)) * lon + col
    table[slot * code.shape[0] : (slot + 1) * code.shape[0], :] = jnp.where(code < 0.0, -65536.0, src)


def table_row(step, ext, rows):
    slot, at = ext // rows, ext % rows
    return slot * rows * rows + step * rows + (at if slot == 1 else rows - 1 - at)


def pull_matrix(out, turned, step, ext, lon, rows):
    span = 4 * lon
    lanes = lax.broadcasted_iota(jnp.int32, (lon, span), 1).astype(F32) + float((ext - 1) * lon)
    for half in range(2):
        k = table_row(step, ext + half, rows)
        column = turned[:, k : k + 1]
        out[half * lon : (half + 1) * lon, :] = jnp.where(column == lanes, 1.0, 0.0).astype(BF16)


def push_matrix(out, table, step, ext, lon, rows):
    dest = lax.broadcasted_iota(jnp.int32, (2 * lon, lon), 0).astype(F32) + float(ext * lon)
    for part in range(4):
        k = table_row(step, ext - 1 + part, rows)
        line = table[k : k + 1, :]
        out[:, part * lon : (part + 1) * lon] = jnp.where(line == dest, 1.0, 0.0).astype(BF16)


def wind_fields(codes, sign, rows):
    code = codes.astype(F32) - 1.0
    lat_q = jnp.where(code >= 5.0, 1.0, 0.0) + jnp.where(code >= 10.0, 1.0, 0.0)
    lat = jnp.where(code < 0.0, 9.0, sign * (lat_q - 1.0))
    lon = code - 5.0 * lat_q - 2.0
    fill = jnp.full((8 - rows, code.shape[1]), 9.0, F32)
    fields = []
    for step in range(code.shape[0] // rows):
        at = slice(step * rows, (step + 1) * rows)
        fields.append((jnp.concatenate([lat[at], fill], axis=0), jnp.concatenate([lon[at], fill], axis=0)))
    return fields


def shift_rows(mask, by):
    blank = jnp.zeros((1, mask.shape[1]), F32)
    if by == 1:
        return jnp.concatenate([blank, mask[:-1]], axis=0)
    if by == -1:
        return jnp.concatenate([mask[1:], blank], axis=0)
    return mask


def cells_pulled(fields, rows):
    lon = fields[0][0].shape[1]
    row = lax.broadcasted_iota(jnp.int32, (8, lon), 0)
    mask = jnp.where(row == 0, 1.0, 0.0)
    for lat, east in reversed(fields[: len(fields) - 1]):
        new = mask
        for a in (-1, 0, 1):
            total = jnp.zeros_like(mask)
            for b in range(-2, 3):
                hit = jnp.where((lat == float(a)) & (east == float(b)), mask, 0.0)
                total = jnp.maximum(total, hit if b == 0 else pltpu.roll(hit, (-b) % lon, 1))
            new = jnp.maximum(new, shift_rows(total, -a))
        mask = jnp.where(row < rows, new, 0.0)
    return mask


def cells_reached(fields, rows):
    lon = fields[0][0].shape[1]
    row = lax.broadcasted_iota(jnp.int32, (8, lon), 0)
    mask = jnp.zeros((8, lon), F32)
    for lat, east in fields:
        new = mask
        for a in (-1, 0, 1):
            source = shift_rows(mask, a)
            if a == 1:
                source = jnp.where(row == 0, 1.0, source)
            for b in range(-2, 3):
                seen = source if b == 0 else pltpu.roll(source, b % lon, 1)
                new = jnp.maximum(new, jnp.where((lat == float(a)) & (east == float(b)), seen, 0.0))
        mask = jnp.where(row < rows, new, 0.0)
    return mask


def slot_of(mask):
    lon = mask.shape[1]
    before = lax.broadcasted_iota(jnp.int32, (lon, lon), 0) < lax.broadcasted_iota(jnp.int32, (lon, lon), 1)
    place = dot(mask.astype(BF16), jnp.where(before, 1.0, 0.0).astype(BF16))
    totals = jnp.sum(mask, axis=1, keepdims=True)
    ahead = jnp.zeros((1, 1), F32)
    lines = []
    for j in range(mask.shape[0]):
        lines.append(place[j : j + 1] + ahead)
        ahead = ahead + totals[j : j + 1]
    return jnp.where(mask > 0.0, jnp.concatenate(lines, axis=0), -1.0), ahead


def choose_matrix(slots, size, rows, first=0):
    lon = slots.shape[1]
    at = lax.broadcasted_iota(jnp.int32, (size, lon), 0).astype(F32) + float(first)
    parts = [jnp.where(slots[j : j + 1] == at, 1.0, 0.0) for j in range(rows)]
    return jnp.concatenate(parts, axis=1).astype(BF16)


def spread_matrix(turned, row, size, first=0):
    at = lax.broadcasted_iota(jnp.int32, (turned.shape[0], size), 1).astype(F32) + float(first)
    return jnp.where(turned[:, row : row + 1] == at, 1.0, 0.0).astype(BF16)


def turn(slots):
    lon = slots.shape[1]
    return jnp.concatenate([slots, jnp.full((lon - slots.shape[0], lon), -1.0, F32)], axis=0).T


def sign_of(flip):
    return jnp.where(flip[0] == 1, -1.0, 1.0)


def pack_kernel(flip, tangent, wind, own, sent, codes, slots, buf, wind_b, sem):
    rows, lon = tangent.shape[0], tangent.shape[1]
    cells = rows * lon
    wind_copy = pltpu.make_async_copy(wind, wind_b, sem.at[rows])
    wind_copy.start()
    copies = []
    for j in range(rows):
        at = jnp.where(flip[0] == 1, rows - 1 - j, j)
        copies.append(pltpu.make_async_copy(tangent.at[at], buf.at[j], sem.at[j]))
        copies[-1].start()
    wind_copy.wait()
    for step in range(wind_b.shape[0]):
        for j in range(rows):
            code = jnp.where(flip[0] == 1, wind_b[step, rows - 1 - j : rows - j, :], wind_b[step, j : j + 1, :])
            codes[step * rows + j : step * rows + j + 1, :] = code.astype(F32) + 1.0
    mask = cells_pulled(wind_fields(codes[...], sign_of(flip), rows), rows)
    where, total = slot_of(mask)
    slots[...] = where
    head = codes.shape[0]
    capacity = sent.shape[0] - head
    tall = jnp.concatenate([mask, jnp.zeros((head - mask.shape[0], lon), F32)], axis=0)
    flag = jnp.broadcast_to(jnp.where(total > float(capacity), 1.0, 0.0), (head, lon))
    notes = jnp.concatenate([codes[...], tall, flag, jnp.zeros((head, own.shape[1] - 3 * lon), F32)], axis=1)
    notes = notes.astype(BF16)
    own[cells:, :] = notes
    sent[capacity:, :] = notes
    choose = choose_matrix(where, capacity, rows)
    for j in range(rows):
        copies[j].wait()
        own[j * lon : (j + 1) * lon, :] = buf[j].astype(BF16)
    sent[0:capacity, :] = dot(choose, own[0:cells, :]).astype(BF16)


def reach_kernel(flip, linked, own_slots, far_codes, far_slots, over):
    where, total = slot_of(cells_reached(wind_fields(far_codes[...], -sign_of(flip), 4), 4))
    far_slots[...] = where
    most = jnp.maximum(total, jnp.max(own_slots[...], axis=(0, 1), keepdims=True) + 1.0)
    over[0] = jnp.where(jnp.max(most) > float(FAR_COLUMNS), linked[0], 0)


def choose_kernel(flag, _one, _two, redone_one, redone_two, one, two, sem):
    @pl.when(flag[0] > 0)
    def _():
        copies = [
            pltpu.make_async_copy(redone_one, one, sem.at[0]),
            pltpu.make_async_copy(redone_two, two, sem.at[1]),
        ]
        for copy in copies:
            copy.start()
        for copy in copies:
            copy.wait()


def rest_kernel(first, slots, dense, out):
    rows = dense.shape[0] // slots.shape[1]
    cells = rows * slots.shape[1]
    choose = choose_matrix(slots[...], out.shape[0], rows, first)
    out[...] = dot(choose, dense[0:cells, :]).astype(BF16)


def blank_kernel(*outs):
    pass


def near_steps(mats, start_b, start_f, c_ref, outs, mid_b, mid_f, lon, cs):
    c = c_ref[0:1, cs]
    blocks = ((5, 7, 9), (6, 8), (7,))
    read_b, read_f, first = start_b, start_f, 4
    k = 0
    for step, exts in enumerate(blocks):
        for ext in exts:
            at = (ext - 1 - first) * lon
            pulled = dot(mats[k], read_b(at, 4 * lon))
            value = (1.0 - c) * read_f(at + lon, 2 * lon) + c * pulled
            k += 1
            if ext == exts[0]:
                outs[step][:, cs] = value
            if step < 2:
                to = (ext - exts[0]) * lon
                mid_f[step, to : to + 2 * lon, :] = value
                mid_b[step, to : to + 2 * lon, :] = value.astype(BF16)
        first = exts[0]
        read_b = functools.partial(lambda s, a, n: mid_b[s, a : a + n, :], step)
        read_f = functools.partial(lambda s, a, n: mid_f[s, a : a + n, :], step)


def by_parts(levels, body):
    @pl.loop(0, levels // PART)
    def _(i):
        body(pl.ds(pl.multiple_of(i * PART, PART), PART))


def far_steps(mats, start_b, start_f, c_ref, kept, mid_b, mid_f, lon, finish):
    c = c_ref[0:1, :]
    k = 0
    for step in range(4):
        now, last = step % 2, (step + 1) % 2
        for half in range(2):
            at = 2 * half * lon
            if step == 0:
                window, own = start_b(at, 4 * lon), start_f(at + lon, 2 * lon)
            else:
                window = mid_b[last, at : at + 4 * lon, :]
                own = mid_f[last, at + lon : at + 3 * lon, :]
            value = (1.0 - c) * own + c * dot(mats[k][...], window)
            k += 1
            if step < 3:
                mid_f[now, at : at + 2 * lon, :] = value
                mid_b[now, at : at + 2 * lon, :] = value.astype(BF16)
            else:
                finish(half, value)
        if step < 3:
            carried = kept[step][...]
            mid_f[now, 4 * lon :, :] = carried
            mid_b[now, 4 * lon :, :] = carried.astype(BF16)


def near_kernel(
    flip, obs_count, tangent, codes, near, courant, background, w_first, w_second, obs_index, obs_quality,
    slope_one, slope_two, kept_a, kept_b, kept_c, pick, place, place_far, near_codes, quality, slots, own_mats, own_f, own_b,
    table, mats, cells_b, mid_b, mid_f, hidden,
):
    rows, lon = tangent.shape[0], tangent.shape[1]
    cells = rows * lon
    sign = sign_of(flip)
    table[...] = jnp.zeros_like(table)
    near_codes[...] = near[cells:, 0:lon].astype(F32)
    store_sources(table, 1, codes[...], False, sign, lon, rows)
    store_sources(table, 2, near_codes[...], True, sign, lon, rows)
    turned = table[...].T
    k = 0
    for step, exts in enumerate(((5, 7, 9), (6, 8), (7,))):
        for ext in exts:
            pull_matrix(mats.at[k], turned, step, ext, lon, rows)
            k += 1
    for k, (step, half) in enumerate(OWN_BLOCKS):
        pull_matrix(own_mats.at[k], turned, step, step + 1 + 2 * half, lon, rows)
    for j in range(rows):
        row = tangent[jnp.where(flip[0] == 1, rows - 1 - j, j)]
        cells_b[j * lon : (j + 1) * lon, :] = row.astype(BF16)
        cells_b[(rows + j) * lon : (rows + j + 1) * lon, :] = near[(rows - 1 - j) * lon : (rows - j) * lon, :]

    own_f[...] = tangent[jnp.where(flip[0] == 1, rows - 1, 0)]
    own_b[...] = cells_b[0 : 2 * lon, :]

    def advect(cs):
        def start_f(at, size):
            pieces = []
            for row in range(at // lon, (at + size) // lon):
                if row < rows:
                    pieces.append(tangent[jnp.where(flip[0] == 1, rows - 1 - row, row), :, cs])
                else:
                    pieces.append(cells_b[row * lon : (row + 1) * lon, cs].astype(F32))
            return jnp.concatenate(pieces, axis=0)

        near_steps(
            mats, lambda at, size: cells_b[at : at + size, cs], start_f, courant,
            (kept_a, kept_b, kept_c), mid_b, mid_f, lon, cs,
        )

    by_parts(tangent.shape[2], advect)

    def first_layer(cs):
        first_tanh = jnp.tanh(dot(background[...], w_first[:, cs]))
        hidden[:, cs] = first_tanh.astype(BF16)
        slope_one[:, cs] = 1.0 - first_tanh * first_tanh

    by_parts(w_first.shape[1], first_layer)

    def second_layer(cs):
        second_tanh = jnp.tanh(dot(hidden[...], w_second[:, cs]))
        slope_two[:, cs] = 1.0 - second_tanh * second_tanh

    by_parts(w_second.shape[1], second_layer)

    count = obs_index.shape[1]
    at = obs_index[...]
    at = jnp.where(flip[0] == 1, at + (rows - 1 - 2 * lax.div(at, lon)) * lon, at)
    live = lax.broadcasted_iota(jnp.int32, at.shape, 1) < obs_count[0]
    at = jnp.where(live, at, -1)
    chosen = at == lax.broadcasted_iota(jnp.int32, (cells, count), 0)
    place[...] = jnp.where(chosen, 1.0, 0.0).astype(BF16)
    lines = jnp.concatenate([at.astype(F32), jnp.where(live, obs_quality[...].astype(F32), 0.0)], axis=0)
    lines = jnp.concatenate([lines, jnp.zeros((6, count), F32)], axis=0)
    lines = jnp.concatenate([lines, jnp.zeros((8, cells - count), F32)], axis=1).T
    quality[...] = lines[0:count, 1:2]
    columns = lax.broadcasted_iota(jnp.int32, (count, cells), 1).astype(F32)
    pick[...] = jnp.where(lines[0:count, 0:1] == columns, 1.0, 0.0).astype(BF16)
    where, _ = slot_of(cells_reached(wind_fields(codes[...], sign, rows), rows))
    slots[...] = where
    place_far[...] = dot(choose_matrix(slots[...], place_far.shape[0], rows), place[...]).astype(BF16)


def observe_kernel(
    redo, flip, linked, slots, own_f, own_b, codes, far, rest, courant, slope_one, slope_two, kept_a, kept_b, kept_c,
    hbm_first, hbm_second, hbm_third, pick, place, place_far, quality, chan_weight, own_mats,
    hbm_out, hbm_sent, hbm_codes, over,
    table, mats, cells_b, mid_b, mid_f, last_b, one_b, two_b, w_first, w_second, w_third, out, sent, far_codes, sem,
    rest_b,
):
    rows, lon = 4, own_f.shape[0]
    cells = rows * lon
    sign = sign_of(flip)
    capacity = far.shape[0] - codes.shape[0]
    loads = [
        pltpu.make_async_copy(hbm_first, w_first, sem.at[0]),
        pltpu.make_async_copy(hbm_second, w_second, sem.at[1]),
        pltpu.make_async_copy(hbm_third, w_third, sem.at[2]),
    ]
    for copy in loads:
        copy.start()
    table[...] = jnp.zeros_like(table)
    far_codes[...] = far[capacity:, 0:lon].astype(F32)
    store_sources(table, 0, far_codes[...], True, sign, lon, rows)
    store_sources(table, 1, codes[...], False, sign, lon, rows)
    turned = table[...].T
    keep_codes = pltpu.make_async_copy(far_codes, hbm_codes, sem.at[3])
    keep_codes.start()
    chosen = [None] * 8
    for k, (step, half) in enumerate(OWN_BLOCKS):
        chosen[2 * step + half] = own_mats.at[k]
    for k, (step, half) in enumerate(FAR_BLOCKS):
        pull_matrix(mats.at[k], turned, step, step + 1 + 2 * half, lon, rows)
        chosen[2 * step + half] = mats.at[k]
    where, _ = slot_of(far[capacity:, lon : 2 * lon].astype(F32)[0:8])
    where = turn(where)
    most = jnp.maximum(jnp.max(far[capacity:, 2 * lon : 3 * lon].astype(F32)), jnp.where(jnp.max(slots[...]) >= float(capacity), 1.0, 0.0))
    over[0] = jnp.where(most > 0.0, linked[0], 0)
    for j in range(rows):
        value = dot(spread_matrix(where, j, capacity), far[0:capacity, :])
        cells_b[(rows - 1 - j) * lon : (rows - j) * lon, :] = value.astype(BF16)
    cells_b[cells:, :] = own_b[...]

    if redo:
        copy = pltpu.make_async_copy(rest, rest_b, sem.at[5])
        copy.start()
        copy.wait()
        for j in range(rows):
            value = dot(spread_matrix(where, j, rest_b.shape[0], capacity), rest_b[...])
            at = slice((rows - 1 - j) * lon, (rows - j) * lon)
            cells_b[at, :] = (cells_b[at, :].astype(F32) + value).astype(BF16)

    def start_f(at, size):
        pieces = []
        for row in range(at // lon, (at + size) // lon):
            if row == rows:
                pieces.append(own_f[...])
            else:
                pieces.append(cells_b[row * lon : (row + 1) * lon, :].astype(F32))
        return jnp.concatenate(pieces, axis=0)

    def finish(half, value):
        last_b[2 * half * lon : 2 * (half + 1) * lon, :] = value.astype(BF16)

    far_steps(
        chosen, lambda at, size: cells_b[at : at + size, :], start_f, courant,
        (kept_a, kept_b, kept_c), mid_b, mid_f, lon, finish,
    )
    one_b[...] = dot(pick[...], last_b[...]).astype(BF16)
    loads[0].wait()
    two_b[...] = (slope_one[...] * dot(one_b[...], w_first[...])).astype(BF16)
    loads[1].wait()
    one_b[...] = (slope_two[...] * dot(two_b[...], w_second[...])).astype(BF16)
    loads[2].wait()
    scale = quality[...] * chan_weight[0:1, :]
    two_b[...] = (scale * dot(one_b[...], w_third[...])).astype(BF16)
    one_b[...] = (slope_two[...] * dot_t(two_b[...], w_third[...])).astype(BF16)
    two_b[...] = (slope_one[...] * dot_t(one_b[...], w_second[...])).astype(BF16)
    one_b[...] = dot_t(two_b[...], w_first[...]).astype(BF16)
    sent[...] = dot(place_far[...], one_b[...]).astype(BF16)
    keep_sent = pltpu.make_async_copy(sent, hbm_sent, sem.at[4])
    keep_sent.start()
    out[...] = dot(place[...], one_b[...]).astype(BF16)
    keep_out = pltpu.make_async_copy(out, hbm_out, sem.at[0])
    keep_out.start()
    keep_codes.wait()
    keep_sent.wait()
    keep_out.wait()


def near_adjoint_kernel(
    flip, rest, cells_own, cells_near, codes, near_codes, far_codes, far_slots, courant,
    kept_a, kept_b, kept_c, far_mats, spread,
    table, mats, cells_b, mid_b, mid_f,
):
    rows, lon = 4, table.shape[1]
    cells = rows * lon
    sign = sign_of(flip)
    store_sources(table, 0, far_codes[...], True, sign, lon, rows)
    store_sources(table, 1, codes[...], False, sign, lon, rows)
    store_sources(table, 2, near_codes[...], True, sign, lon, rows)
    k = 0
    for order, exts in enumerate(((5, 7, 9), (6, 8), (7,))):
        for ext in exts:
            push_matrix(mats.at[k], table, 3 - order, ext, lon, rows)
            k += 1
    cells_b[0:cells, :] = cells_own[...]
    for j in range(rows):
        cells_b[(rows + j) * lon : (rows + j + 1) * lon, :] = cells_near[
            (rows - 1 - j) * lon : (rows - j) * lon, :
        ]

    def advect(cs):
        near_steps(
            mats, lambda at, size: cells_b[at : at + size, cs],
            lambda at, size: cells_b[at : at + size, cs].astype(F32), courant,
            (kept_a, kept_b, kept_c), mid_b, mid_f, lon, cs,
        )

    by_parts(cells_own.shape[1], advect)
    for order in range(4):
        for half in range(2):
            push_matrix(far_mats.at[2 * order + half], table, 3 - order, order + 1 + 2 * half, lon, rows)
    where = turn(far_slots[...])
    capacity = spread.shape[1]
    for j in range(rows):
        spread[j * lon : (j + 1) * lon, :] = spread_matrix(where, j, capacity)


def far_adjoint_kernel(
    flip, flag, cells_own, far, rest, courant, kept_a, kept_b, kept_c, mats, spread, far_slots,
    out,
    cells_b, mid_b, mid_f, result, rest_b, sem,
):
    rows, lon = out.shape[0], out.shape[1]
    cells = rows * lon
    for j in range(rows):
        value = dot(spread[j * lon : (j + 1) * lon, :], far[...])
        cells_b[(rows - 1 - j) * lon : (rows - j) * lon, :] = value.astype(BF16)
    cells_b[cells:, :] = cells_own[0 : 2 * lon, :]

    @pl.when(flag[0] > 0)
    def _():
        copy = pltpu.make_async_copy(rest, rest_b, sem.at[rows])
        copy.start()
        copy.wait()
        where = turn(far_slots[...])
        for j in range(rows):
            value = dot(spread_matrix(where, j, rest_b.shape[0], spread.shape[1]), rest_b[...])
            at = slice((rows - 1 - j) * lon, (rows - j) * lon)
            cells_b[at, :] = (cells_b[at, :].astype(F32) + value).astype(BF16)

    copies = []

    def finish(half, value):
        for part in range(2):
            j = 2 * half + part
            result[j] = value[part * lon : (part + 1) * lon, :]
            at = jnp.where(flip[0] == 1, rows - 1 - j, j)
            copies.append(pltpu.make_async_copy(result.at[j], out.at[at], sem.at[j]))
            copies[-1].start()

    far_steps(
        [mats.at[k] for k in range(8)], lambda at, size: cells_b[at : at + size, :],
        lambda at, size: cells_b[at : at + size, :].astype(F32), courant,
        (kept_a, kept_b, kept_c), mid_b, mid_f, lon, finish,
    )
    for copy in copies:
        copy.wait()


def params():
    return pltpu.CompilerParams(vmem_limit_bytes=VMEM_LIMIT)


def shape(dims, dtype):
    return jax.ShapeDtypeStruct(dims, dtype)


def send_rest(first, slots, dense, size, links):
    rest = pl.pallas_call(
        functools.partial(rest_kernel, first),
        out_shape=shape((size, dense.shape[1]), BF16),
        in_specs=[VMEM, VMEM],
        out_specs=VMEM,
        name="rest",
    )(slots, dense)
    return lax.ppermute(rest, "lat", links)


def blank(outs):
    return pl.pallas_call(blank_kernel, out_shape=outs, out_specs=[ANY] * len(outs), name="blank")()


def local(
    tangent,
    wind_code,
    courant,
    obs_index,
    obs_count,
    obs_quality,
    background,
    w_first,
    w_second,
    w_third,
    chan_weight,
):
    rows, lon, levels = tangent.shape
    cells = rows * lon
    head = wind_code.shape[0] * rows
    listed = obs_index.shape[1]
    hidden_size = w_first.shape[1]
    count = lax.axis_size("lat")
    here = lax.axis_index("lat")
    odd = (here % 2).astype(jnp.int32)
    flip = odd.reshape(1)
    linked = ((here > 0) & (here < count - 1)).astype(jnp.int32).reshape(1)
    pairs = [(i, i ^ 1) for i in range(count)]
    links = [(i, i + 1) for i in range(1, count - 1, 2)]
    links = links + [(b, a) for a, b in links]

    own, sent, codes, slots = pl.pallas_call(
        pack_kernel,
        out_shape=[
            shape((cells + head, levels), BF16),
            shape((FAR_CELLS + head, levels), BF16),
            shape((head, lon), F32),
            shape((8, lon), F32),
        ],
        in_specs=[SMEM, HBM, HBM],
        out_specs=[VMEM] * 4,
        scratch_shapes=[
            pltpu.VMEM((rows, lon, levels), F32),
            pltpu.VMEM(wind_code.shape, jnp.int32),
            pltpu.SemaphoreType.DMA((rows + 1,)),
        ],
        compiler_params=pltpu.CompilerParams(vmem_limit_bytes=PACK_LIMIT),
        name="pack",
    )(flip, tangent, wind_code)

    far = lax.ppermute(sent, "lat", links)
    near = lax.ppermute(own, "lat", pairs)

    c_row = courant.reshape(1, levels)
    kept_shape = [shape((2 * lon, levels), F32)] * 3
    slope_shape = shape((listed, hidden_size), F32)

    def run_near():
        return pl.pallas_call(
            near_kernel,
            out_shape=[slope_shape, slope_shape]
            + kept_shape
            + [
                shape((listed, cells), BF16),
                shape((cells, listed), BF16),
                shape((FAR_COLUMNS, listed), BF16),
                shape((head, lon), F32),
                shape((listed, 1), F32),
                shape((8, lon), F32),
                shape((4, 2 * lon, 4 * lon), BF16),
                shape((lon, levels), F32),
                shape((2 * lon, levels), BF16),
            ],
            in_specs=[SMEM, SMEM] + [VMEM] * 9,
            out_specs=[VMEM] * 14,
            scratch_shapes=[
                pltpu.VMEM((lon, lon), F32),
                pltpu.VMEM((6, 2 * lon, 4 * lon), BF16),
                pltpu.VMEM((2 * cells, levels), BF16),
                pltpu.VMEM((2, 6 * lon, PART), BF16),
                pltpu.VMEM((2, 6 * lon, PART), F32),
                pltpu.VMEM((listed, hidden_size), BF16),
            ],
            compiler_params=params(),
            cost_estimate=pl.CostEstimate(flops=4_000_000_000, bytes_accessed=16_000_000, transcendentals=1_000_000),
            name="near",
        )(
            flip, obs_count, tangent, codes, near, c_row, background[0], w_first, w_second, obs_index, obs_quality,
        )

    column_shape = [pltpu.HBM((cells, levels), BF16), pltpu.HBM((FAR_COLUMNS, levels), BF16)]

    def run_observe(redo, parts, rest):
        slope_one, slope_two, kept_a, kept_b, kept_c, pick, place, place_far = parts[:8]
        quality, _, own_mats, own_f, own_b = parts[9:]
        rest_specs = [ANY] if redo else []
        body = functools.partial(observe_kernel, redo)
        rest_args = [rest] if redo else []
        rest_scratch = [pltpu.VMEM((cells - FAR_CELLS, levels), BF16)]

        def kernel(*refs):
            refs = list(refs)
            if not redo:
                refs.insert(7, None)
                refs.append(None)
            body(*refs)

        return pl.pallas_call(
            kernel,
            out_shape=column_shape + [pltpu.HBM((head, lon), F32), shape((1,), jnp.int32)],
            in_specs=[SMEM, SMEM] + [VMEM] * 5 + rest_specs + [VMEM] * 6 + [ANY] * 3 + [VMEM] * 6,
            out_specs=[HBM] * 3 + [SMEM],
            scratch_shapes=[
                pltpu.VMEM((lon, lon), F32),
                pltpu.VMEM((4, 2 * lon, 4 * lon), BF16),
                pltpu.VMEM((6 * lon, levels), BF16),
                pltpu.VMEM((2, 6 * lon, levels), BF16),
                pltpu.VMEM((2, 6 * lon, levels), F32),
                pltpu.VMEM((cells, levels), BF16),
                pltpu.VMEM((listed, levels), BF16),
                pltpu.VMEM((listed, levels), BF16),
                pltpu.VMEM(w_first.shape, BF16),
                pltpu.VMEM(w_second.shape, BF16),
                pltpu.VMEM(w_third.shape, BF16),
                pltpu.VMEM((cells, levels), BF16),
                pltpu.VMEM((FAR_COLUMNS, levels), BF16),
                pltpu.VMEM((head, lon), F32),
                pltpu.SemaphoreType.DMA((6,)),
            ]
            + (rest_scratch if redo else []),
            compiler_params=params(),
            name="observe",
        )(
            flip, linked, slots, own_f, own_b, codes, far, *rest_args, c_row,
            slope_one, slope_two, kept_a, kept_b, kept_c, w_first, w_second, w_third,
            pick, place, place_far, quality, chan_weight.reshape(1, -1), own_mats,
        )

    parts = run_near()
    near_codes, own_slots = parts[8], parts[10]
    cells_own, sent, far_codes, over = run_observe(False, parts, None)

    def observe_again():
        rest = send_rest(FAR_CELLS, slots, own, cells - FAR_CELLS, links)
        return run_observe(True, run_near(), rest)[:2]

    redone = lax.cond(over[0] > 0, observe_again, lambda: blank(column_shape))
    cells_own, sent = pl.pallas_call(
        choose_kernel,
        out_shape=column_shape,
        in_specs=[SMEM] + [HBM] * 4,
        out_specs=[HBM] * 2,
        scratch_shapes=[pltpu.SemaphoreType.DMA((2,))],
        input_output_aliases={1: 0, 2: 1},
        name="choose",
    )(over, cells_own, sent, *redone)

    columns_far = lax.ppermute(sent, "lat", links)
    cells_near = lax.ppermute(cells_own, "lat", pairs)

    far_slots, over = pl.pallas_call(
        reach_kernel,
        out_shape=[shape((8, lon), F32), shape((1,), jnp.int32)],
        in_specs=[SMEM, SMEM, VMEM, VMEM],
        out_specs=[VMEM, SMEM],
        name="reach",
    )(flip, linked, own_slots, far_codes)
    left = cells - FAR_COLUMNS
    rest = lax.cond(
        over[0] > 0,
        lambda: send_rest(FAR_COLUMNS, own_slots, cells_own, left, links),
        lambda: blank([shape((left, levels), BF16)])[0],
    )
    kept_a, kept_b, kept_c, mats, spread = pl.pallas_call(
        near_adjoint_kernel,
        out_shape=kept_shape
        + [
            shape((8, 2 * lon, 4 * lon), BF16),
            shape((cells, FAR_COLUMNS), BF16),
        ],
        in_specs=[SMEM, ANY] + [VMEM] * 7,
        out_specs=[VMEM] * 5,
        scratch_shapes=[
            pltpu.VMEM((lon, lon), F32),
            pltpu.VMEM((6, 2 * lon, 4 * lon), BF16),
            pltpu.VMEM((2 * cells, levels), BF16),
            pltpu.VMEM((2, 6 * lon, PART), BF16),
            pltpu.VMEM((2, 6 * lon, PART), F32),
        ],
        compiler_params=params(),
        cost_estimate=pl.CostEstimate(flops=2_000_000_000, bytes_accessed=8_000_000, transcendentals=0),
        name="near_adjoint",
    )(flip, rest, cells_own, cells_near, codes, near_codes, far_codes, far_slots, c_row)

    return pl.pallas_call(
        far_adjoint_kernel,
        out_shape=shape((rows, lon, levels), F32),
        in_specs=[SMEM, SMEM, VMEM, VMEM, ANY] + [VMEM] * 7,
        out_specs=HBM,
        scratch_shapes=[
            pltpu.VMEM((6 * lon, levels), BF16),
            pltpu.VMEM((2, 6 * lon, levels), BF16),
            pltpu.VMEM((2, 6 * lon, levels), F32),
            pltpu.VMEM((rows, lon, levels), F32),
            pltpu.VMEM((cells - FAR_COLUMNS, levels), BF16),
            pltpu.SemaphoreType.DMA((rows + 1,)),
        ],
        compiler_params=params(),
        name="far_adjoint",
    )(
        flip, over, cells_own, columns_far, rest, c_row,
        kept_a, kept_b, kept_c, mats, spread, far_slots,
    )


def solution(mesh):
    placed = (
        P(("groups", "lat"), None, None),
        P(None, ("groups", "lat"), None),
        P(),
        P(("groups", "lat"), None),
        P(("groups", "lat")),
        P(("groups", "lat"), None),
        P(("groups", "lat"), None, None),
        P(),
        P(),
        P(),
        P(),
    )
    return jax.shard_map(
        local,
        mesh=mesh,
        in_specs=placed,
        out_specs=P(("groups", "lat"), None, None),
        check_vma=False,
    )
```

```python
import functools

import jax
import jax.numpy as jnp
from jax import lax
from jax.experimental import pallas as pl
from jax.experimental.pallas import tpu as pltpu
from jax.sharding import PartitionSpec as P

F32 = jnp.float32
BF16 = jnp.bfloat16
PART = 512
FAR_CELLS = 304
FAR_COLUMNS = 256
ANY = pl.BlockSpec(memory_space=pl.ANY)
VMEM = pl.BlockSpec(memory_space=pltpu.VMEM)
HBM = pl.BlockSpec(memory_space=pltpu.HBM)
SMEM = pl.BlockSpec(memory_space=pltpu.SMEM)
VMEM_LIMIT = 32 * 1024 * 1024
PACK_LIMIT = 60 * 1024 * 1024

OWN_BLOCKS = ((1, 1), (2, 1), (3, 0), (3, 1))
FAR_BLOCKS = ((0, 0), (0, 1), (1, 0), (2, 0))


def dot_t(left, right):
    return lax.dot_general(left, right, (((1,), (1,)), ((), ())), preferred_element_type=F32)


def dot(left, right):
    return jnp.dot(left, right, preferred_element_type=F32)


def store_sources(table, slot, codes, mirrored, sign, lon, rows):
    code = codes.astype(F32) - 1.0
    lat_q = jnp.where(code >= 5.0, 1.0, 0.0) + jnp.where(code >= 10.0, 1.0, 0.0)
    lon_step = code - 5.0 * lat_q - 2.0
    col = lax.broadcasted_iota(jnp.int32, code.shape, 1).astype(F32) - lon_step
    col = jnp.where(col < 0.0, col + lon, jnp.where(col >= lon, col - lon, col))
    stored = lax.broadcasted_iota(jnp.int32, code.shape, 0) & (rows - 1)
    row = (rows - 1 - stored) if mirrored else stored
    row = (row + slot * rows).astype(F32)
    src = (row - sign * (lat_q - 1.0)) * lon + col
    table[slot * code.shape[0] : (slot + 1) * code.shape[0], :] = jnp.where(code < 0.0, -65536.0, src)


def table_row(step, ext, rows):
    slot, at = ext // rows, ext % rows
    return slot * rows * rows + step * rows + (at if slot == 1 else rows - 1 - at)


def pull_matrix(out, turned, step, ext, lon, rows):
    span = 4 * lon
    lanes = lax.broadcasted_iota(jnp.int32, (lon, span), 1).astype(F32) + float((ext - 1) * lon)
    for half in range(2):
        k = table_row(step, ext + half, rows)
        column = turned[:, k : k + 1]
        out[half * lon : (half + 1) * lon, :] = jnp.where(column == lanes, 1.0, 0.0).astype(BF16)


def push_matrix(out, table, step, ext, lon, rows):
    dest = lax.broadcasted_iota(jnp.int32, (2 * lon, lon), 0).astype(F32) + float(ext * lon)
    for part in range(4):
        k = table_row(step, ext - 1 + part, rows)
        line = table[k : k + 1, :]
        out[:, part * lon : (part + 1) * lon] = jnp.where(line == dest, 1.0, 0.0).astype(BF16)


def wind_fields(codes, sign, rows):
    code = codes.astype(F32) - 1.0
    lat_q = jnp.where(code >= 5.0, 1.0, 0.0) + jnp.where(code >= 10.0, 1.0, 0.0)
    lat = jnp.where(code < 0.0, 9.0, sign * (lat_q - 1.0))
    lon = code - 5.0 * lat_q - 2.0
    fill = jnp.full((8 - rows, code.shape[1]), 9.0, F32)
    fields = []
    for step in range(code.shape[0] // rows):
        at = slice(step * rows, (step + 1) * rows)
        fields.append((jnp.concatenate([lat[at], fill], axis=0), jnp.concatenate([lon[at], fill], axis=0)))
    return fields


def shift_rows(mask, by):
    blank = jnp.zeros((1, mask.shape[1]), F32)
    if by == 1:
        return jnp.concatenate([blank, mask[:-1]], axis=0)
    if by == -1:
        return jnp.concatenate([mask[1:], blank], axis=0)
    return mask


def cells_pulled(fields, rows):
    lon = fields[0][0].shape[1]
    row = lax.broadcasted_iota(jnp.int32, (8, lon), 0)
    mask = jnp.where(row == 0, 1.0, 0.0)
    for lat, east in reversed(fields[: len(fields) - 1]):
        new = mask
        for a in (-1, 0, 1):
            total = jnp.zeros_like(mask)
            for b in range(-2, 3):
                hit = jnp.where((lat == float(a)) & (east == float(b)), mask, 0.0)
                total = jnp.maximum(total, hit if b == 0 else pltpu.roll(hit, (-b) % lon, 1))
            new = jnp.maximum(new, shift_rows(total, -a))
        mask = jnp.where(row < rows, new, 0.0)
    return mask


def cells_reached(fields, rows):
    lon = fields[0][0].shape[1]
    row = lax.broadcasted_iota(jnp.int32, (8, lon), 0)
    mask = jnp.zeros((8, lon), F32)
    for lat, east in fields:
        new = mask
        for a in (-1, 0, 1):
            source = shift_rows(mask, a)
            if a == 1:
                source = jnp.where(row == 0, 1.0, source)
            for b in range(-2, 3):
                seen = source if b == 0 else pltpu.roll(source, b % lon, 1)
                new = jnp.maximum(new, jnp.where((lat == float(a)) & (east == float(b)), seen, 0.0))
        mask = jnp.where(row < rows, new, 0.0)
    return mask


def slot_of(mask):
    lon = mask.shape[1]
    before = lax.broadcasted_iota(jnp.int32, (lon, lon), 0) < lax.broadcasted_iota(jnp.int32, (lon, lon), 1)
    place = dot(mask.astype(BF16), jnp.where(before, 1.0, 0.0).astype(BF16))
    totals = jnp.sum(mask, axis=1, keepdims=True)
    ahead = jnp.zeros((1, 1), F32)
    lines = []
    for j in range(mask.shape[0]):
        lines.append(place[j : j + 1] + ahead)
        ahead = ahead + totals[j : j + 1]
    return jnp.where(mask > 0.0, jnp.concatenate(lines, axis=0), -1.0), ahead


def choose_matrix(slots, size, rows, first=0):
    lon = slots.shape[1]
    at = lax.broadcasted_iota(jnp.int32, (size, lon), 0).astype(F32) + float(first)
    parts = [jnp.where(slots[j : j + 1] == at, 1.0, 0.0) for j in range(rows)]
    return jnp.concatenate(parts, axis=1).astype(BF16)


def spread_matrix(turned, row, size, first=0):
    at = lax.broadcasted_iota(jnp.int32, (turned.shape[0], size), 1).astype(F32) + float(first)
    return jnp.where(turned[:, row : row + 1] == at, 1.0, 0.0).astype(BF16)


def turn(slots):
    lon = slots.shape[1]
    return jnp.concatenate([slots, jnp.full((lon - slots.shape[0], lon), -1.0, F32)], axis=0).T


def sign_of(flip):
    return jnp.where(flip[0] == 1, -1.0, 1.0)


def pack_kernel(flip, tangent, wind, own, sent, codes, slots, buf, wind_b, sem):
    rows, lon = tangent.shape[0], tangent.shape[1]
    cells = rows * lon
    wind_copy = pltpu.make_async_copy(wind, wind_b, sem.at[rows])
    wind_copy.start()
    copies = []
    for j in range(rows):
        at = jnp.where(flip[0] == 1, rows - 1 - j, j)
        copies.append(pltpu.make_async_copy(tangent.at[at], buf.at[j], sem.at[j]))
        copies[-1].start()
    wind_copy.wait()
    for step in range(wind_b.shape[0]):
        for j in range(rows):
            code = jnp.where(flip[0] == 1, wind_b[step, rows - 1 - j : rows - j, :], wind_b[step, j : j + 1, :])
            codes[step * rows + j : step * rows + j + 1, :] = code.astype(F32) + 1.0
    mask = cells_pulled(wind_fields(codes[...], sign_of(flip), rows), rows)
    where, total = slot_of(mask)
    slots[...] = where
    head = codes.shape[0]
    capacity = sent.shape[0] - head
    tall = jnp.concatenate([mask, jnp.zeros((head - mask.shape[0], lon), F32)], axis=0)
    flag = jnp.broadcast_to(jnp.where(total > float(capacity), 1.0, 0.0), (head, lon))
    notes = jnp.concatenate([codes[...], tall, flag, jnp.zeros((head, own.shape[1] - 3 * lon), F32)], axis=1)
    notes = notes.astype(BF16)
    own[cells:, :] = notes
    sent[capacity:, :] = notes
    choose = choose_matrix(where, capacity, rows)
    for j in range(rows):
        copies[j].wait()
        own[j * lon : (j + 1) * lon, :] = buf[j].astype(BF16)
    sent[0:capacity, :] = dot(choose, own[0:cells, :]).astype(BF16)


def choose_kernel(flag, *refs):
    count = len(refs) // 3
    redone, outs, sem = refs[count : 2 * count], refs[2 * count : 3 * count], refs[-1]

    @pl.when(flag[0] > 0)
    def _():
        copies = [pltpu.make_async_copy(redone[k], outs[k], sem.at[k]) for k in range(count)]
        for copy in copies:
            copy.start()
        for copy in copies:
            copy.wait()


def rest_kernel(first, slots, dense, out):
    rows = dense.shape[0] // slots.shape[1]
    cells = rows * slots.shape[1]
    choose = choose_matrix(slots[...], out.shape[0], rows, first)
    out[...] = dot(choose, dense[0:cells, :]).astype(BF16)


def blank_kernel(*outs):
    pass


def near_steps(mats, start_b, start_f, c_ref, outs, mid_b, mid_f, lon, cs):
    c = c_ref[0:1, cs]
    blocks = ((5, 7, 9), (6, 8), (7,))
    read_b, read_f, first = start_b, start_f, 4
    k = 0
    for step, exts in enumerate(blocks):
        for ext in exts:
            at = (ext - 1 - first) * lon
            pulled = dot(mats[k], read_b(at, 4 * lon))
            value = (1.0 - c) * read_f(at + lon, 2 * lon) + c * pulled
            k += 1
            if ext == exts[0]:
                outs[step][:, cs] = value
            if step < 2:
                to = (ext - exts[0]) * lon
                mid_f[step, to : to + 2 * lon, :] = value
                mid_b[step, to : to + 2 * lon, :] = value.astype(BF16)
        first = exts[0]
        read_b = functools.partial(lambda s, a, n: mid_b[s, a : a + n, :], step)
        read_f = functools.partial(lambda s, a, n: mid_f[s, a : a + n, :], step)


def by_parts(levels, body):
    @pl.loop(0, levels // PART)
    def _(i):
        body(pl.ds(pl.multiple_of(i * PART, PART), PART))


def far_steps(mats, start_b, start_f, c_ref, kept, mid_b, mid_f, lon, finish):
    c = c_ref[0:1, :]
    k = 0
    for step in range(4):
        now, last = step % 2, (step + 1) % 2
        for half in range(2):
            at = 2 * half * lon
            if step == 0:
                window, own = start_b(at, 4 * lon), start_f(at + lon, 2 * lon)
            else:
                window = mid_b[last, at : at + 4 * lon, :]
                own = mid_f[last, at + lon : at + 3 * lon, :]
            value = (1.0 - c) * own + c * dot(mats[k][...], window)
            k += 1
            if step < 3:
                mid_f[now, at : at + 2 * lon, :] = value
                mid_b[now, at : at + 2 * lon, :] = value.astype(BF16)
            else:
                finish(half, value)
        if step < 3:
            carried = kept[step][...]
            mid_f[now, 4 * lon :, :] = carried
            mid_b[now, 4 * lon :, :] = carried.astype(BF16)


def near_kernel(
    flip, obs_count, tangent, codes, near, courant, background, w_first, w_second, obs_index, obs_quality,
    slope_one, slope_two, kept_a, kept_b, kept_c, pick, place, place_far, near_codes, quality, slots, own_mats, own_f, own_b,
    table, mats, cells_b, mid_b, mid_f, hidden,
):
    rows, lon = tangent.shape[0], tangent.shape[1]
    cells = rows * lon
    sign = sign_of(flip)
    table[...] = jnp.zeros_like(table)
    near_codes[...] = near[cells:, 0:lon].astype(F32)
    store_sources(table, 1, codes[...], False, sign, lon, rows)
    store_sources(table, 2, near_codes[...], True, sign, lon, rows)
    turned = table[...].T
    k = 0
    for step, exts in enumerate(((5, 7, 9), (6, 8), (7,))):
        for ext in exts:
            pull_matrix(mats.at[k], turned, step, ext, lon, rows)
            k += 1
    for k, (step, half) in enumerate(OWN_BLOCKS):
        pull_matrix(own_mats.at[k], turned, step, step + 1 + 2 * half, lon, rows)
    for j in range(rows):
        row = tangent[jnp.where(flip[0] == 1, rows - 1 - j, j)]
        cells_b[j * lon : (j + 1) * lon, :] = row.astype(BF16)
        cells_b[(rows + j) * lon : (rows + j + 1) * lon, :] = near[(rows - 1 - j) * lon : (rows - j) * lon, :]

    own_f[...] = tangent[jnp.where(flip[0] == 1, rows - 1, 0)]
    own_b[...] = cells_b[0 : 2 * lon, :]

    def advect(cs):
        def start_f(at, size):
            pieces = []
            for row in range(at // lon, (at + size) // lon):
                if row < rows:
                    pieces.append(tangent[jnp.where(flip[0] == 1, rows - 1 - row, row), :, cs])
                else:
                    pieces.append(cells_b[row * lon : (row + 1) * lon, cs].astype(F32))
            return jnp.concatenate(pieces, axis=0)

        near_steps(
            mats, lambda at, size: cells_b[at : at + size, cs], start_f, courant,
            (kept_a, kept_b, kept_c), mid_b, mid_f, lon, cs,
        )

    by_parts(tangent.shape[2], advect)

    def first_layer(cs):
        first_tanh = jnp.tanh(dot(background[...], w_first[:, cs]))
        hidden[:, cs] = first_tanh.astype(BF16)
        slope_one[:, cs] = 1.0 - first_tanh * first_tanh

    by_parts(w_first.shape[1], first_layer)

    def second_layer(cs):
        second_tanh = jnp.tanh(dot(hidden[...], w_second[:, cs]))
        slope_two[:, cs] = 1.0 - second_tanh * second_tanh

    by_parts(w_second.shape[1], second_layer)

    count = obs_index.shape[1]
    at = obs_index[...]
    at = jnp.where(flip[0] == 1, at + (rows - 1 - 2 * lax.div(at, lon)) * lon, at)
    live = lax.broadcasted_iota(jnp.int32, at.shape, 1) < obs_count[0]
    at = jnp.where(live, at, -1)
    chosen = at == lax.broadcasted_iota(jnp.int32, (cells, count), 0)
    place[...] = jnp.where(chosen, 1.0, 0.0).astype(BF16)
    lines = jnp.concatenate([at.astype(F32), jnp.where(live, obs_quality[...].astype(F32), 0.0)], axis=0)
    lines = jnp.concatenate([lines, jnp.zeros((6, count), F32)], axis=0)
    lines = jnp.concatenate([lines, jnp.zeros((8, cells - count), F32)], axis=1).T
    quality[...] = lines[0:count, 1:2]
    columns = lax.broadcasted_iota(jnp.int32, (count, cells), 1).astype(F32)
    pick[...] = jnp.where(lines[0:count, 0:1] == columns, 1.0, 0.0).astype(BF16)
    where, _ = slot_of(cells_reached(wind_fields(codes[...], sign, rows), rows))
    slots[...] = where
    place_far[...] = dot(choose_matrix(slots[...], place_far.shape[0], rows), place[...]).astype(BF16)


def observe_kernel(
    redo, flip, linked, slots, own_f, own_b, codes, far, rest, courant, slope_one, slope_two, kept_a, kept_b, kept_c,
    hbm_first, hbm_second, hbm_third, pick, place, place_far, quality, chan_weight, own_mats, own_slots,
    hbm_out, hbm_low, hbm_high, hbm_codes, hbm_slots, over, over_columns,
    table, mats, cells_b, mid_b, mid_f, last_b, one_b, two_b, w_first, w_second, w_third, out, low, high, far_codes, far_slots, sem,
    rest_b,
):
    rows, lon = 4, own_f.shape[0]
    cells = rows * lon
    sign = sign_of(flip)
    capacity = far.shape[0] - codes.shape[0]
    loads = [
        pltpu.make_async_copy(hbm_first, w_first, sem.at[0]),
        pltpu.make_async_copy(hbm_second, w_second, sem.at[1]),
        pltpu.make_async_copy(hbm_third, w_third, sem.at[2]),
    ]
    for copy in loads:
        copy.start()
    table[...] = jnp.zeros_like(table)
    far_codes[...] = far[capacity:, 0:lon].astype(F32)
    store_sources(table, 0, far_codes[...], True, sign, lon, rows)
    store_sources(table, 1, codes[...], False, sign, lon, rows)
    turned = table[...].T
    keep_codes = pltpu.make_async_copy(far_codes, hbm_codes, sem.at[3])
    keep_codes.start()
    reached, total = slot_of(cells_reached(wind_fields(far_codes[...], -sign, rows), rows))
    far_slots[...] = reached
    keep_slots = pltpu.make_async_copy(far_slots, hbm_slots, sem.at[6])
    keep_slots.start()
    most = jnp.maximum(jnp.max(total), jnp.max(own_slots[...]) + 1.0)
    over_columns[0] = jnp.where(most > float(FAR_COLUMNS), linked[0], 0)
    chosen = [None] * 8
    for k, (step, half) in enumerate(OWN_BLOCKS):
        chosen[2 * step + half] = own_mats.at[k]
    for k, (step, half) in enumerate(FAR_BLOCKS):
        pull_matrix(mats.at[k], turned, step, step + 1 + 2 * half, lon, rows)
        chosen[2 * step + half] = mats.at[k]
    where, _ = slot_of(far[capacity:, lon : 2 * lon].astype(F32)[0:8])
    where = turn(where)
    most = jnp.maximum(jnp.max(far[capacity:, 2 * lon : 3 * lon].astype(F32)), jnp.where(jnp.max(slots[...]) >= float(capacity), 1.0, 0.0))
    over[0] = jnp.where(most > 0.0, linked[0], 0)
    for j in range(rows):
        value = dot(spread_matrix(where, j, capacity), far[0:capacity, :])
        cells_b[(rows - 1 - j) * lon : (rows - j) * lon, :] = value.astype(BF16)
    cells_b[cells:, :] = own_b[...]

    if redo:
        copy = pltpu.make_async_copy(rest, rest_b, sem.at[5])
        copy.start()
        copy.wait()
        for j in range(rows):
            value = dot(spread_matrix(where, j, rest_b.shape[0], capacity), rest_b[...])
            at = slice((rows - 1 - j) * lon, (rows - j) * lon)
            cells_b[at, :] = (cells_b[at, :].astype(F32) + value).astype(BF16)

    def start_f(at, size):
        pieces = []
        for row in range(at // lon, (at + size) // lon):
            if row == rows:
                pieces.append(own_f[...])
            else:
                pieces.append(cells_b[row * lon : (row + 1) * lon, :].astype(F32))
        return jnp.concatenate(pieces, axis=0)

    def finish(half, value):
        last_b[2 * half * lon : 2 * (half + 1) * lon, :] = value.astype(BF16)

    far_steps(
        chosen, lambda at, size: cells_b[at : at + size, :], start_f, courant,
        (kept_a, kept_b, kept_c), mid_b, mid_f, lon, finish,
    )
    one_b[...] = dot(pick[...], last_b[...]).astype(BF16)
    loads[0].wait()
    two_b[...] = (slope_one[...] * dot(one_b[...], w_first[...])).astype(BF16)
    loads[1].wait()
    one_b[...] = (slope_two[...] * dot(two_b[...], w_second[...])).astype(BF16)
    loads[2].wait()
    scale = quality[...] * chan_weight[0:1, :]
    two_b[...] = (scale * dot(one_b[...], w_third[...])).astype(BF16)
    one_b[...] = (slope_two[...] * dot_t(two_b[...], w_third[...])).astype(BF16)
    two_b[...] = (slope_one[...] * dot_t(one_b[...], w_second[...])).astype(BF16)
    one_b[...] = dot_t(two_b[...], w_first[...]).astype(BF16)
    half = low.shape[1]
    low[...] = dot(place_far[...], one_b[:, :half]).astype(BF16)
    keep_low = pltpu.make_async_copy(low, hbm_low, sem.at[4])
    keep_low.start()
    high[...] = dot(place_far[...], one_b[:, half:]).astype(BF16)
    keep_high = pltpu.make_async_copy(high, hbm_high, sem.at[1])
    keep_high.start()
    out[...] = dot(place[...], one_b[...]).astype(BF16)
    keep_out = pltpu.make_async_copy(out, hbm_out, sem.at[0])
    keep_out.start()
    keep_codes.wait()
    keep_slots.wait()
    keep_low.wait()
    keep_high.wait()
    keep_out.wait()


def near_adjoint_kernel(
    flip, rest, cells_own, cells_near, codes, near_codes, far_codes, far_slots, courant,
    kept_a, kept_b, kept_c, far_mats, spread,
    table, mats, cells_b, mid_b, mid_f, slots_b, codes_b, sem,
):
    rows, lon = 4, table.shape[1]
    cells = rows * lon
    own_copy = pltpu.make_async_copy(cells_own, cells_b.at[0:cells], sem.at[0])
    own_copy.start()
    slots_copy = pltpu.make_async_copy(far_slots, slots_b, sem.at[1])
    slots_copy.start()
    codes_copy = pltpu.make_async_copy(far_codes, codes_b, sem.at[2])
    codes_copy.start()
    codes_copy.wait()
    sign = sign_of(flip)
    store_sources(table, 0, codes_b[...], True, sign, lon, rows)
    store_sources(table, 1, codes[...], False, sign, lon, rows)
    store_sources(table, 2, near_codes[...], True, sign, lon, rows)
    k = 0
    for order, exts in enumerate(((5, 7, 9), (6, 8), (7,))):
        for ext in exts:
            push_matrix(mats.at[k], table, 3 - order, ext, lon, rows)
            k += 1
    for j in range(rows):
        cells_b[(rows + j) * lon : (rows + j + 1) * lon, :] = cells_near[
            (rows - 1 - j) * lon : (rows - j) * lon, :
        ]

    own_copy.wait()

    def advect(cs):
        near_steps(
            mats, lambda at, size: cells_b[at : at + size, cs],
            lambda at, size: cells_b[at : at + size, cs].astype(F32), courant,
            (kept_a, kept_b, kept_c), mid_b, mid_f, lon, cs,
        )

    advect(slice(None))
    for order in range(4):
        for half in range(2):
            push_matrix(far_mats.at[2 * order + half], table, 3 - order, order + 1 + 2 * half, lon, rows)
    slots_copy.wait()
    where = turn(slots_b[...])
    capacity = spread.shape[1]
    for j in range(rows):
        spread[j * lon : (j + 1) * lon, :] = spread_matrix(where, j, capacity)


def far_adjoint_kernel(
    part, flip, flag, cells_own, far, rest, courant, kept_a, kept_b, kept_c, mats, spread, far_slots, _given,
    out,
    cells_b, mid_b, mid_f, result, rest_b, slots_b, sem,
):
    rows, lon = out.shape[0], out.shape[1]
    cells = rows * lon
    width = far.shape[1]
    cs = slice(part * width, (part + 1) * width)
    for j in range(rows):
        value = dot(spread[j * lon : (j + 1) * lon, :], far[...])
        cells_b[(rows - 1 - j) * lon : (rows - j) * lon, :] = value.astype(BF16)
    cells_b[cells:, :] = cells_own[0 : 2 * lon, cs]

    @pl.when(flag[0] > 0)
    def _():
        fetches = [
            pltpu.make_async_copy(rest.at[:, cs], rest_b, sem.at[rows]),
            pltpu.make_async_copy(far_slots, slots_b, sem.at[rows + 1]),
        ]
        for copy in fetches:
            copy.start()
        for copy in fetches:
            copy.wait()
        where = turn(slots_b[...])
        for j in range(rows):
            value = dot(spread_matrix(where, j, rest_b.shape[0], spread.shape[1]), rest_b[...])
            at = slice((rows - 1 - j) * lon, (rows - j) * lon)
            cells_b[at, :] = (cells_b[at, :].astype(F32) + value).astype(BF16)

    copies = []

    def finish(half, value):
        for piece in range(2):
            j = 2 * half + piece
            result[j] = value[piece * lon : (piece + 1) * lon, :]
            at = jnp.where(flip[0] == 1, rows - 1 - j, j)
            copies.append(pltpu.make_async_copy(result.at[j], out.at[at, :, cs], sem.at[j]))
            copies[-1].start()

    far_steps(
        [mats.at[k] for k in range(8)], lambda at, size: cells_b[at : at + size, :],
        lambda at, size: cells_b[at : at + size, :].astype(F32), courant.at[:, cs],
        tuple(kept.at[:, cs] for kept in (kept_a, kept_b, kept_c)), mid_b, mid_f, lon, finish,
    )
    for copy in copies:
        copy.wait()


def params():
    return pltpu.CompilerParams(vmem_limit_bytes=VMEM_LIMIT)


def shape(dims, dtype):
    return jax.ShapeDtypeStruct(dims, dtype)


def send_rest(first, slots, dense, size, links):
    rest = pl.pallas_call(
        functools.partial(rest_kernel, first),
        out_shape=shape((size, dense.shape[1]), BF16),
        in_specs=[VMEM, VMEM],
        out_specs=VMEM,
        name="rest",
    )(slots, dense)
    return lax.ppermute(rest, "lat", links)


def blank(outs):
    return pl.pallas_call(blank_kernel, out_shape=outs, out_specs=[ANY] * len(outs), name="blank")()


def local(
    tangent,
    wind_code,
    courant,
    obs_index,
    obs_count,
    obs_quality,
    background,
    w_first,
    w_second,
    w_third,
    chan_weight,
):
    rows, lon, levels = tangent.shape
    cells = rows * lon
    head = wind_code.shape[0] * rows
    listed = obs_index.shape[1]
    hidden_size = w_first.shape[1]
    count = lax.axis_size("lat")
    here = lax.axis_index("lat")
    odd = (here % 2).astype(jnp.int32)
    flip = odd.reshape(1)
    linked = ((here > 0) & (here < count - 1)).astype(jnp.int32).reshape(1)
    pairs = [(i, i ^ 1) for i in range(count)]
    links = [(i, i + 1) for i in range(1, count - 1, 2)]
    links = links + [(b, a) for a, b in links]

    own, sent, codes, slots = pl.pallas_call(
        pack_kernel,
        out_shape=[
            shape((cells + head, levels), BF16),
            shape((FAR_CELLS + head, levels), BF16),
            shape((head, lon), F32),
            shape((8, lon), F32),
        ],
        in_specs=[SMEM, HBM, HBM],
        out_specs=[VMEM] * 4,
        scratch_shapes=[
            pltpu.VMEM((rows, lon, levels), F32),
            pltpu.VMEM(wind_code.shape, jnp.int32),
            pltpu.SemaphoreType.DMA((rows + 1,)),
        ],
        compiler_params=pltpu.CompilerParams(vmem_limit_bytes=PACK_LIMIT),
        name="pack",
    )(flip, tangent, wind_code)

    far = lax.ppermute(sent, "lat", links)
    near = lax.ppermute(own, "lat", pairs)

    c_row = courant.reshape(1, levels)
    kept_shape = [shape((2 * lon, levels), F32)] * 3
    slope_shape = shape((listed, hidden_size), F32)

    def run_near():
        return pl.pallas_call(
            near_kernel,
            out_shape=[slope_shape, slope_shape]
            + kept_shape
            + [
                shape((listed, cells), BF16),
                shape((cells, listed), BF16),
                shape((FAR_COLUMNS, listed), BF16),
                shape((head, lon), F32),
                shape((listed, 1), F32),
                shape((8, lon), F32),
                shape((4, 2 * lon, 4 * lon), BF16),
                shape((lon, levels), F32),
                shape((2 * lon, levels), BF16),
            ],
            in_specs=[SMEM, SMEM] + [VMEM] * 9,
            out_specs=[VMEM] * 14,
            scratch_shapes=[
                pltpu.VMEM((lon, lon), F32),
                pltpu.VMEM((6, 2 * lon, 4 * lon), BF16),
                pltpu.VMEM((2 * cells, levels), BF16),
                pltpu.VMEM((2, 6 * lon, PART), BF16),
                pltpu.VMEM((2, 6 * lon, PART), F32),
                pltpu.VMEM((listed, hidden_size), BF16),
            ],
            compiler_params=params(),
            cost_estimate=pl.CostEstimate(flops=4_000_000_000, bytes_accessed=16_000_000, transcendentals=1_000_000),
            name="near",
        )(
            flip, obs_count, tangent, codes, near, c_row, background[0], w_first, w_second, obs_index, obs_quality,
        )

    column_shape = [pltpu.HBM((cells, levels), BF16)] + [pltpu.HBM((FAR_COLUMNS, levels // 2), BF16)] * 2

    def run_observe(redo, parts, rest):
        slope_one, slope_two, kept_a, kept_b, kept_c, pick, place, place_far = parts[:8]
        quality, columns_list, own_mats, own_f, own_b = parts[9:]
        rest_specs = [ANY] if redo else []
        body = functools.partial(observe_kernel, redo)
        rest_args = [rest] if redo else []
        rest_scratch = [pltpu.VMEM((cells - FAR_CELLS, levels), BF16)]

        def kernel(*refs):
            refs = list(refs)
            if not redo:
                refs.insert(7, None)
                refs.append(None)
            body(*refs)

        return pl.pallas_call(
            kernel,
            out_shape=column_shape
            + [pltpu.HBM((head, lon), F32), pltpu.HBM((8, lon), F32)]
            + [shape((1,), jnp.int32)] * 2,
            in_specs=[SMEM, SMEM] + [VMEM] * 5 + rest_specs + [VMEM] * 6 + [ANY] * 3 + [VMEM] * 7,
            out_specs=[HBM] * 5 + [SMEM] * 2,
            scratch_shapes=[
                pltpu.VMEM((lon, lon), F32),
                pltpu.VMEM((4, 2 * lon, 4 * lon), BF16),
                pltpu.VMEM((6 * lon, levels), BF16),
                pltpu.VMEM((2, 6 * lon, levels), BF16),
                pltpu.VMEM((2, 6 * lon, levels), F32),
                pltpu.VMEM((cells, levels), BF16),
                pltpu.VMEM((listed, levels), BF16),
                pltpu.VMEM((listed, levels), BF16),
                pltpu.VMEM(w_first.shape, BF16),
                pltpu.VMEM(w_second.shape, BF16),
                pltpu.VMEM(w_third.shape, BF16),
                pltpu.VMEM((cells, levels), BF16),
                pltpu.VMEM((FAR_COLUMNS, levels // 2), BF16),
                pltpu.VMEM((FAR_COLUMNS, levels // 2), BF16),
                pltpu.VMEM((head, lon), F32),
                pltpu.VMEM((8, lon), F32),
                pltpu.SemaphoreType.DMA((7,)),
            ]
            + (rest_scratch if redo else []),
            compiler_params=params(),
            name="observe",
        )(
            flip, linked, slots, own_f, own_b, codes, far, *rest_args, c_row,
            slope_one, slope_two, kept_a, kept_b, kept_c, w_first, w_second, w_third,
            pick, place, place_far, quality, chan_weight.reshape(1, -1), own_mats, columns_list,
        )

    parts = run_near()
    near_codes, own_slots = parts[8], parts[10]
    cells_own, low, high, far_codes, far_slots, over, over_columns = run_observe(False, parts, None)

    def observe_again():
        rest = send_rest(FAR_CELLS, slots, own, cells - FAR_CELLS, links)
        return run_observe(True, run_near(), rest)[:3]

    redone = lax.cond(over[0] > 0, observe_again, lambda: blank(column_shape))
    cells_own, low, high = pl.pallas_call(
        choose_kernel,
        out_shape=column_shape,
        in_specs=[SMEM] + [HBM] * 6,
        out_specs=[HBM] * 3,
        scratch_shapes=[pltpu.SemaphoreType.DMA((3,))],
        input_output_aliases={1: 0, 2: 1, 3: 2},
        name="choose",
    )(over, cells_own, low, high, *redone)

    far_low = lax.ppermute(low, "lat", links)
    far_high = lax.ppermute(high, "lat", links)
    cells_near = lax.ppermute(cells_own, "lat", pairs)

    left = cells - FAR_COLUMNS
    rest = lax.cond(
        over_columns[0] > 0,
        lambda: send_rest(FAR_COLUMNS, own_slots, cells_own, left, links),
        lambda: blank([shape((left, levels), BF16)])[0],
    )
    kept_a, kept_b, kept_c, mats, spread = pl.pallas_call(
        near_adjoint_kernel,
        out_shape=kept_shape
        + [
            shape((8, 2 * lon, 4 * lon), BF16),
            shape((cells, FAR_COLUMNS), BF16),
        ],
        in_specs=[SMEM, ANY, ANY] + [VMEM] * 3 + [ANY, ANY, VMEM],
        out_specs=[VMEM] * 5,
        scratch_shapes=[
            pltpu.VMEM((lon, lon), F32),
            pltpu.VMEM((6, 2 * lon, 4 * lon), BF16),
            pltpu.VMEM((2 * cells, levels), BF16),
            pltpu.VMEM((2, 6 * lon, levels), BF16),
            pltpu.VMEM((2, 6 * lon, levels), F32),
            pltpu.VMEM((8, lon), F32),
            pltpu.VMEM((head, lon), F32),
            pltpu.SemaphoreType.DMA((3,)),
        ],
        compiler_params=params(),
        cost_estimate=pl.CostEstimate(flops=2_000_000_000, bytes_accessed=8_000_000, transcendentals=0),
        name="near_adjoint",
    )(flip, rest, cells_own, cells_near, codes, near_codes, far_codes, far_slots, c_row)

    width = levels // 2

    def finish(part, columns, given):
        body = functools.partial(far_adjoint_kernel, part)
        given_specs = [HBM] if part else []

        def kernel(*refs):
            refs = list(refs)
            if not part:
                refs.insert(12, None)
            body(*refs)

        return pl.pallas_call(
            kernel,
            out_shape=shape((rows, lon, levels), F32),
            in_specs=[SMEM, SMEM, VMEM, VMEM, ANY] + [VMEM] * 6 + [ANY] + given_specs,
            out_specs=HBM,
            scratch_shapes=[
                pltpu.VMEM((6 * lon, width), BF16),
                pltpu.VMEM((2, 6 * lon, width), BF16),
                pltpu.VMEM((2, 6 * lon, width), F32),
                pltpu.VMEM((rows, lon, width), F32),
                pltpu.VMEM((left, width), BF16),
                pltpu.VMEM((8, lon), F32),
                pltpu.SemaphoreType.DMA((rows + 2,)),
            ],
            input_output_aliases={12: 0} if part else {},
            compiler_params=params(),
            cost_estimate=pl.CostEstimate(flops=2_000_000_000, bytes_accessed=4_000_000, transcendentals=0),
            name="far_adjoint",
        )(
            flip, over_columns, cells_own, columns, rest, c_row, kept_a, kept_b, kept_c, mats, spread, far_slots, *given,
        )

    half_done = finish(0, far_low, [])
    return finish(1, far_high, [half_done])


def solution(mesh):
    placed = (
        P(("groups", "lat"), None, None),
        P(None, ("groups", "lat"), None),
        P(),
        P(("groups", "lat"), None),
        P(("groups", "lat")),
        P(("groups", "lat"), None),
        P(("groups", "lat"), None, None),
        P(),
        P(),
        P(),
        P(),
    )
    return jax.shard_map(
        local,
        mesh=mesh,
        in_specs=placed,
        out_specs=P(("groups", "lat"), None, None),
        check_vma=False,
    )
```

```python
import functools

import jax
import jax.numpy as jnp
from jax import lax
from jax.experimental import pallas as pl
from jax.experimental.pallas import tpu as pltpu
from jax.sharding import PartitionSpec as P

F32 = jnp.float32
BF16 = jnp.bfloat16
PART = 512
NOTE_ROWS = 8
FAR_CELLS = 296
FAR_COLUMNS = 256
ANY = pl.BlockSpec(memory_space=pl.ANY)
VMEM = pl.BlockSpec(memory_space=pltpu.VMEM)
HBM = pl.BlockSpec(memory_space=pltpu.HBM)
SMEM = pl.BlockSpec(memory_space=pltpu.SMEM)
VMEM_LIMIT = 32 * 1024 * 1024
PACK_LIMIT = 60 * 1024 * 1024

OWN_BLOCKS = ((1, 1), (2, 1), (3, 0), (3, 1))
FAR_BLOCKS = ((0, 0), (0, 1), (1, 0), (2, 0))


def dot_t(left, right):
    return lax.dot_general(left, right, (((1,), (1,)), ((), ())), preferred_element_type=F32)


def dot(left, right):
    return jnp.dot(left, right, preferred_element_type=F32)


def store_sources(table, slot, codes, mirrored, sign, lon, rows):
    code = codes.astype(F32) - 1.0
    lat_q = jnp.where(code >= 5.0, 1.0, 0.0) + jnp.where(code >= 10.0, 1.0, 0.0)
    lon_step = code - 5.0 * lat_q - 2.0
    col = lax.broadcasted_iota(jnp.int32, code.shape, 1).astype(F32) - lon_step
    col = jnp.where(col < 0.0, col + lon, jnp.where(col >= lon, col - lon, col))
    stored = lax.broadcasted_iota(jnp.int32, code.shape, 0) & (rows - 1)
    row = (rows - 1 - stored) if mirrored else stored
    row = (row + slot * rows).astype(F32)
    src = (row - sign * (lat_q - 1.0)) * lon + col
    table[slot * code.shape[0] : (slot + 1) * code.shape[0], :] = jnp.where(code < 0.0, -65536.0, src)


def table_row(step, ext, rows):
    slot, at = ext // rows, ext % rows
    return slot * rows * rows + step * rows + (at if slot == 1 else rows - 1 - at)


def pull_matrix(out, turned, step, ext, lon, rows):
    span = 4 * lon
    lanes = lax.broadcasted_iota(jnp.int32, (lon, span), 1).astype(F32) + float((ext - 1) * lon)
    for half in range(2):
        k = table_row(step, ext + half, rows)
        column = turned[:, k : k + 1]
        out[half * lon : (half + 1) * lon, :] = jnp.where(column == lanes, 1.0, 0.0).astype(BF16)


def push_matrix(out, table, step, ext, lon, rows):
    dest = lax.broadcasted_iota(jnp.int32, (2 * lon, lon), 0).astype(F32) + float(ext * lon)
    for part in range(4):
        k = table_row(step, ext - 1 + part, rows)
        line = table[k : k + 1, :]
        out[:, part * lon : (part + 1) * lon] = jnp.where(line == dest, 1.0, 0.0).astype(BF16)


def wind_fields(codes, sign, rows):
    code = codes.astype(F32) - 1.0
    lat_q = jnp.where(code >= 5.0, 1.0, 0.0) + jnp.where(code >= 10.0, 1.0, 0.0)
    lat = jnp.where(code < 0.0, 9.0, sign * (lat_q - 1.0))
    lon = code - 5.0 * lat_q - 2.0
    fill = jnp.full((8 - rows, code.shape[1]), 9.0, F32)
    fields = []
    for step in range(code.shape[0] // rows):
        at = slice(step * rows, (step + 1) * rows)
        fields.append((jnp.concatenate([lat[at], fill], axis=0), jnp.concatenate([lon[at], fill], axis=0)))
    return fields


def shift_rows(mask, by):
    blank = jnp.zeros((1, mask.shape[1]), F32)
    if by == 1:
        return jnp.concatenate([blank, mask[:-1]], axis=0)
    if by == -1:
        return jnp.concatenate([mask[1:], blank], axis=0)
    return mask


def cells_pulled(fields, rows):
    lon = fields[0][0].shape[1]
    row = lax.broadcasted_iota(jnp.int32, (8, lon), 0)
    mask = jnp.where(row == 0, 1.0, 0.0)
    for lat, east in reversed(fields[: len(fields) - 1]):
        new = mask
        for a in (-1, 0, 1):
            total = jnp.zeros_like(mask)
            for b in range(-2, 3):
                hit = jnp.where((lat == float(a)) & (east == float(b)), mask, 0.0)
                total = jnp.maximum(total, hit if b == 0 else pltpu.roll(hit, (-b) % lon, 1))
            new = jnp.maximum(new, shift_rows(total, -a))
        mask = jnp.where(row < rows, new, 0.0)
    return mask


def cells_reached(fields, rows):
    lon = fields[0][0].shape[1]
    row = lax.broadcasted_iota(jnp.int32, (8, lon), 0)
    mask = jnp.zeros((8, lon), F32)
    for lat, east in fields:
        new = mask
        for a in (-1, 0, 1):
            source = shift_rows(mask, a)
            if a == 1:
                source = jnp.where(row == 0, 1.0, source)
            for b in range(-2, 3):
                seen = source if b == 0 else pltpu.roll(source, b % lon, 1)
                new = jnp.maximum(new, jnp.where((lat == float(a)) & (east == float(b)), seen, 0.0))
        mask = jnp.where(row < rows, new, 0.0)
    return mask


def slot_of(mask):
    lon = mask.shape[1]
    before = lax.broadcasted_iota(jnp.int32, (lon, lon), 0) < lax.broadcasted_iota(jnp.int32, (lon, lon), 1)
    place = dot(mask.astype(BF16), jnp.where(before, 1.0, 0.0).astype(BF16))
    totals = jnp.sum(mask, axis=1, keepdims=True)
    ahead = jnp.zeros((1, 1), F32)
    lines = []
    for j in range(mask.shape[0]):
        lines.append(place[j : j + 1] + ahead)
        ahead = ahead + totals[j : j + 1]
    return jnp.where(mask > 0.0, jnp.concatenate(lines, axis=0), -1.0), ahead


def choose_matrix(slots, size, rows, first=0):
    lon = slots.shape[1]
    at = lax.broadcasted_iota(jnp.int32, (size, lon), 0).astype(F32) + float(first)
    parts = [jnp.where(slots[j : j + 1] == at, 1.0, 0.0) for j in range(rows)]
    return jnp.concatenate(parts, axis=1).astype(BF16)


def spread_matrix(turned, row, size, first=0):
    at = lax.broadcasted_iota(jnp.int32, (turned.shape[0], size), 1).astype(F32) + float(first)
    return jnp.where(turned[:, row : row + 1] == at, 1.0, 0.0).astype(BF16)


def turn(slots):
    lon = slots.shape[1]
    return jnp.concatenate([slots, jnp.full((lon - slots.shape[0], lon), -1.0, F32)], axis=0).T


def sign_of(flip):
    return jnp.where(flip[0] == 1, -1.0, 1.0)


def pack_kernel(flip, tangent, wind, own, sent, codes, slots, buf, wind_b, sem):
    rows, lon = tangent.shape[0], tangent.shape[1]
    cells = rows * lon
    wind_copy = pltpu.make_async_copy(wind, wind_b, sem.at[rows])
    wind_copy.start()
    copies = []
    for j in range(rows):
        at = jnp.where(flip[0] == 1, rows - 1 - j, j)
        copies.append(pltpu.make_async_copy(tangent.at[at], buf.at[j], sem.at[j]))
        copies[-1].start()
    wind_copy.wait()
    for step in range(wind_b.shape[0]):
        for j in range(rows):
            code = jnp.where(flip[0] == 1, wind_b[step, rows - 1 - j : rows - j, :], wind_b[step, j : j + 1, :])
            codes[step * rows + j : step * rows + j + 1, :] = code.astype(F32) + 1.0
    mask = cells_pulled(wind_fields(codes[...], sign_of(flip), rows), rows)
    where, total = slot_of(mask)
    slots[...] = where
    head = codes.shape[0]
    flag = jnp.broadcast_to(jnp.where(total > float(FAR_CELLS), 1.0, 0.0), (NOTE_ROWS, lon))
    blank_lanes = own.shape[1] - lon
    own[cells:, :] = jnp.concatenate([codes[...], jnp.zeros((head, blank_lanes), F32)], axis=1).astype(BF16)
    notes = [codes[0:NOTE_ROWS], codes[NOTE_ROWS:], mask, flag, jnp.zeros((NOTE_ROWS, blank_lanes - 3 * lon), F32)]
    choose = choose_matrix(where, sent.shape[0], rows)
    for j in range(rows):
        copies[j].wait()
        own[j * lon : (j + 1) * lon, :] = buf[j].astype(BF16)
    chosen = dot(choose, own[0:cells, :])
    last = FAR_CELLS - NOTE_ROWS
    sent[0:last, :] = chosen[0:last].astype(BF16)
    tail = jnp.concatenate([chosen[last:FAR_CELLS], jnp.concatenate(notes, axis=1)], axis=0)
    sent[last:, :] = tail.astype(BF16)


def choose_kernel(flag, *refs):
    count = len(refs) // 3
    redone, outs, sem = refs[count : 2 * count], refs[2 * count : 3 * count], refs[-1]

    @pl.when(flag[0] > 0)
    def _():
        copies = [pltpu.make_async_copy(redone[k], outs[k], sem.at[k]) for k in range(count)]
        for copy in copies:
            copy.start()
        for copy in copies:
            copy.wait()


def rest_kernel(first, slots, dense, out):
    rows = dense.shape[0] // slots.shape[1]
    cells = rows * slots.shape[1]
    choose = choose_matrix(slots[...], out.shape[0], rows, first)
    out[...] = dot(choose, dense[0:cells, :]).astype(BF16)


def blank_kernel(*outs):
    pass


def near_steps(mats, start_b, start_f, c_ref, outs, mid_b, mid_f, lon, cs):
    c = c_ref[0:1, cs]
    blocks = ((5, 7, 9), (6, 8), (7,))
    read_b, read_f, first = start_b, start_f, 4
    k = 0
    for step, exts in enumerate(blocks):
        for ext in exts:
            at = (ext - 1 - first) * lon
            pulled = dot(mats[k], read_b(at, 4 * lon))
            value = (1.0 - c) * read_f(at + lon, 2 * lon) + c * pulled
            k += 1
            if ext == exts[0]:
                outs[step][:, cs] = value
            if step < 2:
                to = (ext - exts[0]) * lon
                mid_f[step, to : to + 2 * lon, :] = value
                mid_b[step, to : to + 2 * lon, :] = value.astype(BF16)
        first = exts[0]
        read_b = functools.partial(lambda s, a, n: mid_b[s, a : a + n, :], step)
        read_f = functools.partial(lambda s, a, n: mid_f[s, a : a + n, :], step)


def by_parts(levels, body):
    @pl.loop(0, levels // PART)
    def _(i):
        body(pl.ds(pl.multiple_of(i * PART, PART), PART))


def far_steps(mats, start_b, start_f, c_ref, kept, mid_b, mid_f, lon, finish):
    c = c_ref[0:1, :]
    k = 0
    for step in range(4):
        now, last = step % 2, (step + 1) % 2
        for half in range(2):
            at = 2 * half * lon
            if step == 0:
                window, own = start_b(at, 4 * lon), start_f(at + lon, 2 * lon)
            else:
                window = mid_b[last, at : at + 4 * lon, :]
                own = mid_f[last, at + lon : at + 3 * lon, :]
            value = (1.0 - c) * own + c * dot(mats[k][...], window)
            k += 1
            if step < 3:
                if half == 0:
                    mid_f[now, lon : 2 * lon, :] = value[lon:]
                else:
                    mid_f[now, at : at + 2 * lon, :] = value
                mid_b[now, at : at + 2 * lon, :] = value.astype(BF16)
            else:
                finish(half, value)
        if step < 3:
            carried = kept[step][...]
            mid_f[now, 4 * lon : 5 * lon, :] = carried[0:lon]
            mid_b[now, 4 * lon :, :] = carried.astype(BF16)


def near_kernel(
    flip, obs_count, tangent, codes, near, courant, background, w_first, w_second, obs_index, obs_quality,
    slope_one, slope_two, kept_a, kept_b, kept_c, pick, place, place_far, near_codes, quality, slots, own_mats, own_f, own_b,
    table, mats, cells_b, mid_b, mid_f, hidden,
):
    rows, lon = tangent.shape[0], tangent.shape[1]
    cells = rows * lon
    sign = sign_of(flip)
    table[...] = jnp.zeros_like(table)
    near_codes[...] = near[cells:, 0:lon].astype(F32)
    store_sources(table, 1, codes[...], False, sign, lon, rows)
    store_sources(table, 2, near_codes[...], True, sign, lon, rows)
    turned = table[...].T
    k = 0
    for step, exts in enumerate(((5, 7, 9), (6, 8), (7,))):
        for ext in exts:
            pull_matrix(mats.at[k], turned, step, ext, lon, rows)
            k += 1
    for k, (step, half) in enumerate(OWN_BLOCKS):
        pull_matrix(own_mats.at[k], turned, step, step + 1 + 2 * half, lon, rows)
    for j in range(rows):
        row = tangent[jnp.where(flip[0] == 1, rows - 1 - j, j)]
        cells_b[j * lon : (j + 1) * lon, :] = row.astype(BF16)
        cells_b[(rows + j) * lon : (rows + j + 1) * lon, :] = near[(rows - 1 - j) * lon : (rows - j) * lon, :]

    own_f[...] = tangent[jnp.where(flip[0] == 1, rows - 1, 0)]
    own_b[...] = cells_b[0 : 2 * lon, :]

    def advect(cs):
        def start_f(at, size):
            pieces = []
            for row in range(at // lon, (at + size) // lon):
                if row < rows:
                    pieces.append(tangent[jnp.where(flip[0] == 1, rows - 1 - row, row), :, cs])
                else:
                    pieces.append(cells_b[row * lon : (row + 1) * lon, cs].astype(F32))
            return jnp.concatenate(pieces, axis=0)

        near_steps(
            mats, lambda at, size: cells_b[at : at + size, cs], start_f, courant,
            (kept_a, kept_b, kept_c), mid_b, mid_f, lon, cs,
        )

    by_parts(tangent.shape[2], advect)

    def first_layer(cs):
        first_tanh = jnp.tanh(dot(background[...], w_first[:, cs]))
        hidden[:, cs] = first_tanh.astype(BF16)
        slope_one[:, cs] = 1.0 - first_tanh * first_tanh

    by_parts(w_first.shape[1], first_layer)

    def second_layer(cs):
        second_tanh = jnp.tanh(dot(hidden[...], w_second[:, cs]))
        slope_two[:, cs] = 1.0 - second_tanh * second_tanh

    by_parts(w_second.shape[1], second_layer)

    count = obs_index.shape[1]
    at = obs_index[...]
    at = jnp.where(flip[0] == 1, at + (rows - 1 - 2 * lax.div(at, lon)) * lon, at)
    live = lax.broadcasted_iota(jnp.int32, at.shape, 1) < obs_count[0]
    at = jnp.where(live, at, -1)
    chosen = at == lax.broadcasted_iota(jnp.int32, (cells, count), 0)
    place[...] = jnp.where(chosen, 1.0, 0.0).astype(BF16)
    lines = jnp.concatenate([at.astype(F32), jnp.where(live, obs_quality[...].astype(F32), 0.0)], axis=0)
    lines = jnp.concatenate([lines, jnp.zeros((6, count), F32)], axis=0)
    lines = jnp.concatenate([lines, jnp.zeros((8, cells - count), F32)], axis=1).T
    quality[...] = lines[0:count, 1:2]
    columns = lax.broadcasted_iota(jnp.int32, (count, cells), 1).astype(F32)
    pick[...] = jnp.where(lines[0:count, 0:1] == columns, 1.0, 0.0).astype(BF16)
    where, _ = slot_of(cells_reached(wind_fields(codes[...], sign, rows), rows))
    slots[...] = where
    place_far[...] = dot(choose_matrix(slots[...], place_far.shape[0], rows), place[...]).astype(BF16)


def observe_kernel(
    redo, flip, linked, slots, own_f, own_b, codes, far, rest, courant, slope_one, slope_two, kept_a, kept_b, kept_c,
    hbm_first, hbm_second, hbm_third, pick, place, place_far, quality, chan_weight, own_mats, own_slots,
    hbm_out, hbm_low, hbm_high, hbm_codes, hbm_slots, over, over_columns,
    table, mats, cells_b, mid_b, mid_f, last_b, one_b, two_b, w_first, w_second, w_third, out, low, high, far_codes, far_slots, sem,
    rest_b,
):
    rows, lon = 4, own_f.shape[0]
    cells = rows * lon
    sign = sign_of(flip)
    loads = [
        pltpu.make_async_copy(hbm_first, w_first, sem.at[0]),
        pltpu.make_async_copy(hbm_second, w_second, sem.at[1]),
        pltpu.make_async_copy(hbm_third, w_third, sem.at[2]),
    ]
    for copy in loads:
        copy.start()
    table[...] = jnp.zeros_like(table)
    tail = far[FAR_CELLS - NOTE_ROWS :, 0 : 4 * lon].astype(F32)[NOTE_ROWS:]
    far_codes[0:NOTE_ROWS, :] = tail[:, 0:lon]
    far_codes[NOTE_ROWS:, :] = tail[:, lon : 2 * lon]
    store_sources(table, 0, far_codes[...], True, sign, lon, rows)
    store_sources(table, 1, codes[...], False, sign, lon, rows)
    turned = table[...].T
    keep_codes = pltpu.make_async_copy(far_codes, hbm_codes, sem.at[3])
    keep_codes.start()
    reached, total = slot_of(cells_reached(wind_fields(far_codes[...], -sign, rows), rows))
    far_slots[...] = reached
    keep_slots = pltpu.make_async_copy(far_slots, hbm_slots, sem.at[6])
    keep_slots.start()
    most = jnp.maximum(jnp.max(total), jnp.max(own_slots[...]) + 1.0)
    over_columns[0] = jnp.where(most > float(FAR_COLUMNS), linked[0], 0)
    chosen = [None] * 8
    for k, (step, half) in enumerate(OWN_BLOCKS):
        chosen[2 * step + half] = own_mats.at[k]
    for k, (step, half) in enumerate(FAR_BLOCKS):
        pull_matrix(mats.at[k], turned, step, step + 1 + 2 * half, lon, rows)
        chosen[2 * step + half] = mats.at[k]
    listed, _ = slot_of(tail[:, 2 * lon : 3 * lon])
    where = turn(jnp.where(listed < float(FAR_CELLS), listed, -1.0))
    most = jnp.maximum(jnp.max(tail[:, 3 * lon :]), jnp.where(jnp.max(slots[...]) >= float(FAR_CELLS), 1.0, 0.0))
    over[0] = jnp.where(most > 0.0, linked[0], 0)
    for j in range(rows):
        value = dot(spread_matrix(where, j, far.shape[0]), far[...])
        cells_b[(rows - 1 - j) * lon : (rows - j) * lon, :] = value.astype(BF16)
    cells_b[cells:, :] = own_b[...]

    if redo:
        copy = pltpu.make_async_copy(rest, rest_b, sem.at[5])
        copy.start()
        copy.wait()
        where = turn(jnp.where(listed < float(FAR_CELLS), -1.0, listed))
        for j in range(rows):
            value = dot(spread_matrix(where, j, rest_b.shape[0], FAR_CELLS - NOTE_ROWS), rest_b[...])
            at = slice((rows - 1 - j) * lon, (rows - j) * lon)
            cells_b[at, :] = (cells_b[at, :].astype(F32) + value).astype(BF16)

    def start_f(at, size):
        pieces = []
        for row in range(at // lon, (at + size) // lon):
            if row == rows:
                pieces.append(own_f[...])
            else:
                pieces.append(cells_b[row * lon : (row + 1) * lon, :].astype(F32))
        return jnp.concatenate(pieces, axis=0)

    def finish(half, value):
        last_b[2 * half * lon : 2 * (half + 1) * lon, :] = value.astype(BF16)

    far_steps(
        chosen, lambda at, size: cells_b[at : at + size, :], start_f, courant,
        (kept_a, kept_b, kept_c), mid_b, mid_f, lon, finish,
    )
    one_b[...] = dot(pick[...], last_b[...]).astype(BF16)
    loads[0].wait()
    two_b[...] = (slope_one[...] * dot(one_b[...], w_first[...])).astype(BF16)
    loads[1].wait()
    one_b[...] = (slope_two[...] * dot(two_b[...], w_second[...])).astype(BF16)
    loads[2].wait()
    scale = quality[...] * chan_weight[0:1, :]
    two_b[...] = (scale * dot(one_b[...], w_third[...])).astype(BF16)
    one_b[...] = (slope_two[...] * dot_t(two_b[...], w_third[...])).astype(BF16)
    two_b[...] = (slope_one[...] * dot_t(one_b[...], w_second[...])).astype(BF16)
    one_b[...] = dot_t(two_b[...], w_first[...]).astype(BF16)
    half = low.shape[1]
    low[...] = dot(place_far[...], one_b[:, :half]).astype(BF16)
    keep_low = pltpu.make_async_copy(low, hbm_low, sem.at[4])
    keep_low.start()
    high[...] = dot(place_far[...], one_b[:, half:]).astype(BF16)
    keep_high = pltpu.make_async_copy(high, hbm_high, sem.at[1])
    keep_high.start()
    out[...] = dot(place[...], one_b[...]).astype(BF16)
    keep_out = pltpu.make_async_copy(out, hbm_out, sem.at[0])
    keep_out.start()
    keep_codes.wait()
    keep_slots.wait()
    keep_low.wait()
    keep_high.wait()
    keep_out.wait()


def near_adjoint_kernel(
    flip, rest, cells_own, cells_near, codes, near_codes, far_codes, far_slots, courant,
    kept_a, kept_b, kept_c, far_mats, spread,
    table, mats, cells_b, mid_b, mid_f, slots_b, codes_b, sem,
):
    rows, lon = 4, table.shape[1]
    cells = rows * lon
    own_copy = pltpu.make_async_copy(cells_own, cells_b.at[0:cells], sem.at[0])
    own_copy.start()
    slots_copy = pltpu.make_async_copy(far_slots, slots_b, sem.at[1])
    slots_copy.start()
    codes_copy = pltpu.make_async_copy(far_codes, codes_b, sem.at[2])
    codes_copy.start()
    codes_copy.wait()
    sign = sign_of(flip)
    store_sources(table, 0, codes_b[...], True, sign, lon, rows)
    store_sources(table, 1, codes[...], False, sign, lon, rows)
    store_sources(table, 2, near_codes[...], True, sign, lon, rows)
    k = 0
    for order, exts in enumerate(((5, 7, 9), (6, 8), (7,))):
        for ext in exts:
            push_matrix(mats.at[k], table, 3 - order, ext, lon, rows)
            k += 1
    for j in range(rows):
        cells_b[(rows + j) * lon : (rows + j + 1) * lon, :] = cells_near[
            (rows - 1 - j) * lon : (rows - j) * lon, :
        ]

    own_copy.wait()

    def advect(cs):
        near_steps(
            mats, lambda at, size: cells_b[at : at + size, cs],
            lambda at, size: cells_b[at : at + size, cs].astype(F32), courant,
            (kept_a, kept_b, kept_c), mid_b, mid_f, lon, cs,
        )

    advect(slice(None))
    for order in range(4):
        for half in range(2):
            push_matrix(far_mats.at[2 * order + half], table, 3 - order, order + 1 + 2 * half, lon, rows)
    slots_copy.wait()
    where = turn(slots_b[...])
    capacity = spread.shape[1]
    for j in range(rows):
        spread[j * lon : (j + 1) * lon, :] = spread_matrix(where, j, capacity)


def far_adjoint_kernel(
    part, flip, flag, cells_own, far, rest, courant, kept_a, kept_b, kept_c, mats, spread, far_slots, _given,
    out,
    cells_b, mid_b, mid_f, result, rest_b, slots_b, sem,
):
    rows, lon = out.shape[0], out.shape[1]
    cells = rows * lon
    width = far.shape[1]
    cs = slice(part * width, (part + 1) * width)
    for j in range(rows):
        value = dot(spread[j * lon : (j + 1) * lon, :], far[...])
        cells_b[(rows - 1 - j) * lon : (rows - j) * lon, :] = value.astype(BF16)
    cells_b[cells:, :] = cells_own[0 : 2 * lon, cs]

    @pl.when(flag[0] > 0)
    def _():
        fetches = [
            pltpu.make_async_copy(rest.at[:, cs], rest_b, sem.at[rows]),
            pltpu.make_async_copy(far_slots, slots_b, sem.at[rows + 1]),
        ]
        for copy in fetches:
            copy.start()
        for copy in fetches:
            copy.wait()
        where = turn(slots_b[...])
        for j in range(rows):
            value = dot(spread_matrix(where, j, rest_b.shape[0], spread.shape[1]), rest_b[...])
            at = slice((rows - 1 - j) * lon, (rows - j) * lon)
            cells_b[at, :] = (cells_b[at, :].astype(F32) + value).astype(BF16)

    copies = []

    def finish(half, value):
        for piece in range(2):
            j = 2 * half + piece
            result[j] = value[piece * lon : (piece + 1) * lon, :]
            at = jnp.where(flip[0] == 1, rows - 1 - j, j)
            copies.append(pltpu.make_async_copy(result.at[j], out.at[at, :, cs], sem.at[j]))
            copies[-1].start()

    far_steps(
        [mats.at[k] for k in range(8)], lambda at, size: cells_b[at : at + size, :],
        lambda at, size: cells_b[at : at + size, :].astype(F32), courant.at[:, cs],
        tuple(kept.at[:, cs] for kept in (kept_a, kept_b, kept_c)), mid_b, mid_f, lon, finish,
    )
    for copy in copies:
        copy.wait()


def params():
    return pltpu.CompilerParams(vmem_limit_bytes=VMEM_LIMIT)


def shape(dims, dtype):
    return jax.ShapeDtypeStruct(dims, dtype)


def send_rest(first, slots, dense, size, links):
    rest = pl.pallas_call(
        functools.partial(rest_kernel, first),
        out_shape=shape((size, dense.shape[1]), BF16),
        in_specs=[VMEM, VMEM],
        out_specs=VMEM,
        name="rest",
    )(slots, dense)
    return lax.ppermute(rest, "lat", links)


def blank(outs):
    return pl.pallas_call(blank_kernel, out_shape=outs, out_specs=[ANY] * len(outs), name="blank")()


def local(
    tangent,
    wind_code,
    courant,
    obs_index,
    obs_count,
    obs_quality,
    background,
    w_first,
    w_second,
    w_third,
    chan_weight,
):
    rows, lon, levels = tangent.shape
    cells = rows * lon
    head = wind_code.shape[0] * rows
    listed = obs_index.shape[1]
    hidden_size = w_first.shape[1]
    count = lax.axis_size("lat")
    here = lax.axis_index("lat")
    odd = (here % 2).astype(jnp.int32)
    flip = odd.reshape(1)
    linked = ((here > 0) & (here < count - 1)).astype(jnp.int32).reshape(1)
    pairs = [(i, i ^ 1) for i in range(count)]
    links = [(i, i + 1) for i in range(1, count - 1, 2)]
    links = links + [(b, a) for a, b in links]

    own, sent, codes, slots = pl.pallas_call(
        pack_kernel,
        out_shape=[
            shape((cells + head, levels), BF16),
            shape((FAR_CELLS + NOTE_ROWS, levels), BF16),
            shape((head, lon), F32),
            shape((8, lon), F32),
        ],
        in_specs=[SMEM, HBM, HBM],
        out_specs=[VMEM] * 4,
        scratch_shapes=[
            pltpu.VMEM((rows, lon, levels), F32),
            pltpu.VMEM(wind_code.shape, jnp.int32),
            pltpu.SemaphoreType.DMA((rows + 1,)),
        ],
        compiler_params=pltpu.CompilerParams(vmem_limit_bytes=PACK_LIMIT),
        name="pack",
    )(flip, tangent, wind_code)

    far = lax.ppermute(sent, "lat", links)
    near = lax.ppermute(own, "lat", pairs)

    c_row = courant.reshape(1, levels)
    kept_shape = [shape((2 * lon, levels), F32)] * 3
    slope_shape = shape((listed, hidden_size), F32)

    def run_near():
        return pl.pallas_call(
            near_kernel,
            out_shape=[slope_shape, slope_shape]
            + kept_shape
            + [
                shape((listed, cells), BF16),
                shape((cells, listed), BF16),
                shape((FAR_COLUMNS, listed), BF16),
                shape((head, lon), F32),
                shape((listed, 1), F32),
                shape((8, lon), F32),
                shape((4, 2 * lon, 4 * lon), BF16),
                shape((lon, levels), F32),
                shape((2 * lon, levels), BF16),
            ],
            in_specs=[SMEM, SMEM] + [VMEM] * 9,
            out_specs=[VMEM] * 14,
            scratch_shapes=[
                pltpu.VMEM((lon, lon), F32),
                pltpu.VMEM((6, 2 * lon, 4 * lon), BF16),
                pltpu.VMEM((2 * cells, levels), BF16),
                pltpu.VMEM((2, 6 * lon, PART), BF16),
                pltpu.VMEM((2, 6 * lon, PART), F32),
                pltpu.VMEM((listed, hidden_size), BF16),
            ],
            compiler_params=params(),
            cost_estimate=pl.CostEstimate(flops=4_000_000_000, bytes_accessed=16_000_000, transcendentals=1_000_000),
            name="near",
        )(
            flip, obs_count, tangent, codes, near, c_row, background[0], w_first, w_second, obs_index, obs_quality,
        )

    column_shape = [pltpu.HBM((cells, levels), BF16)] + [pltpu.HBM((FAR_COLUMNS, levels // 2), BF16)] * 2

    def run_observe(redo, parts, rest):
        slope_one, slope_two, kept_a, kept_b, kept_c, pick, place, place_far = parts[:8]
        quality, columns_list, own_mats, own_f, own_b = parts[9:]
        rest_specs = [ANY] if redo else []
        body = functools.partial(observe_kernel, redo)
        rest_args = [rest] if redo else []
        rest_scratch = [pltpu.VMEM((cells - FAR_CELLS + NOTE_ROWS, levels), BF16)]

        def kernel(*refs):
            refs = list(refs)
            if not redo:
                refs.insert(7, None)
                refs.append(None)
            body(*refs)

        return pl.pallas_call(
            kernel,
            out_shape=column_shape
            + [pltpu.HBM((head, lon), F32), pltpu.HBM((8, lon), F32)]
            + [shape((1,), jnp.int32)] * 2,
            in_specs=[SMEM, SMEM] + [VMEM] * 5 + rest_specs + [VMEM] * 6 + [ANY] * 3 + [VMEM] * 7,
            out_specs=[HBM] * 5 + [SMEM] * 2,
            scratch_shapes=[
                pltpu.VMEM((lon, lon), F32),
                pltpu.VMEM((4, 2 * lon, 4 * lon), BF16),
                pltpu.VMEM((6 * lon, levels), BF16),
                pltpu.VMEM((2, 6 * lon, levels), BF16),
                pltpu.VMEM((2, 6 * lon, levels), F32),
                pltpu.VMEM((cells, levels), BF16),
                pltpu.VMEM((listed, levels), BF16),
                pltpu.VMEM((listed, levels), BF16),
                pltpu.VMEM(w_first.shape, BF16),
                pltpu.VMEM(w_second.shape, BF16),
                pltpu.VMEM(w_third.shape, BF16),
                pltpu.VMEM((cells, levels), BF16),
                pltpu.VMEM((FAR_COLUMNS, levels // 2), BF16),
                pltpu.VMEM((FAR_COLUMNS, levels // 2), BF16),
                pltpu.VMEM((head, lon), F32),
                pltpu.VMEM((8, lon), F32),
                pltpu.SemaphoreType.DMA((7,)),
            ]
            + (rest_scratch if redo else []),
            compiler_params=params(),
            name="observe",
        )(
            flip, linked, slots, own_f, own_b, codes, far, *rest_args, c_row,
            slope_one, slope_two, kept_a, kept_b, kept_c, w_first, w_second, w_third,
            pick, place, place_far, quality, chan_weight.reshape(1, -1), own_mats, columns_list,
        )

    parts = run_near()
    near_codes, own_slots = parts[8], parts[10]
    cells_own, low, high, far_codes, far_slots, over, over_columns = run_observe(False, parts, None)

    def observe_again():
        first = FAR_CELLS - NOTE_ROWS
        rest = send_rest(first, slots, own, cells - first, links)
        return run_observe(True, run_near(), rest)[:3]

    redone = lax.cond(over[0] > 0, observe_again, lambda: blank(column_shape))
    cells_own, low, high = pl.pallas_call(
        choose_kernel,
        out_shape=column_shape,
        in_specs=[SMEM] + [HBM] * 6,
        out_specs=[HBM] * 3,
        scratch_shapes=[pltpu.SemaphoreType.DMA((3,))],
        input_output_aliases={1: 0, 2: 1, 3: 2},
        name="choose",
    )(over, cells_own, low, high, *redone)

    far_low = lax.ppermute(low, "lat", links)
    far_high = lax.ppermute(high, "lat", links)
    cells_near = lax.ppermute(cells_own, "lat", pairs)

    left = cells - FAR_COLUMNS
    rest = lax.cond(
        over_columns[0] > 0,
        lambda: send_rest(FAR_COLUMNS, own_slots, cells_own, left, links),
        lambda: blank([shape((left, levels), BF16)])[0],
    )
    kept_a, kept_b, kept_c, mats, spread = pl.pallas_call(
        near_adjoint_kernel,
        out_shape=kept_shape
        + [
            shape((8, 2 * lon, 4 * lon), BF16),
            shape((cells, FAR_COLUMNS), BF16),
        ],
        in_specs=[SMEM, ANY, ANY] + [VMEM] * 3 + [ANY, ANY, VMEM],
        out_specs=[VMEM] * 5,
        scratch_shapes=[
            pltpu.VMEM((lon, lon), F32),
            pltpu.VMEM((6, 2 * lon, 4 * lon), BF16),
            pltpu.VMEM((2 * cells, levels), BF16),
            pltpu.VMEM((2, 6 * lon, levels), BF16),
            pltpu.VMEM((2, 6 * lon, levels), F32),
            pltpu.VMEM((8, lon), F32),
            pltpu.VMEM((head, lon), F32),
            pltpu.SemaphoreType.DMA((3,)),
        ],
        compiler_params=params(),
        cost_estimate=pl.CostEstimate(flops=2_000_000_000, bytes_accessed=8_000_000, transcendentals=0),
        name="near_adjoint",
    )(flip, rest, cells_own, cells_near, codes, near_codes, far_codes, far_slots, c_row)

    width = levels // 2

    def finish(part, columns, given):
        body = functools.partial(far_adjoint_kernel, part)
        given_specs = [HBM] if part else []

        def kernel(*refs):
            refs = list(refs)
            if not part:
                refs.insert(12, None)
            body(*refs)

        return pl.pallas_call(
            kernel,
            out_shape=shape((rows, lon, levels), F32),
            in_specs=[SMEM, SMEM, VMEM, VMEM, ANY] + [VMEM] * 6 + [ANY] + given_specs,
            out_specs=HBM,
            scratch_shapes=[
                pltpu.VMEM((6 * lon, width), BF16),
                pltpu.VMEM((2, 6 * lon, width), BF16),
                pltpu.VMEM((2, 6 * lon, width), F32),
                pltpu.VMEM((rows, lon, width), F32),
                pltpu.VMEM((left, width), BF16),
                pltpu.VMEM((8, lon), F32),
                pltpu.SemaphoreType.DMA((rows + 2,)),
            ],
            input_output_aliases={12: 0} if part else {},
            compiler_params=params(),
            cost_estimate=pl.CostEstimate(flops=2_000_000_000, bytes_accessed=4_000_000, transcendentals=0),
            name="far_adjoint",
        )(
            flip, over_columns, cells_own, columns, rest, c_row, kept_a, kept_b, kept_c, mats, spread, far_slots, *given,
        )

    half_done = finish(0, far_low, [])
    return finish(1, far_high, [half_done])


def solution(mesh):
    placed = (
        P(("groups", "lat"), None, None),
        P(None, ("groups", "lat"), None),
        P(),
        P(("groups", "lat"), None),
        P(("groups", "lat")),
        P(("groups", "lat"), None),
        P(("groups", "lat"), None, None),
        P(),
        P(),
        P(),
        P(),
    )
    return jax.shard_map(
        local,
        mesh=mesh,
        in_specs=placed,
        out_specs=P(("groups", "lat"), None, None),
        check_vma=False,
    )
```

```python
import functools

import jax
import jax.numpy as jnp
from jax import lax
from jax.experimental import pallas as pl
from jax.experimental.pallas import tpu as pltpu
from jax.sharding import PartitionSpec as P

F32 = jnp.float32
BF16 = jnp.bfloat16
PART = 512
NOTE_ROWS = 8
FAR_CELLS = 296
FAR_COLUMNS = 256
ANY = pl.BlockSpec(memory_space=pl.ANY)
VMEM = pl.BlockSpec(memory_space=pltpu.VMEM)
HBM = pl.BlockSpec(memory_space=pltpu.HBM)
SMEM = pl.BlockSpec(memory_space=pltpu.SMEM)
VMEM_LIMIT = 32 * 1024 * 1024
PACK_LIMIT = 60 * 1024 * 1024

OWN_BLOCKS = ((1, 1), (2, 1), (3, 0), (3, 1))
FAR_BLOCKS = ((0, 0), (0, 1), (1, 0), (2, 0))


def dot_t(left, right):
    return lax.dot_general(left, right, (((1,), (1,)), ((), ())), preferred_element_type=F32)


def dot(left, right):
    return jnp.dot(left, right, preferred_element_type=F32)


def store_sources(table, slot, codes, mirrored, sign, lon, rows):
    code = codes.astype(F32) - 1.0
    lat_q = jnp.where(code >= 5.0, 1.0, 0.0) + jnp.where(code >= 10.0, 1.0, 0.0)
    lon_step = code - 5.0 * lat_q - 2.0
    col = lax.broadcasted_iota(jnp.int32, code.shape, 1).astype(F32) - lon_step
    col = jnp.where(col < 0.0, col + lon, jnp.where(col >= lon, col - lon, col))
    stored = lax.broadcasted_iota(jnp.int32, code.shape, 0) & (rows - 1)
    row = (rows - 1 - stored) if mirrored else stored
    row = (row + slot * rows).astype(F32)
    src = (row - sign * (lat_q - 1.0)) * lon + col
    table[slot * code.shape[0] : (slot + 1) * code.shape[0], :] = jnp.where(code < 0.0, -65536.0, src)


def table_row(step, ext, rows):
    slot, at = ext // rows, ext % rows
    return slot * rows * rows + step * rows + (at if slot == 1 else rows - 1 - at)


def pull_matrix(out, turned, step, ext, lon, rows):
    span = 4 * lon
    lanes = lax.broadcasted_iota(jnp.int32, (lon, span), 1).astype(F32) + float((ext - 1) * lon)
    for half in range(2):
        k = table_row(step, ext + half, rows)
        column = turned[:, k : k + 1]
        out[half * lon : (half + 1) * lon, :] = jnp.where(column == lanes, 1.0, 0.0).astype(BF16)


def push_matrix(out, table, step, ext, lon, rows):
    dest = lax.broadcasted_iota(jnp.int32, (2 * lon, lon), 0).astype(F32) + float(ext * lon)
    for part in range(4):
        k = table_row(step, ext - 1 + part, rows)
        line = table[k : k + 1, :]
        out[:, part * lon : (part + 1) * lon] = jnp.where(line == dest, 1.0, 0.0).astype(BF16)


def wind_fields(codes, sign, rows):
    code = codes.astype(F32) - 1.0
    lat_q = jnp.where(code >= 5.0, 1.0, 0.0) + jnp.where(code >= 10.0, 1.0, 0.0)
    lat = jnp.where(code < 0.0, 9.0, sign * (lat_q - 1.0))
    lon = code - 5.0 * lat_q - 2.0
    fill = jnp.full((8 - rows, code.shape[1]), 9.0, F32)
    fields = []
    for step in range(code.shape[0] // rows):
        at = slice(step * rows, (step + 1) * rows)
        fields.append((jnp.concatenate([lat[at], fill], axis=0), jnp.concatenate([lon[at], fill], axis=0)))
    return fields


def shift_rows(mask, by):
    blank = jnp.zeros((1, mask.shape[1]), F32)
    if by == 1:
        return jnp.concatenate([blank, mask[:-1]], axis=0)
    if by == -1:
        return jnp.concatenate([mask[1:], blank], axis=0)
    return mask


def cells_pulled(fields, rows):
    lon = fields[0][0].shape[1]
    row = lax.broadcasted_iota(jnp.int32, (8, lon), 0)
    mask = jnp.where(row == 0, 1.0, 0.0)
    for lat, east in reversed(fields[: len(fields) - 1]):
        new = mask
        for a in (-1, 0, 1):
            total = jnp.zeros_like(mask)
            for b in range(-2, 3):
                hit = jnp.where((lat == float(a)) & (east == float(b)), mask, 0.0)
                total = jnp.maximum(total, hit if b == 0 else pltpu.roll(hit, (-b) % lon, 1))
            new = jnp.maximum(new, shift_rows(total, -a))
        mask = jnp.where(row < rows, new, 0.0)
    return mask


def cells_reached(fields, rows):
    lon = fields[0][0].shape[1]
    row = lax.broadcasted_iota(jnp.int32, (8, lon), 0)
    mask = jnp.zeros((8, lon), F32)
    for lat, east in fields:
        new = mask
        for a in (-1, 0, 1):
            source = shift_rows(mask, a)
            if a == 1:
                source = jnp.where(row == 0, 1.0, source)
            for b in range(-2, 3):
                seen = source if b == 0 else pltpu.roll(source, b % lon, 1)
                new = jnp.maximum(new, jnp.where((lat == float(a)) & (east == float(b)), seen, 0.0))
        mask = jnp.where(row < rows, new, 0.0)
    return mask


def slot_of(mask):
    lon = mask.shape[1]
    before = lax.broadcasted_iota(jnp.int32, (lon, lon), 0) < lax.broadcasted_iota(jnp.int32, (lon, lon), 1)
    place = dot(mask.astype(BF16), jnp.where(before, 1.0, 0.0).astype(BF16))
    totals = jnp.sum(mask, axis=1, keepdims=True)
    ahead = jnp.zeros((1, 1), F32)
    lines = []
    for j in range(mask.shape[0]):
        lines.append(place[j : j + 1] + ahead)
        ahead = ahead + totals[j : j + 1]
    return jnp.where(mask > 0.0, jnp.concatenate(lines, axis=0), -1.0), ahead


def choose_matrix(slots, size, rows, first=0):
    lon = slots.shape[1]
    at = lax.broadcasted_iota(jnp.int32, (size, lon), 0).astype(F32) + float(first)
    parts = [jnp.where(slots[j : j + 1] == at, 1.0, 0.0) for j in range(rows)]
    return jnp.concatenate(parts, axis=1).astype(BF16)


def spread_matrix(turned, row, size, first=0):
    at = lax.broadcasted_iota(jnp.int32, (turned.shape[0], size), 1).astype(F32) + float(first)
    return jnp.where(turned[:, row : row + 1] == at, 1.0, 0.0).astype(BF16)


def turn(slots):
    lon = slots.shape[1]
    return jnp.concatenate([slots, jnp.full((lon - slots.shape[0], lon), -1.0, F32)], axis=0).T


def sign_of(flip):
    return jnp.where(flip[0] == 1, -1.0, 1.0)


def pack_kernel(flip, tangent, wind, own, sent, codes, slots, buf, wind_b, sem):
    rows, lon = tangent.shape[0], tangent.shape[1]
    cells = rows * lon
    wind_copy = pltpu.make_async_copy(wind, wind_b, sem.at[rows])
    wind_copy.start()
    copies = []
    for j in range(rows):
        at = jnp.where(flip[0] == 1, rows - 1 - j, j)
        copies.append(pltpu.make_async_copy(tangent.at[at], buf.at[j], sem.at[j]))
        copies[-1].start()
    wind_copy.wait()
    for step in range(wind_b.shape[0]):
        for j in range(rows):
            code = jnp.where(flip[0] == 1, wind_b[step, rows - 1 - j : rows - j, :], wind_b[step, j : j + 1, :])
            codes[step * rows + j : step * rows + j + 1, :] = code.astype(F32) + 1.0
    mask = cells_pulled(wind_fields(codes[...], sign_of(flip), rows), rows)
    where, total = slot_of(mask)
    slots[...] = where
    head = codes.shape[0]
    flag = jnp.broadcast_to(jnp.where(total > float(FAR_CELLS), 1.0, 0.0), (NOTE_ROWS, lon))
    blank_lanes = own.shape[1] - lon
    own[cells:, :] = jnp.concatenate([codes[...], jnp.zeros((head, blank_lanes), F32)], axis=1).astype(BF16)
    notes = [codes[0:NOTE_ROWS], codes[NOTE_ROWS:], mask, flag, jnp.zeros((NOTE_ROWS, blank_lanes - 3 * lon), F32)]
    choose = choose_matrix(where, sent.shape[0], rows)
    for j in range(rows):
        copies[j].wait()
        own[j * lon : (j + 1) * lon, :] = buf[j].astype(BF16)
    chosen = dot(choose, own[0:cells, :])
    last = FAR_CELLS - NOTE_ROWS
    sent[0:last, :] = chosen[0:last].astype(BF16)
    tail = jnp.concatenate([chosen[last:FAR_CELLS], jnp.concatenate(notes, axis=1)], axis=0)
    sent[last:, :] = tail.astype(BF16)


def choose_kernel(flag, *refs):
    count = len(refs) // 3
    redone, outs, sem = refs[count : 2 * count], refs[2 * count : 3 * count], refs[-1]

    @pl.when(flag[0] > 0)
    def _():
        copies = [pltpu.make_async_copy(redone[k], outs[k], sem.at[k]) for k in range(count)]
        for copy in copies:
            copy.start()
        for copy in copies:
            copy.wait()


def rest_kernel(first, slots, dense, out):
    rows = dense.shape[0] // slots.shape[1]
    cells = rows * slots.shape[1]
    choose = choose_matrix(slots[...], out.shape[0], rows, first)
    out[...] = dot(choose, dense[0:cells, :]).astype(BF16)


def blank_kernel(*outs):
    pass


def near_steps(mats, start_b, start_f, c_ref, outs, mid_b, mid_f, lon, cs):
    c = c_ref[0:1, cs]
    blocks = ((5, 7, 9), (6, 8), (7,))
    read_b, read_f, first = start_b, start_f, 4
    k = 0
    for step, exts in enumerate(blocks):
        for ext in exts:
            at = (ext - 1 - first) * lon
            pulled = dot(mats[k], read_b(at, 4 * lon))
            value = (1.0 - c) * read_f(at + lon, 2 * lon) + c * pulled
            k += 1
            if ext == exts[0]:
                outs[step][:, cs] = value
            if step < 2:
                to = (ext - exts[0]) * lon
                mid_f[step, to : to + 2 * lon, :] = value
                mid_b[step, to : to + 2 * lon, :] = value.astype(BF16)
        first = exts[0]
        read_b = functools.partial(lambda s, a, n: mid_b[s, a : a + n, :], step)
        read_f = functools.partial(lambda s, a, n: mid_f[s, a : a + n, :], step)


def by_parts(levels, body):
    @pl.loop(0, levels // PART)
    def _(i):
        body(pl.ds(pl.multiple_of(i * PART, PART), PART))


def far_steps(mats, start_b, start_f, c_ref, kept, mid_b, mid_f, lon, finish):
    c = c_ref[0:1, :]
    k = 0
    for step in range(4):
        now, last = step % 2, (step + 1) % 2
        for half in range(2):
            at = 2 * half * lon
            if step == 0:
                window, own = start_b(at, 4 * lon), start_f(at + lon, 2 * lon)
            else:
                window = mid_b[last, at : at + 4 * lon, :]
                own = mid_f[last, at + lon : at + 3 * lon, :]
            value = own + c * (dot(mats[k][...], window) - own)
            k += 1
            if step < 3:
                if half == 0:
                    mid_f[now, lon : 2 * lon, :] = value[lon:]
                else:
                    mid_f[now, at : at + 2 * lon, :] = value
                mid_b[now, at : at + 2 * lon, :] = value.astype(BF16)
            else:
                finish(half, value)
        if step < 3:
            carried = kept[step][...]
            mid_f[now, 4 * lon : 5 * lon, :] = carried[0:lon]
            mid_b[now, 4 * lon :, :] = carried.astype(BF16)


def near_kernel(
    flip, obs_count, tangent, codes, near, courant, background, w_first, w_second, obs_index, obs_quality,
    slope_one, slope_two, kept_a, kept_b, kept_c, pick, place, place_far, near_codes, quality, slots, own_mats, own_f, own_b,
    table, mats, cells_b, mid_b, mid_f, hidden,
):
    rows, lon = tangent.shape[0], tangent.shape[1]
    cells = rows * lon
    sign = sign_of(flip)
    table[...] = jnp.zeros_like(table)
    near_codes[...] = near[cells:, 0:lon].astype(F32)
    store_sources(table, 1, codes[...], False, sign, lon, rows)
    store_sources(table, 2, near_codes[...], True, sign, lon, rows)
    turned = table[...].T
    k = 0
    for step, exts in enumerate(((5, 7, 9), (6, 8), (7,))):
        for ext in exts:
            pull_matrix(mats.at[k], turned, step, ext, lon, rows)
            k += 1
    for k, (step, half) in enumerate(OWN_BLOCKS):
        pull_matrix(own_mats.at[k], turned, step, step + 1 + 2 * half, lon, rows)
    for j in range(rows):
        row = tangent[jnp.where(flip[0] == 1, rows - 1 - j, j)]
        cells_b[j * lon : (j + 1) * lon, :] = row.astype(BF16)
        cells_b[(rows + j) * lon : (rows + j + 1) * lon, :] = near[(rows - 1 - j) * lon : (rows - j) * lon, :]

    own_f[...] = tangent[jnp.where(flip[0] == 1, rows - 1, 0)]
    own_b[...] = cells_b[0 : 2 * lon, :]

    def advect(cs):
        def start_f(at, size):
            pieces = []
            for row in range(at // lon, (at + size) // lon):
                if row < rows:
                    pieces.append(tangent[jnp.where(flip[0] == 1, rows - 1 - row, row), :, cs])
                else:
                    pieces.append(cells_b[row * lon : (row + 1) * lon, cs].astype(F32))
            return jnp.concatenate(pieces, axis=0)

        near_steps(
            mats, lambda at, size: cells_b[at : at + size, cs], start_f, courant,
            (kept_a, kept_b, kept_c), mid_b, mid_f, lon, cs,
        )

    by_parts(tangent.shape[2], advect)

    def first_layer(cs):
        first_tanh = jnp.tanh(dot(background[...], w_first[:, cs]))
        hidden[:, cs] = first_tanh.astype(BF16)
        slope_one[:, cs] = 1.0 - first_tanh * first_tanh

    by_parts(w_first.shape[1], first_layer)

    def second_layer(cs):
        second_tanh = jnp.tanh(dot(hidden[...], w_second[:, cs]))
        slope_two[:, cs] = 1.0 - second_tanh * second_tanh

    by_parts(w_second.shape[1], second_layer)

    count = obs_index.shape[1]
    at = obs_index[...]
    at = jnp.where(flip[0] == 1, at + (rows - 1 - 2 * lax.div(at, lon)) * lon, at)
    live = lax.broadcasted_iota(jnp.int32, at.shape, 1) < obs_count[0]
    at = jnp.where(live, at, -1)
    chosen = at == lax.broadcasted_iota(jnp.int32, (cells, count), 0)
    place[...] = jnp.where(chosen, 1.0, 0.0).astype(BF16)
    lines = jnp.concatenate([at.astype(F32), jnp.where(live, obs_quality[...].astype(F32), 0.0)], axis=0)
    lines = jnp.concatenate([lines, jnp.zeros((6, count), F32)], axis=0)
    lines = jnp.concatenate([lines, jnp.zeros((8, cells - count), F32)], axis=1).T
    quality[...] = lines[0:count, 1:2]
    columns = lax.broadcasted_iota(jnp.int32, (count, cells), 1).astype(F32)
    pick[...] = jnp.where(lines[0:count, 0:1] == columns, 1.0, 0.0).astype(BF16)
    where, _ = slot_of(cells_reached(wind_fields(codes[...], sign, rows), rows))
    slots[...] = where
    place_far[...] = dot(choose_matrix(slots[...], place_far.shape[0], rows), place[...]).astype(BF16)


def observe_kernel(
    redo, flip, linked, slots, own_f, own_b, codes, far, rest, courant, slope_one, slope_two, kept_a, kept_b, kept_c,
    hbm_first, hbm_second, hbm_third, pick, place, place_far, quality, chan_weight, own_mats, own_slots,
    hbm_out, hbm_low, hbm_high, hbm_codes, hbm_slots, over, over_columns,
    table, mats, cells_b, mid_b, mid_f, last_b, one_b, two_b, w_first, w_second, w_third, out, low, high, far_codes, far_slots, sem,
    rest_b,
):
    rows, lon = 4, own_f.shape[0]
    cells = rows * lon
    sign = sign_of(flip)
    loads = [
        pltpu.make_async_copy(hbm_first, w_first, sem.at[0]),
        pltpu.make_async_copy(hbm_second, w_second, sem.at[1]),
        pltpu.make_async_copy(hbm_third, w_third, sem.at[2]),
    ]
    for copy in loads:
        copy.start()
    table[...] = jnp.zeros_like(table)
    tail = far[FAR_CELLS - NOTE_ROWS :, 0 : 4 * lon].astype(F32)[NOTE_ROWS:]
    far_codes[0:NOTE_ROWS, :] = tail[:, 0:lon]
    far_codes[NOTE_ROWS:, :] = tail[:, lon : 2 * lon]
    store_sources(table, 0, far_codes[...], True, sign, lon, rows)
    store_sources(table, 1, codes[...], False, sign, lon, rows)
    turned = table[...].T
    keep_codes = pltpu.make_async_copy(far_codes, hbm_codes, sem.at[3])
    keep_codes.start()
    reached, total = slot_of(cells_reached(wind_fields(far_codes[...], -sign, rows), rows))
    far_slots[...] = reached
    keep_slots = pltpu.make_async_copy(far_slots, hbm_slots, sem.at[6])
    keep_slots.start()
    most = jnp.maximum(jnp.max(total), jnp.max(own_slots[...]) + 1.0)
    over_columns[0] = jnp.where(most > float(FAR_COLUMNS), linked[0], 0)
    chosen = [None] * 8
    for k, (step, half) in enumerate(OWN_BLOCKS):
        chosen[2 * step + half] = own_mats.at[k]
    for k, (step, half) in enumerate(FAR_BLOCKS):
        pull_matrix(mats.at[k], turned, step, step + 1 + 2 * half, lon, rows)
        chosen[2 * step + half] = mats.at[k]
    listed, _ = slot_of(tail[:, 2 * lon : 3 * lon])
    where = turn(jnp.where(listed < float(FAR_CELLS), listed, -1.0))
    most = jnp.maximum(jnp.max(tail[:, 3 * lon :]), jnp.where(jnp.max(slots[...]) >= float(FAR_CELLS), 1.0, 0.0))
    over[0] = jnp.where(most > 0.0, linked[0], 0)
    for j in range(rows):
        value = dot(spread_matrix(where, j, far.shape[0]), far[...])
        cells_b[(rows - 1 - j) * lon : (rows - j) * lon, :] = value.astype(BF16)
    cells_b[cells:, :] = own_b[...]

    if redo:
        copy = pltpu.make_async_copy(rest, rest_b, sem.at[5])
        copy.start()
        copy.wait()
        where = turn(jnp.where(listed < float(FAR_CELLS), -1.0, listed))
        for j in range(rows):
            value = dot(spread_matrix(where, j, rest_b.shape[0], FAR_CELLS - NOTE_ROWS), rest_b[...])
            at = slice((rows - 1 - j) * lon, (rows - j) * lon)
            cells_b[at, :] = (cells_b[at, :].astype(F32) + value).astype(BF16)

    def start_f(at, size):
        pieces = []
        for row in range(at // lon, (at + size) // lon):
            if row == rows:
                pieces.append(own_f[...])
            else:
                pieces.append(cells_b[row * lon : (row + 1) * lon, :].astype(F32))
        return jnp.concatenate(pieces, axis=0)

    def finish(half, value):
        last_b[2 * half * lon : 2 * (half + 1) * lon, :] = value.astype(BF16)

    far_steps(
        chosen, lambda at, size: cells_b[at : at + size, :], start_f, courant,
        (kept_a, kept_b, kept_c), mid_b, mid_f, lon, finish,
    )
    one_b[...] = dot(pick[...], last_b[...]).astype(BF16)
    loads[0].wait()
    two_b[...] = (slope_one[...] * dot(one_b[...], w_first[...])).astype(BF16)
    loads[1].wait()
    one_b[...] = (slope_two[...] * dot(two_b[...], w_second[...])).astype(BF16)
    loads[2].wait()
    scale = quality[...] * chan_weight[0:1, :]
    two_b[...] = (scale * dot(one_b[...], w_third[...])).astype(BF16)
    one_b[...] = (slope_two[...] * dot_t(two_b[...], w_third[...])).astype(BF16)
    two_b[...] = (slope_one[...] * dot_t(one_b[...], w_second[...])).astype(BF16)
    one_b[...] = dot_t(two_b[...], w_first[...]).astype(BF16)
    half = low.shape[1]
    low[...] = dot(place_far[...], one_b[:, :half]).astype(BF16)
    keep_low = pltpu.make_async_copy(low, hbm_low, sem.at[4])
    keep_low.start()
    high[...] = dot(place_far[...], one_b[:, half:]).astype(BF16)
    keep_high = pltpu.make_async_copy(high, hbm_high, sem.at[1])
    keep_high.start()
    out[...] = dot(place[...], one_b[...]).astype(BF16)
    keep_out = pltpu.make_async_copy(out, hbm_out, sem.at[0])
    keep_out.start()
    keep_codes.wait()
    keep_slots.wait()
    keep_low.wait()
    keep_high.wait()
    keep_out.wait()


def near_adjoint_kernel(
    flip, rest, cells_own, cells_near, codes, near_codes, far_codes, far_slots, courant,
    kept_a, kept_b, kept_c, far_mats, spread,
    table, mats, cells_b, mid_b, mid_f, slots_b, codes_b, sem,
):
    rows, lon = 4, table.shape[1]
    cells = rows * lon
    own_copy = pltpu.make_async_copy(cells_own, cells_b.at[0:cells], sem.at[0])
    own_copy.start()
    slots_copy = pltpu.make_async_copy(far_slots, slots_b, sem.at[1])
    slots_copy.start()
    codes_copy = pltpu.make_async_copy(far_codes, codes_b, sem.at[2])
    codes_copy.start()
    codes_copy.wait()
    sign = sign_of(flip)
    store_sources(table, 0, codes_b[...], True, sign, lon, rows)
    store_sources(table, 1, codes[...], False, sign, lon, rows)
    store_sources(table, 2, near_codes[...], True, sign, lon, rows)
    k = 0
    for order, exts in enumerate(((5, 7, 9), (6, 8), (7,))):
        for ext in exts:
            push_matrix(mats.at[k], table, 3 - order, ext, lon, rows)
            k += 1
    for j in range(rows):
        cells_b[(rows + j) * lon : (rows + j + 1) * lon, :] = cells_near[
            (rows - 1 - j) * lon : (rows - j) * lon, :
        ]

    own_copy.wait()

    def advect(cs):
        near_steps(
            mats, lambda at, size: cells_b[at : at + size, cs],
            lambda at, size: cells_b[at : at + size, cs].astype(F32), courant,
            (kept_a, kept_b, kept_c), mid_b, mid_f, lon, cs,
        )

    advect(slice(None))
    for order in range(4):
        for half in range(2):
            push_matrix(far_mats.at[2 * order + half], table, 3 - order, order + 1 + 2 * half, lon, rows)
    slots_copy.wait()
    where = turn(slots_b[...])
    capacity = spread.shape[1]
    for j in range(rows):
        spread[j * lon : (j + 1) * lon, :] = spread_matrix(where, j, capacity)


def far_adjoint_kernel(
    part, flip, flag, cells_own, far, rest, courant, kept_a, kept_b, kept_c, mats, spread, far_slots, _given,
    out,
    cells_b, mid_b, mid_f, result, rest_b, slots_b, sem,
):
    rows, lon = out.shape[0], out.shape[1]
    cells = rows * lon
    width = far.shape[1]
    cs = slice(part * width, (part + 1) * width)
    for j in range(rows):
        value = dot(spread[j * lon : (j + 1) * lon, :], far[...])
        cells_b[(rows - 1 - j) * lon : (rows - j) * lon, :] = value.astype(BF16)
    cells_b[cells:, :] = cells_own[0 : 2 * lon, cs]

    @pl.when(flag[0] > 0)
    def _():
        fetches = [
            pltpu.make_async_copy(rest.at[:, cs], rest_b, sem.at[rows]),
            pltpu.make_async_copy(far_slots, slots_b, sem.at[rows + 1]),
        ]
        for copy in fetches:
            copy.start()
        for copy in fetches:
            copy.wait()
        where = turn(slots_b[...])
        for j in range(rows):
            value = dot(spread_matrix(where, j, rest_b.shape[0], spread.shape[1]), rest_b[...])
            at = slice((rows - 1 - j) * lon, (rows - j) * lon)
            cells_b[at, :] = (cells_b[at, :].astype(F32) + value).astype(BF16)

    copies = []

    def finish(half, value):
        for piece in range(2):
            j = 2 * half + piece
            result[j] = value[piece * lon : (piece + 1) * lon, :]
            at = jnp.where(flip[0] == 1, rows - 1 - j, j)
            copies.append(pltpu.make_async_copy(result.at[j], out.at[at, :, cs], sem.at[j]))
            copies[-1].start()

    far_steps(
        [mats.at[k] for k in range(8)], lambda at, size: cells_b[at : at + size, :],
        lambda at, size: cells_b[at : at + size, :].astype(F32), courant.at[:, cs],
        tuple(kept.at[:, cs] for kept in (kept_a, kept_b, kept_c)), mid_b, mid_f, lon, finish,
    )
    for copy in copies:
        copy.wait()


def params():
    return pltpu.CompilerParams(vmem_limit_bytes=VMEM_LIMIT)


def shape(dims, dtype):
    return jax.ShapeDtypeStruct(dims, dtype)


def send_rest(first, slots, dense, size, links):
    rest = pl.pallas_call(
        functools.partial(rest_kernel, first),
        out_shape=shape((size, dense.shape[1]), BF16),
        in_specs=[VMEM, VMEM],
        out_specs=VMEM,
        name="rest",
    )(slots, dense)
    return lax.ppermute(rest, "lat", links)


def blank(outs):
    return pl.pallas_call(blank_kernel, out_shape=outs, out_specs=[ANY] * len(outs), name="blank")()


def local(
    tangent,
    wind_code,
    courant,
    obs_index,
    obs_count,
    obs_quality,
    background,
    w_first,
    w_second,
    w_third,
    chan_weight,
):
    rows, lon, levels = tangent.shape
    cells = rows * lon
    head = wind_code.shape[0] * rows
    listed = obs_index.shape[1]
    hidden_size = w_first.shape[1]
    count = lax.axis_size("lat")
    here = lax.axis_index("lat")
    odd = (here % 2).astype(jnp.int32)
    flip = odd.reshape(1)
    linked = ((here > 0) & (here < count - 1)).astype(jnp.int32).reshape(1)
    pairs = [(i, i ^ 1) for i in range(count)]
    links = [(i, i + 1) for i in range(1, count - 1, 2)]
    links = links + [(b, a) for a, b in links]

    own, sent, codes, slots = pl.pallas_call(
        pack_kernel,
        out_shape=[
            shape((cells + head, levels), BF16),
            shape((FAR_CELLS + NOTE_ROWS, levels), BF16),
            shape((head, lon), F32),
            shape((8, lon), F32),
        ],
        in_specs=[SMEM, HBM, HBM],
        out_specs=[VMEM] * 4,
        scratch_shapes=[
            pltpu.VMEM((rows, lon, levels), F32),
            pltpu.VMEM(wind_code.shape, jnp.int32),
            pltpu.SemaphoreType.DMA((rows + 1,)),
        ],
        compiler_params=pltpu.CompilerParams(vmem_limit_bytes=PACK_LIMIT),
        name="pack",
    )(flip, tangent, wind_code)

    far = lax.ppermute(sent, "lat", links)
    near = lax.ppermute(own, "lat", pairs)

    c_row = courant.reshape(1, levels)
    kept_shape = [shape((2 * lon, levels), F32)] * 3
    slope_shape = shape((listed, hidden_size), F32)

    def run_near():
        return pl.pallas_call(
            near_kernel,
            out_shape=[slope_shape, slope_shape]
            + kept_shape
            + [
                shape((listed, cells), BF16),
                shape((cells, listed), BF16),
                shape((FAR_COLUMNS, listed), BF16),
                shape((head, lon), F32),
                shape((listed, 1), F32),
                shape((8, lon), F32),
                shape((4, 2 * lon, 4 * lon), BF16),
                shape((lon, levels), F32),
                shape((2 * lon, levels), BF16),
            ],
            in_specs=[SMEM, SMEM] + [VMEM] * 9,
            out_specs=[VMEM] * 14,
            scratch_shapes=[
                pltpu.VMEM((lon, lon), F32),
                pltpu.VMEM((6, 2 * lon, 4 * lon), BF16),
                pltpu.VMEM((2 * cells, levels), BF16),
                pltpu.VMEM((2, 6 * lon, PART), BF16),
                pltpu.VMEM((2, 6 * lon, PART), F32),
                pltpu.VMEM((listed, hidden_size), BF16),
            ],
            compiler_params=params(),
            cost_estimate=pl.CostEstimate(flops=4_000_000_000, bytes_accessed=16_000_000, transcendentals=1_000_000),
            name="near",
        )(
            flip, obs_count, tangent, codes, near, c_row, background[0], w_first, w_second, obs_index, obs_quality,
        )

    column_shape = [pltpu.HBM((cells, levels), BF16)] + [pltpu.HBM((FAR_COLUMNS, levels // 2), BF16)] * 2

    def run_observe(redo, parts, rest):
        slope_one, slope_two, kept_a, kept_b, kept_c, pick, place, place_far = parts[:8]
        quality, columns_list, own_mats, own_f, own_b = parts[9:]
        rest_specs = [ANY] if redo else []
        body = functools.partial(observe_kernel, redo)
        rest_args = [rest] if redo else []
        rest_scratch = [pltpu.VMEM((cells - FAR_CELLS + NOTE_ROWS, levels), BF16)]

        def kernel(*refs):
            refs = list(refs)
            if not redo:
                refs.insert(7, None)
                refs.append(None)
            body(*refs)

        return pl.pallas_call(
            kernel,
            out_shape=column_shape
            + [pltpu.HBM((head, lon), F32), pltpu.HBM((8, lon), F32)]
            + [shape((1,), jnp.int32)] * 2,
            in_specs=[SMEM, SMEM] + [VMEM] * 5 + rest_specs + [VMEM] * 6 + [ANY] * 3 + [VMEM] * 7,
            out_specs=[HBM] * 5 + [SMEM] * 2,
            scratch_shapes=[
                pltpu.VMEM((lon, lon), F32),
                pltpu.VMEM((4, 2 * lon, 4 * lon), BF16),
                pltpu.VMEM((6 * lon, levels), BF16),
                pltpu.VMEM((2, 6 * lon, levels), BF16),
                pltpu.VMEM((2, 6 * lon, levels), F32),
                pltpu.VMEM((cells, levels), BF16),
                pltpu.VMEM((listed, levels), BF16),
                pltpu.VMEM((listed, levels), BF16),
                pltpu.VMEM(w_first.shape, BF16),
                pltpu.VMEM(w_second.shape, BF16),
                pltpu.VMEM(w_third.shape, BF16),
                pltpu.VMEM((cells, levels), BF16),
                pltpu.VMEM((FAR_COLUMNS, levels // 2), BF16),
                pltpu.VMEM((FAR_COLUMNS, levels // 2), BF16),
                pltpu.VMEM((head, lon), F32),
                pltpu.VMEM((8, lon), F32),
                pltpu.SemaphoreType.DMA((7,)),
            ]
            + (rest_scratch if redo else []),
            compiler_params=params(),
            name="observe",
        )(
            flip, linked, slots, own_f, own_b, codes, far, *rest_args, c_row,
            slope_one, slope_two, kept_a, kept_b, kept_c, w_first, w_second, w_third,
            pick, place, place_far, quality, chan_weight.reshape(1, -1), own_mats, columns_list,
        )

    parts = run_near()
    near_codes, own_slots = parts[8], parts[10]
    cells_own, low, high, far_codes, far_slots, over, over_columns = run_observe(False, parts, None)

    def observe_again():
        first = FAR_CELLS - NOTE_ROWS
        rest = send_rest(first, slots, own, cells - first, links)
        return run_observe(True, run_near(), rest)[:3]

    redone = lax.cond(over[0] > 0, observe_again, lambda: blank(column_shape))
    cells_own, low, high = pl.pallas_call(
        choose_kernel,
        out_shape=column_shape,
        in_specs=[SMEM] + [HBM] * 6,
        out_specs=[HBM] * 3,
        scratch_shapes=[pltpu.SemaphoreType.DMA((3,))],
        input_output_aliases={1: 0, 2: 1, 3: 2},
        name="choose",
    )(over, cells_own, low, high, *redone)

    far_low = lax.ppermute(low, "lat", links)
    far_high = lax.ppermute(high, "lat", links)
    cells_near = lax.ppermute(cells_own, "lat", pairs)

    left = cells - FAR_COLUMNS
    rest = lax.cond(
        over_columns[0] > 0,
        lambda: send_rest(FAR_COLUMNS, own_slots, cells_own, left, links),
        lambda: blank([shape((left, levels), BF16)])[0],
    )
    kept_a, kept_b, kept_c, mats, spread = pl.pallas_call(
        near_adjoint_kernel,
        out_shape=kept_shape
        + [
            shape((8, 2 * lon, 4 * lon), BF16),
            shape((cells, FAR_COLUMNS), BF16),
        ],
        in_specs=[SMEM, ANY, ANY] + [VMEM] * 3 + [ANY, ANY, VMEM],
        out_specs=[VMEM] * 5,
        scratch_shapes=[
            pltpu.VMEM((lon, lon), F32),
            pltpu.VMEM((6, 2 * lon, 4 * lon), BF16),
            pltpu.VMEM((2 * cells, levels), BF16),
            pltpu.VMEM((2, 6 * lon, levels), BF16),
            pltpu.VMEM((2, 6 * lon, levels), F32),
            pltpu.VMEM((8, lon), F32),
            pltpu.VMEM((head, lon), F32),
            pltpu.SemaphoreType.DMA((3,)),
        ],
        compiler_params=params(),
        cost_estimate=pl.CostEstimate(flops=2_000_000_000, bytes_accessed=8_000_000, transcendentals=0),
        name="near_adjoint",
    )(flip, rest, cells_own, cells_near, codes, near_codes, far_codes, far_slots, c_row)

    width = levels // 2

    def finish(part, columns, given):
        body = functools.partial(far_adjoint_kernel, part)
        given_specs = [HBM] if part else []

        def kernel(*refs):
            refs = list(refs)
            if not part:
                refs.insert(12, None)
            body(*refs)

        return pl.pallas_call(
            kernel,
            out_shape=shape((rows, lon, levels), F32),
            in_specs=[SMEM, SMEM, VMEM, VMEM, ANY] + [VMEM] * 6 + [ANY] + given_specs,
            out_specs=HBM,
            scratch_shapes=[
                pltpu.VMEM((6 * lon, width), BF16),
                pltpu.VMEM((2, 6 * lon, width), BF16),
                pltpu.VMEM((2, 6 * lon, width), F32),
                pltpu.VMEM((rows, lon, width), F32),
                pltpu.VMEM((left, width), BF16),
                pltpu.VMEM((8, lon), F32),
                pltpu.SemaphoreType.DMA((rows + 2,)),
            ],
            input_output_aliases={12: 0} if part else {},
            compiler_params=params(),
            cost_estimate=pl.CostEstimate(flops=2_000_000_000, bytes_accessed=4_000_000, transcendentals=0),
            name="far_adjoint",
        )(
            flip, over_columns, cells_own, columns, rest, c_row, kept_a, kept_b, kept_c, mats, spread, far_slots, *given,
        )

    half_done = finish(0, far_low, [])
    return finish(1, far_high, [half_done])


def solution(mesh):
    placed = (
        P(("groups", "lat"), None, None),
        P(None, ("groups", "lat"), None),
        P(),
        P(("groups", "lat"), None),
        P(("groups", "lat")),
        P(("groups", "lat"), None),
        P(("groups", "lat"), None, None),
        P(),
        P(),
        P(),
        P(),
    )
    return jax.shard_map(
        local,
        mesh=mesh,
        in_specs=placed,
        out_specs=P(("groups", "lat"), None, None),
        check_vma=False,
    )
```
